32 devices in a mesh: gx: 4 (over z), gy: 8 (over y, x, core).
Axes of the slice: x: 2, y: 2, z: 4, core: 2. Of those that a mesh axis runs over, the one named last changes fastest.
Arguments:
- features: bfloat16 [64, 128, 64, 128], P('gx', 'gy'), may hold values from -6 to 6
- tile_mask: int32 [64, 128, 9], P('gx', 'gy'), may hold values from 0 to 1, as said below
- pool_map: int32 [64, 128, 64], P('gx', 'gy'), may hold values from 0 to 63
- readers: int32 [32, 8], replicated, may hold values from -1 to 31, as said below
- w_query: bfloat16 [128, 128], replicated, may hold values from -0.5 to 0.5
- w_key: bfloat16 [128, 128], replicated, may hold values from -0.5 to 0.5
- w_value: bfloat16 [128, 128], replicated, may hold values from -0.5 to 0.5
- w_cquery: bfloat16 [128, 128], replicated, may hold values from -0.5 to 0.5
- w_ckey: bfloat16 [128, 128], replicated, may hold values from -0.5 to 0.5
- w_cvalue: bfloat16 [128, 128], replicated, may hold values from -0.5 to 0.5
Outputs:
- update: bfloat16 [64, 128, 64, 128], P('gx', 'gy')
The draws below stay inside these ranges and needn't reach their ends.
Inputs may be any that keep to these rules, and one draw needn't show every extreme that they name: `tile_mask`: entry 4 (the cell with itself) is always 1; all entries are 0 or 1. `readers`: A row lists between 1 and 8 distinct domains other than its own, then -1 entries; some row lists 8.
All inputs are finite; a program needn't handle non-finite values.
Results may differ from the reference program's by a relative error of at most 0.0065.
Values may be sent and summed in bfloat16 or wider, within the bound.
No kernel may reach another device: no remote copies, remote signals or barrier semaphores. Data moves between devices by JAX's collectives and lax.ppermute only.
A program may use at most 256 MiB of HBM per device.

```python
import math
import jax
import jax.numpy as jnp
from jax import lax

F = 128
TILE = 64
S = 64
RMAX = 8
CX = 16
CY = 16
NCX = 64
NCY = 128
DOMAINS = 32


def draw_tile_mask(key, part):
    key = jax.random.fold_in(key, 3)
    key_density, key_rolls = jax.random.split(key)
    density = jax.random.randint(key_density, (NCX // CX, NCY // CY), 5, 101)
    density = jnp.repeat(jnp.repeat(density, CX, axis=0), CY, axis=1)
    rolls = jax.random.randint(key_rolls, (NCX, NCY, 9), 0, 100)
    active = (rolls < density[:, :, None]).astype(jnp.int32)
    return active.at[:, :, 4].set(1)


def shuffled_offsets(row_key):
    return jax.random.permutation(row_key, DOMAINS - 1)


def draw_readers(key, part):
    key = jax.random.fold_in(key, 7)
    key_counts, key_hot, key_rows = jax.random.split(key, 3)
    counts = jax.random.randint(key_counts, (DOMAINS,), 1, RMAX + 1)
    hot_row = jax.random.randint(key_hot, (), 0, DOMAINS - 1)
    counts = jnp.where(jnp.arange(DOMAINS) == hot_row, RMAX, counts)
    row_keys = jax.random.split(key_rows, DOMAINS)
    offsets = jax.vmap(shuffled_offsets)(row_keys) + 1
    target = DOMAINS - 1 - hot_row
    hot_offsets = offsets[hot_row]
    position = jnp.argmax(hot_offsets == target)
    swapped = hot_offsets.at[position].set(hot_offsets[0]).at[0].set(target)
    offsets = offsets.at[hot_row].set(swapped)
    chosen = offsets[:, :RMAX]
    listed = (jnp.arange(DOMAINS)[:, None] + chosen) % DOMAINS
    live = jnp.arange(RMAX)[None, :] < counts[:, None]
    return jnp.where(live, listed, -1).astype(jnp.int32)


def plant(drawn, key, smallest, largest):
    spot = [jax.random.randint(jax.random.fold_in(key, axis), (), 0, length) for axis, length in enumerate(drawn.shape)]
    widest = drawn.shape.index(max(drawn.shape))
    next_to = spot[:widest] + [(spot[widest] + 1) % drawn.shape[widest]] + spot[widest + 1:]
    return drawn.at[tuple(spot)].set(smallest).at[tuple(next_to)].set(largest)


def block_scale(key, dims, shards, smallest, high):
    factor_of = 1.0
    for dim, blocks in shards:
        steps = jax.random.uniform(jax.random.fold_in(jax.random.fold_in(key, 6), dim), (blocks,), jnp.float32, smallest / len(shards), high / len(shards))
        factor_of = factor_of * jnp.repeat(jnp.exp(steps), dims[dim] // blocks).reshape((-1,) + (1,) * (len(dims) - 1 - dim))
    return factor_of


def noise(stream_key, extent, width, reach, pieces=(), held_as=jnp.bfloat16):
    loudness = block_scale(stream_key, extent, pieces, -0.22, 0.18) if pieces else 1.0
    array = jax.random.normal(stream_key, extent, jnp.float32) * width * loudness
    return jnp.minimum(jnp.maximum(array, -reach), reach).astype(held_as)


def setup_inputs(seed: int = 0) -> dict:
    key_of = jax.random.split(jax.random.key(seed), 11)
    features = noise(key_of[0], (NCX, NCY, TILE, F), 1.0, 6.0, ((0, 4), (1, 8)))
    tile_mask = draw_tile_mask(jax.random.fold_in(key_of[10], 71), 0)
    pool_map = plant(jax.random.randint(key_of[2], (NCX, NCY, TILE), 0, S), jax.random.fold_in(key_of[2], 1), 0, S - 1).astype(jnp.int32)
    readers = draw_readers(jax.random.fold_in(key_of[10], 71), 0)
    w_query = noise(key_of[4], (F, F), F ** -0.5, 0.5)
    w_key = noise(key_of[5], (F, F), F ** -0.5, 0.5)
    w_value = noise(key_of[6], (F, F), F ** -0.5, 0.5)
    w_cquery = noise(key_of[7], (F, F), F ** -0.5, 0.5)
    w_ckey = noise(key_of[8], (F, F), F ** -0.5, 0.5)
    w_cvalue = noise(key_of[9], (F, F), F ** -0.5, 0.5)
    return {"features": features, "tile_mask": tile_mask, "pool_map": pool_map, "readers": readers, "w_query": w_query, "w_key": w_key, "w_value": w_value, "w_cquery": w_cquery, "w_ckey": w_ckey, "w_cvalue": w_cvalue}


def project(rows, weight):
    flat = rows.reshape(-1, rows.shape[-1])
    result = jnp.dot(flat, weight, preferred_element_type=jnp.float32).astype(jnp.bfloat16)
    return result.reshape(rows.shape[:-1] + (weight.shape[1],))

def pair_filter(queries, keys_near, values_near):
    scores = jnp.einsum('...if,...jf->...ij', queries.astype(jnp.float32), keys_near.astype(jnp.float32)) / math.sqrt(queries.shape[-1])
    rounded = lax.optimization_barrier(jax.nn.silu(scores).astype(jnp.bfloat16))
    return jnp.einsum('...ij,...jf->...if', rounded.astype(jnp.float32), values_near.astype(jnp.float32))

def reference(features, tile_mask, pool_map, readers, w_query, w_key, w_value, w_cquery, w_ckey, w_cvalue):
    queries = project(features, w_query)
    keys_near = project(features, w_key)
    values_near = project(features, w_value)
    keys_pad = jnp.pad(keys_near, ((1, 1), (1, 1), (0, 0), (0, 0)))
    values_pad = jnp.pad(values_near, ((1, 1), (1, 1), (0, 0), (0, 0)))

    def cell_row(cell_index):
        row_queries = lax.dynamic_index_in_dim(queries, cell_index, 0, keepdims=False)
        row_keys = lax.dynamic_slice_in_dim(keys_pad, cell_index, 3, 0)
        row_values = lax.dynamic_slice_in_dim(values_pad, cell_index, 3, 0)
        row_mask = lax.dynamic_index_in_dim(tile_mask, cell_index, 0, keepdims=False)
        summed = jnp.zeros(row_queries.shape, jnp.float32)
        for shift_x in (-1, 0, 1):
            for shift_y in (-1, 0, 1):
                offset = 3 * (shift_x + 1) + (shift_y + 1)
                near_keys = row_keys[1 + shift_x, 1 + shift_y:1 + shift_y + NCY]
                near_values = row_values[1 + shift_x, 1 + shift_y:1 + shift_y + NCY]
                weight = row_mask[:, offset].astype(jnp.float32)[:, None, None]
                summed = summed + weight * pair_filter(row_queries, near_keys, near_values)
        return summed
    fine_sum = lax.map(cell_row, jnp.arange(NCX, dtype=jnp.int32)) / math.sqrt(TILE)
    cell_x = jnp.arange(NCX, dtype=jnp.int32)[:, None, None]
    cell_y = jnp.arange(NCY, dtype=jnp.int32)[None, :, None]
    domain = cell_x // CX * (NCY // CY) + cell_y // CY
    global_node = (domain * S + pool_map).astype(jnp.int32)
    summed_nodes = jax.ops.segment_sum(features.astype(jnp.float32).reshape(-1, F), global_node.reshape(-1), num_segments=DOMAINS * S)
    pooled = (summed_nodes * math.sqrt(S / (CX * CY * TILE))).astype(jnp.bfloat16)
    coarse_query = project(pooled, w_cquery).reshape(DOMAINS, S, F)
    coarse_key = project(pooled, w_ckey).reshape(DOMAINS, S, F)
    coarse_value = project(pooled, w_cvalue).reshape(DOMAINS, S, F)
    reads = jnp.any(readers[:, :, None] == jnp.arange(DOMAINS, dtype=jnp.int32)[None, None, :], axis=1).astype(jnp.float32)

    def sender(domain_index):
        own_query = lax.dynamic_index_in_dim(coarse_query, domain_index, 0, keepdims=False)
        read_row = lax.dynamic_index_in_dim(reads, domain_index, 0, keepdims=False)
        scores = jnp.einsum('sf,etf->est', own_query.astype(jnp.float32), coarse_key.astype(jnp.float32)) / math.sqrt(F)
        rounded = lax.optimization_barrier(jax.nn.silu(scores).astype(jnp.bfloat16))
        message = jnp.einsum('est,etf->esf', rounded.astype(jnp.float32), coarse_value.astype(jnp.float32))
        return lax.optimization_barrier(jnp.sum(message * read_row[:, None, None], axis=0)) / math.sqrt(S)
    coarse_msg = lax.map(sender, jnp.arange(DOMAINS, dtype=jnp.int32)).astype(jnp.bfloat16).reshape(DOMAINS * S, F)
    unpooled = coarse_msg[global_node]
    return (fine_sum + unpooled.astype(jnp.float32)).astype(jnp.bfloat16)
```

```python
import functools
import math

import jax
import jax.numpy as jnp
import numpy as np
from jax import lax
from jax.experimental import pallas as pl
from jax.experimental.pallas import tpu as pltpu
from jax.sharding import PartitionSpec as P

BF16 = jnp.bfloat16
F32 = jnp.float32
S = 64
LIMIT = 24 * 1024 * 1024


def dot_t(a, b):
    return lax.dot_general(a, b, (((1,), (1,)), ((), ())), preferred_element_type=F32)


def dot(a, b):
    return jnp.dot(a, b, preferred_element_type=F32)


def whole(a):
    return pl.BlockSpec(a.shape, lambda *_: (0,) * len(a.shape))


IN_VMEM = pl.BlockSpec(memory_space=pltpu.VMEM)
IN_PLACE = pl.BlockSpec(memory_space=pl.ANY)


def params():
    return pltpu.CompilerParams(vmem_limit_bytes=LIMIT)


def pool_kernel(cells, f_ref, pm_ref, tm_ref, wq_ref, wk_ref, fv_ref, mv_ref, pooled_ref, m_ref, acc):
    p, rows = pl.program_id(0), pl.num_programs(0)
    cy, tile, chan = f_ref.shape
    beads = f_ref[...]
    fv_ref[p] = beads.reshape(cy * tile, chan)
    half = cy // 2
    ids = pm_ref[...]
    pairs = jnp.concatenate([ids[:half], ids[half:]], axis=1)
    node = lax.broadcasted_iota(jnp.int32, (S, 2 * tile), 0)
    onehot = jnp.concatenate(
        [(jnp.broadcast_to(pairs[i : i + 1], node.shape) == node).astype(F32).astype(BF16) for i in range(half)], axis=1
    )
    order = [c for i in range(half) for c in (i, i + half)]
    summed = dot(onehot, jnp.concatenate([beads[c] for c in order], axis=0))
    total = summed + jnp.where(p == 0, 0.0, acc[...])
    acc[...] = total

    block = lax.broadcasted_iota(jnp.int32, (9, 12 * tile), 1) // tile
    offset = lax.broadcasted_iota(jnp.int32, (9, 12 * tile), 0)
    mask = tm_ref[...].astype(F32).astype(BF16)
    spread = []
    for second in (0, 1):
        hit = (offset // 3 == block // 4) & (offset % 3 == block % 4 - second)
        pick = jnp.where(hit, 1 / math.sqrt(tile), 0.0).astype(BF16)
        spread.append(dot(mask, pick).astype(BF16))
    even = lax.broadcasted_iota(jnp.int32, (cy, 12 * tile), 0) % 2 == 0
    mv_ref[p] = jnp.where(even, spread[0].astype(F32), spread[1].astype(F32))

    @pl.when(p == rows - 1)
    def _():
        pooled_ref[...] = (total * math.sqrt(S / cells)).astype(BF16)
        m_ref[...] = (dot_t(wq_ref[...], wk_ref[...]) * (0.5 / math.sqrt(chan))).astype(BF16)


def pool(features, tile_mask, pool_map, w_query, w_key):
    cx, cy, tile, chan = features.shape
    return pl.pallas_call(
        functools.partial(pool_kernel, cx * cy * tile),
        grid=(cx,),
        in_specs=[
            pl.BlockSpec((None, cy, tile, chan), lambda p: (p, 0, 0, 0)),
            pl.BlockSpec((None, cy, tile), lambda p: (p, 0, 0)),
            pl.BlockSpec((None, cy, 9), lambda p: (p, 0, 0)),
            whole(w_query),
            whole(w_key),
        ],
        out_specs=[IN_VMEM, IN_VMEM, pl.BlockSpec((S, chan), lambda p: (0, 0)), pl.BlockSpec((chan, chan), lambda p: (0, 0))],
        out_shape=[
            pltpu.VMEM((cx, cy * tile, chan), BF16),
            pltpu.VMEM((cx, cy, 12 * tile), F32),
            jax.ShapeDtypeStruct((S, chan), BF16),
            jax.ShapeDtypeStruct((chan, chan), BF16),
        ],
        scratch_shapes=[pltpu.VMEM((S, chan), F32)],
        compiler_params=params(),
        name="pool",
    )(features, pool_map, tile_mask, w_query, w_key)


def attend_row(cy, tile, queries, masks, window, store):
    waiting = []

    def finish(j, weights):
        near = jnp.concatenate([window(r, j) for r in range(3)], axis=0)
        store(j, dot(jnp.concatenate(weights, axis=1), near).astype(BF16))

    for j in range(cy // 2):
        query = queries[2 * tile * j : 2 * tile * (j + 1)]
        weights = []
        for r in range(3):
            half = dot_t(query, window(r, j)).astype(BF16)
            lanes = slice(4 * tile * r, 4 * tile * (r + 1))
            mask = jnp.concatenate(
                [jnp.broadcast_to(masks(2 * j + h, lanes), (tile, 4 * tile)) for h in (0, 1)], axis=0
            )
            weights.append((half * jnp.tanh(half) + half) * mask.astype(BF16))
        waiting.append((j, weights))
        if len(waiting) > 2:
            finish(*waiting.pop(0))
    while waiting:
        finish(*waiting.pop(0))


def fine_kernel(first, count, edge, fv_ref, mv_ref, m_ref, yl_ref, yr_ref, *rest):
    if edge:
        xl_ref, xr_ref, o_ref, yl, yr, xl, xr, sems = rest
        moves = [(yl_ref, yl), (yr_ref, yr), (xl_ref, xl), (xr_ref, xr)]
    else:
        o_ref, yl, yr, sems = rest
        moves = [(yl_ref, yl), (yr_ref, yr)]
    copies = [pltpu.make_async_copy(src, dst, sems.at[i]) for i, (src, dst) in enumerate(moves)]
    for copy in copies:
        copy.start()
    cx, span, chan = fv_ref.shape
    cy = mv_ref.shape[1]
    tile = span // cy
    for copy in copies:
        copy.wait()

    def inner(row):
        def window(j):
            if j == 0:
                return jnp.concatenate([yl[row], fv_ref[row, : 3 * tile]], axis=0)
            if j == cy // 2 - 1:
                return jnp.concatenate([fv_ref[row, span - 3 * tile :], yr[row]], axis=0)
            return fv_ref[row, tile * (2 * j - 1) : tile * (2 * j + 3)]

        return window

    def outer(ref):
        return lambda j: ref[tile * 2 * j : tile * (2 * j + 4)]

    def attend(row, near, slot):
        queries = dot(fv_ref[row], m_ref[...]).astype(BF16)

        def store(j, value):
            o_ref[slot, 2 * tile * j : 2 * tile * (j + 1)] = value

        attend_row(cy, tile, queries, lambda c, lanes: mv_ref[row, c : c + 1, lanes], lambda r, j: near[r](j), store)

    if edge:
        attend(0, [outer(xl), inner(0), inner(1)], 0)
        attend(cx - 1, [inner(cx - 2), inner(cx - 1), outer(xr)], 1)
    else:

        @pl.loop(0, count)
        def _(i):
            row = first + i
            attend(row, [inner(row - 1), inner(row), inner(row + 1)], i)


def fine(first, count, fv, mv, m, yl, yr, edges=()):
    cx, span, chan = fv.shape
    cy = mv.shape[1]
    tile = span // cy
    halo = [pltpu.VMEM((cx, tile, chan), BF16)] * 2 + [pltpu.VMEM((span + 2 * tile, chan), BF16)] * len(edges)
    rows = 2 if edges else count
    return pl.pallas_call(
        functools.partial(fine_kernel, first, count, bool(edges)),
        in_specs=[IN_VMEM, IN_VMEM, IN_VMEM, IN_PLACE, IN_PLACE] + [IN_PLACE] * len(edges),
        out_specs=IN_VMEM,
        out_shape=pltpu.VMEM((rows, span, chan), BF16),
        scratch_shapes=halo + [pltpu.SemaphoreType.DMA((len(halo),))],
        compiler_params=params(),
        cost_estimate=pl.CostEstimate(flops=rows * 300_000_000 * 4, bytes_accessed=rows * span * chan * 4, transcendentals=0),
        name=f"fine_{first}",
    )(fv, mv, m, yl, yr, *edges)


def final_kernel(starts, g_ref, own_ref, live_ref, pm_ref, wcq_ref, wck_ref, wcv_ref, wv_ref, *rest):
    pieces, o_ref, mix = rest[:-2], rest[-2], rest[-1]
    p = pl.program_id(0)
    cy, tile, chan = o_ref.shape

    @pl.when(p == 0)
    def _():
        nodes = g_ref[...].reshape(-1, chan)
        query = dot(own_ref[...], wcq_ref[...]).astype(BF16)
        key = dot(nodes, wck_ref[...]).astype(BF16)
        value = dot(nodes, wcv_ref[...]).astype(BF16)
        half = dot_t(query, key) * (0.5 / math.sqrt(chan))
        weight = (half * jnp.tanh(half) + half).astype(BF16).astype(F32) * live_ref[...]
        mix[:chan] = wv_ref[...]
        mix[chan:] = (dot(weight.astype(BF16), value) / math.sqrt(S)).astype(BF16)

    half = cy // 2
    ids = pm_ref[...]
    pairs = jnp.concatenate([ids[:half], ids[half:]], axis=1)
    node = lax.broadcasted_iota(jnp.int32, (S, 2 * tile), 0)

    def finish(near):
        hot = [None] * cy
        for i in range(half):
            turned = (jnp.broadcast_to(pairs[i : i + 1], node.shape) == node).astype(F32).T.astype(BF16)
            hot[i], hot[i + half] = turned[:tile], turned[tile:]
        both = jnp.concatenate([near, jnp.concatenate(hot, axis=0)], axis=1)
        o_ref[...] = dot(both, mix[...]).astype(BF16).reshape(cy, tile, chan)

    last = pl.num_programs(0) - 1
    for (first, count), ref in zip(starts, pieces):
        if first is None:
            pl.when(p == 0)(lambda ref=ref: finish(ref[0]))
            pl.when(p == last)(lambda ref=ref: finish(ref[1]))
        else:
            pl.when((p >= first) & (p < first + count))(lambda ref=ref, first=first: finish(ref[p - first]))


def final(starts, pieces, gathered, own, live, pool_map, w_cquery, w_ckey, w_cvalue, w_value):
    cx, cy, tile = pool_map.shape
    chan = own.shape[1]
    return pl.pallas_call(
        functools.partial(final_kernel, starts),
        grid=(cx,),
        in_specs=[whole(gathered), whole(own), whole(live), pl.BlockSpec((None, cy, tile), lambda p: (p, 0, 0))]
        + [whole(w_value)] * 4
        + [IN_VMEM] * len(pieces),
        out_specs=pl.BlockSpec((None, cy, tile, chan), lambda p: (p, 0, 0, 0)),
        out_shape=jax.ShapeDtypeStruct((cx, cy, tile, chan), BF16),
        scratch_shapes=[pltpu.VMEM((chan + S, chan), BF16)],
        compiler_params=params(),
        name="final",
    )(gathered, own, live, pool_map, w_cquery, w_ckey, w_cvalue, w_value, *pieces)


def shift(array, axis, step):
    count = lax.axis_size(axis)
    return lax.ppermute(array, axis, [(i, i + step) for i in range(count) if 0 <= i + step < count])


def swap(array, axis, bit):
    return lax.ppermute(array, axis, [(i, i ^ bit) for i in range(lax.axis_size(axis))])


def per_device(features, tile_mask, pool_map, readers, w_query, w_key, w_value, w_cquery, w_ckey, w_cvalue):
    cx, cy, tile, chan = features.shape
    nx, ny = lax.axis_size("gx"), lax.axis_size("gy")
    mx, my = lax.axis_index("gx"), lax.axis_index("gy")
    yl = shift(features[:, cy - 1], "gy", 1)
    yr = shift(features[:, 0], "gy", -1)
    fv, mv, pooled, m = pool(features, tile_mask, pool_map, w_query, w_key)
    flat = lambda row: jnp.concatenate([yl[row], features[row].reshape(cy * tile, chan), yr[row]], axis=0)
    xl = shift(flat(cx - 1), "gx", 1)
    xr = shift(flat(0), "gx", -1)
    gathered = pooled[None]
    ids = np.zeros((1, 2), np.int32)
    steps = [("gx", 0, 1 << b) for b in range(nx.bit_length() - 1)]
    steps += [("gy", 1, 1 << b) for b in reversed(range(ny.bit_length() - 1))]
    inner = cx - 2
    cuts = [inner * i // len(steps) for i in range(len(steps) + 1)]
    pieces, starts = [], []
    for (axis, dim, bit), lo, hi in zip(steps, cuts, cuts[1:]):
        gathered = jnp.concatenate([gathered, swap(gathered, axis, bit)], axis=0)
        other = ids.copy()
        other[:, dim] ^= bit
        ids = np.concatenate([ids, other])
        if hi > lo:
            starts.append((1 + lo, hi - lo))
            pieces.append(fine(1 + lo, hi - lo, fv, mv, m, yl, yr))
    pieces.append(fine(0, 0, fv, mv, m, yl, yr, (xl, xr)))
    starts.append((None, 2))
    domain = (ids[:, 0] ^ mx) * ny + (ids[:, 1] ^ my)
    mine = lax.dynamic_index_in_dim(readers, mx * ny + my, 0, keepdims=False)
    live = jnp.any(mine[:, None] == domain[None, :], axis=0).astype(F32)
    live = jnp.repeat(live, S)[None]
    return final(tuple(starts), pieces, gathered, pooled, live, pool_map, w_cquery, w_ckey, w_cvalue, w_value)


def solution(mesh):
    in_specs = (P("gx", "gy", None, None), P("gx", "gy", None), P("gx", "gy", None)) + (P(),) * 7
    return jax.shard_map(
        per_device, mesh=mesh, in_specs=in_specs, out_specs=P("gx", "gy", None, None), check_vma=False
    )
```

```python
import functools
import math

import jax
import jax.numpy as jnp
from jax import lax
from jax.experimental import pallas as pl
from jax.experimental.pallas import tpu as pltpu
from jax.sharding import PartitionSpec as P

BF16 = jnp.bfloat16
F32 = jnp.float32
S = 64
DEPTH = 2
IN_VMEM = pl.BlockSpec(memory_space=pltpu.VMEM)
IN_HBM = pl.BlockSpec(memory_space=pltpu.HBM)


def dot(a, b):
    return jnp.dot(a, b, preferred_element_type=F32)


def dot_t(a, b):
    return lax.dot_general(a, b, (((1,), (1,)), ((), ())), preferred_element_type=F32)


def t_dot(a, b):
    return lax.dot_general(a, b, (((0,), (0,)), ((), ())), preferred_element_type=F32)


def in_hbm(array):
    return pltpu.with_memory_space_constraint(array, pltpu.HBM)


def params(mib):
    return pltpu.CompilerParams(vmem_limit_bytes=mib * 1024 * 1024)


def paired(ids):
    half = ids.shape[0] // 2
    return jnp.concatenate([ids[:half], ids[half:]], axis=1)


def pool_kernel(tile, f_ref, pm_ref, tm_ref, wq_ref, wk_ref, fv_ref, pv_ref, mv_ref, m_ref, pooled_ref, up_ref, down_ref, tv, wq, wk, sems):
    rows, span, chan = fv_ref.shape
    cy = span // tile
    small = [(pm_ref, pv_ref), (tm_ref, tv), (wq_ref, wq), (wk_ref, wk)]
    first = [pltpu.make_async_copy(src, dst, sems.at[rows + i]) for i, (src, dst) in enumerate(small)]
    for copy in first:
        copy.start()
    for r in range(rows):
        pltpu.make_async_copy(f_ref.at[r], fv_ref.at[r], sems.at[r]).start()
    for copy in first:
        copy.wait()
    m_ref[...] = (dot_t(wq[...], wk[...]) * (0.5 / math.sqrt(chan))).astype(BF16)

    node = lax.broadcasted_iota(jnp.int32, (S, 2 * tile), 0)
    order = [c for i in range(cy // 2) for c in (i, i + cy // 2)]
    block = lax.broadcasted_iota(jnp.int32, (18, 12 * tile), 1) // tile
    which = lax.broadcasted_iota(jnp.int32, (18, 12 * tile), 0)
    offset, second = which % 9, which // 9
    hit = (offset // 3 == block // 4) & (offset % 3 == block % 4 - second)
    pick = jnp.where(hit, 1 / math.sqrt(tile), 0.0).astype(BF16)
    even = lax.broadcasted_iota(jnp.int32, (9, cy), 1) % 2 == 0

    def row_step(r, total):
        mask = tv[pl.ds(r, 9, stride=rows), :].astype(F32)
        both = jnp.concatenate([jnp.where(even, mask, 0.0), jnp.where(even, 0.0, mask)], axis=0)
        mv_ref[r] = t_dot(both.astype(BF16), pick)
        pairs = paired(pv_ref[r])
        onehot = jnp.concatenate(
            [(jnp.broadcast_to(pairs[i : i + 1], node.shape) == node).astype(F32).astype(BF16) for i in range(cy // 2)],
            axis=1,
        )
        pltpu.make_async_copy(f_ref.at[r], fv_ref.at[r], sems.at[r]).wait()
        beads = jnp.concatenate([fv_ref[r, tile * c : tile * (c + 1)] for c in order], axis=0)
        return total + dot(onehot, beads)

    total = lax.fori_loop(0, rows, row_step, jnp.zeros((S, chan), F32), unroll=4)
    pooled = (total * math.sqrt(S / (rows * span))).astype(BF16)
    pooled_ref[...] = pooled
    for ref, r in ((up_ref, rows - 1), (down_ref, 0)):
        ref[:span] = fv_ref[r]
        ref[span:] = pooled


def pool(features, tile_mask, pool_map, w_query, w_key):
    cx, cy, tile, chan = features.shape
    span = cy * tile
    edge = jax.ShapeDtypeStruct((span + S, chan), BF16)
    return pl.pallas_call(
        functools.partial(pool_kernel, tile),
        in_specs=[IN_HBM] * 5,
        out_specs=[IN_VMEM] * 7,
        out_shape=[
            pltpu.VMEM((cx, span, chan), BF16),
            pltpu.VMEM((cx, cy, tile), jnp.int32),
            pltpu.VMEM((cx, cy, 12 * tile), F32),
            pltpu.VMEM((chan, chan), BF16),
            jax.ShapeDtypeStruct((S, chan), BF16),
            edge,
            edge,
        ],
        scratch_shapes=[
            pltpu.VMEM((9 * cx, cy), jnp.int32),
            pltpu.VMEM((chan, chan), BF16),
            pltpu.VMEM((chan, chan), BF16),
            pltpu.SemaphoreType.DMA((cx + 4,)),
        ],
        compiler_params=params(16),
        name="pool",
    )(
        in_hbm(features.reshape(cx, span, chan)),
        in_hbm(pool_map),
        in_hbm(jnp.transpose(tile_mask, (2, 0, 1)).reshape(9 * cx, cy)),
        in_hbm(w_query),
        in_hbm(w_key),
    )


def attend(tile, tasks):
    waiting = []

    def finish(task, weights):
        _, windows, _, store = task
        near = jnp.concatenate([window() for window in windows], axis=0)
        store(dot(jnp.concatenate(weights, axis=1), near).astype(BF16))

    for task in tasks:
        query, windows, masks, _ = task
        weights = []
        for r, window in enumerate(windows):
            half = dot_t(query, window()).astype(BF16)
            lanes = slice(4 * tile * r, 4 * tile * (r + 1))
            mask = jnp.concatenate([jnp.broadcast_to(masks(h, lanes), (tile, 4 * tile)) for h in (0, 1)], axis=0)
            weights.append((half * jnp.tanh(half) + half) * mask.astype(BF16))
        waiting.append((task, weights))
        if len(waiting) > DEPTH:
            finish(*waiting.pop(0))
    while waiting:
        finish(*waiting.pop(0))


def inner_tasks(refs, row, above, here, below):
    fv, pv, mv, m, o = refs
    _, span, chan = fv.shape
    cy, tile = pv.shape[1:]
    pairs = paired(pv[row])
    node = lax.broadcasted_iota(jnp.int32, (chan, 2 * tile), 0)
    for i in range(cy // 2):
        turned = (jnp.broadcast_to(pairs[i : i + 1], node.shape) == node).astype(F32).T.astype(BF16)
        o[row, tile * i : tile * (i + 1), chan:] = turned[:tile]
        o[row, span // 2 + tile * i : span // 2 + tile * (i + 1), chan:] = turned[tile:]
    queries = dot(here(2 * tile, span - 2 * tile), m[...]).astype(BF16)
    tasks = []
    for j in range(1, cy // 2 - 1):
        lo = 2 * tile * j

        def store(value, lo=lo):
            o[row, lo : lo + 2 * tile, :chan] = value

        tasks.append((
            queries[lo - 2 * tile : lo],
            [functools.partial(near, lo - tile, lo + 3 * tile) for near in (above, here, below)],
            lambda h, lanes, j=j: mv[row, 2 * j + h : 2 * j + h + 1, lanes],
            store,
        ))
    return tasks


def rows_of(ref, row):
    return lambda lo, hi: ref[row, lo:hi]


def flat(ref):
    return lambda lo, hi: ref[lo:hi]


def inner_kernel(first, count, has_out, n_ties, fv, pv, mv, m, *rest):
    o = rest[-1]
    tile = pv.shape[2]
    refs = (fv, pv, mv, m, o)

    def body(row, many):
        tasks = []
        for k in range(many):
            tasks += inner_tasks(refs, row + k, rows_of(fv, row + k - 1), rows_of(fv, row + k), rows_of(fv, row + k + 1))
        attend(tile, tasks)

    if count // 2:

        @pl.loop(0, count // 2)
        def _(i):
            body(first + 2 * i, 2)

    if count % 2:
        body(first + count - 1, 1)


def ends_kernel(fv, pv, mv, m, out_in, above, below, o):
    tile = pv.shape[2]
    last = fv.shape[0] - 1
    refs = (fv, pv, mv, m, o)
    attend(
        tile,
        inner_tasks(refs, 0, flat(above), rows_of(fv, 0), rows_of(fv, 1))
        + inner_tasks(refs, last, rows_of(fv, last - 1), rows_of(fv, last), flat(below)),
    )


def sides_kernel(fv, pv, mv, m, out_in, above, below, left, right, *rest):
    o = rest[-1]
    rows, span, chan = fv.shape
    cy, tile = pv.shape[1:]
    side = 2 * tile
    tasks = []
    for row in range(rows):
        for j in (0, cy // 2 - 1):
            lo = side * j

            def window(r, j=j):
                near = flat(above) if r < 0 else flat(below) if r == rows else rows_of(fv, r)
                halo = (left if j == 0 else right)[tile * (r + 1) : tile * (r + 2)]
                own = near(0, 3 * tile) if j == 0 else near(span - 3 * tile, span)
                return jnp.concatenate([halo, own] if j == 0 else [own, halo], axis=0)

            def store(value, row=row, lo=lo):
                o[row, lo : lo + side, :chan] = value

            tasks.append((
                dot(fv[row, lo : lo + side], m[...]).astype(BF16),
                [functools.partial(window, r) for r in (row - 1, row, row + 1)],
                lambda h, lanes, row=row, j=j: mv[row, 2 * j + h : 2 * j + h + 1, lanes],
                store,
            ))
    attend(tile, tasks)


def piece(kernel, rows_done, name, base, out, near=(), ties=()):
    fv, _, _, _ = base
    cx, span, chan = fv.shape
    done = [] if out is None else [out]
    return pl.pallas_call(
        kernel,
        in_specs=[IN_VMEM] * (4 + len(done) + len(near)) + [pl.BlockSpec(memory_space=pl.ANY)] * len(ties),
        out_specs=IN_VMEM,
        out_shape=pltpu.VMEM((cx, span, 2 * chan), BF16),
        input_output_aliases={4: 0} if done else {},
        compiler_params=params(16),
        cost_estimate=pl.CostEstimate(
            flops=int(rows_done * 1_200_000_000), bytes_accessed=1_000_000, transcendentals=0
        ),
        name=name,
    )(*base, *done, *near, *ties)


def final_kernel(nx, ny, g0_ref, g1_ref, readers_ref, wcq_ref, wck_ref, wcv_ref, wv_ref, o_ref, out_ref, mix, rows_out, sems):
    cx, span, chan = rows_out.shape
    nodes = jnp.concatenate([g0_ref[...], g1_ref[...]], axis=0)
    count = nodes.shape[0]
    mx, my = lax.axis_index("gx"), lax.axis_index("gy")
    block = lax.broadcasted_iota(jnp.int32, (readers_ref.shape[0], count), 1) // S
    domain = ((block % nx) ^ mx) * ny + ((block // nx) ^ my)
    lane = lax.broadcasted_iota(jnp.int32, readers_ref.shape, 1)
    mine = jnp.sum(jnp.where(lane == mx * ny + my, readers_ref[...], 0), axis=1, keepdims=True)
    live = jnp.sum(jnp.where(domain == mine, 1.0, 0.0), axis=0, keepdims=True)
    query = dot(nodes[:S], wcq_ref[...]).astype(BF16)
    key = dot(nodes, wck_ref[...]).astype(BF16)
    value = dot(nodes, wcv_ref[...]).astype(BF16)
    half = dot_t(query, key) * (0.5 / math.sqrt(chan))
    weight = (half * jnp.tanh(half) + half).astype(BF16).astype(F32) * live
    mix[:chan] = wv_ref[...]
    mix[chan : chan + S] = (dot(weight.astype(BF16), value) / math.sqrt(S)).astype(BF16)
    mix[chan + S :] = jnp.zeros((chan - S, chan), BF16)

    def send(r):
        return pltpu.make_async_copy(rows_out.at[r], out_ref.at[r], sems.at[r])

    @pl.loop(0, cx)
    def _(r):
        rows_out[r] = dot(o_ref[r], mix[...]).astype(BF16)
        send(r).start()

    @pl.loop(0, cx)
    def _(r):
        send(r).wait()


def final(nx, ny, g0, g1, readers, w_cquery, w_ckey, w_cvalue, w_value, out):
    cx, span, wide = out.shape
    chan = wide // 2
    return pl.pallas_call(
        functools.partial(final_kernel, nx, ny),
        in_specs=[IN_VMEM] * 8,
        out_specs=IN_HBM,
        out_shape=jax.ShapeDtypeStruct((cx, span, chan), BF16),
        scratch_shapes=[
            pltpu.VMEM((2 * chan, chan), BF16),
            pltpu.VMEM((cx, span, chan), BF16),
            pltpu.SemaphoreType.DMA((cx,)),
        ],
        compiler_params=params(16),
        name="final",
    )(g0, g1, readers.T, w_cquery, w_ckey, w_cvalue, w_value, out)


def shift(array, axis, step):
    count = lax.axis_size(axis)
    return lax.ppermute(array, axis, [(i, i + step) for i in range(count) if 0 <= i + step < count])


def swap(array, axis, bit):
    return lax.ppermute(array, axis, [(i, i ^ bit) for i in range(lax.axis_size(axis))])


def pack_kernel(axis, lo, own_ref, before_ref, after_ref, out_ref):
    size = own_ref.shape[0]
    out_ref[:size] = own_ref[...]
    odd = lax.axis_index(axis) % 2 == 1

    @pl.when(odd)
    def _():
        out_ref[size:] = before_ref[lo : lo + size]

    @pl.when(jnp.logical_not(odd))
    def _():
        out_ref[size:] = after_ref[lo : lo + size]


def pack_pair(axis, lo, own, before, after):
    return pl.pallas_call(
        functools.partial(pack_kernel, axis, lo),
        in_specs=[IN_VMEM] * 3,
        out_specs=IN_VMEM,
        out_shape=pltpu.VMEM((2 * own.shape[0], own.shape[1]), BF16),
        compiler_params=params(4),
        name="pair_" + axis,
    )(own, before, after)


def join_kernel(first_ref, second_ref, out_ref):
    size = first_ref.shape[0]
    out_ref[:size] = first_ref[...]
    out_ref[size:] = second_ref[...]


def join(first, second):
    return pl.pallas_call(
        join_kernel,
        in_specs=[IN_VMEM] * 2,
        out_specs=IN_VMEM,
        out_shape=pltpu.VMEM((2 * first.shape[0], first.shape[1]), BF16),
        compiler_params=params(4),
        name="join",
    )(first, second)


def columns_kernel(tile, fv_ref, above_ref, below_ref, first_ref, second_ref, left_ref, right_ref, blocks_ref):
    rows, span, _ = fv_ref.shape
    size = first_ref.shape[0]
    halo = (rows + 2) * tile
    for ref, lo in ((left_ref, 0), (right_ref, span - tile)):
        ref[:tile] = above_ref[lo : lo + tile]
        for r in range(rows):
            ref[(r + 1) * tile : (r + 2) * tile] = fv_ref[r, lo : lo + tile]
        ref[halo - tile : halo] = below_ref[lo : lo + tile]
        ref[halo : halo + size] = first_ref[...]
        ref[halo + size :] = second_ref[...]
    blocks_ref[:size] = first_ref[...]
    blocks_ref[size:] = second_ref[...]


def columns(tile, fv, above, below, first, second):
    rows, _, chan = fv.shape
    count = 2 * first.shape[0]
    edge = pltpu.VMEM(((rows + 2) * tile + count, chan), BF16)
    return pl.pallas_call(
        functools.partial(columns_kernel, tile),
        in_specs=[IN_VMEM] * 5,
        out_specs=[IN_VMEM] * 3,
        out_shape=[edge, edge, pltpu.VMEM((count, chan), BF16)],
        compiler_params=params(4),
        name="columns",
    )(fv, above, below, first, second)


def per_device(features, tile_mask, pool_map, readers, w_query, w_key, w_value, w_cquery, w_ckey, w_cvalue):
    cx, cy, tile, chan = features.shape
    span = cy * tile
    nx, ny = lax.axis_size("gx"), lax.axis_size("gy")
    *base, pooled, up, down = pool(features, tile_mask, pool_map, w_query, w_key)
    fv = base[0]

    def inner(first, count, out, ties):
        kernel = functools.partial(inner_kernel, first, count, out is not None, len(ties))
        return piece(kernel, 0.75 * count, f"inner_{first}", base, out, (), ties)

    cuts = [1, 1 + (cx - 2) * 5 // 14, 1 + (cx - 2) * 7 // 14, cx - 1]
    above = shift(up, "gx", 1)
    below = shift(down, "gx", -1)
    out = inner(cuts[0], cuts[1] - cuts[0], None, ())
    first = pack_pair("gx", span, pooled, above, below)
    second = swap(first, "gx", 2)
    out = inner(cuts[1], cuts[2] - cuts[1], out, (first,))
    for bit in (1 << b for b in range(2, nx.bit_length() - 1)):
        first = join(first, second)
        second = swap(first, "gx", bit)
    to_left, to_right, blocks = columns(tile, fv, above, below, first, second)
    left = shift(to_right, "gy", 1)
    right = shift(to_left, "gy", -1)
    out = inner(cuts[2], cuts[3] - cuts[2], out, (to_right, to_left))
    first = pack_pair("gy", (cx + 2) * tile, blocks, left, right)
    second = swap(first, "gy", 2)
    out = piece(ends_kernel, 1.5, "ends", base, out, (above, below))
    for bit in (1 << b for b in range(2, ny.bit_length() - 1)):
        first = join(first, second)
        second = swap(first, "gy", bit)
    out = piece(sides_kernel, 4, "sides", base, out, (above, below, left, right), (first,))
    update = final(nx, ny, first, second, readers, w_cquery, w_ckey, w_cvalue, w_value, out)
    return update.reshape(features.shape)


def solution(mesh):
    in_specs = (P("gx", "gy", None, None), P("gx", "gy", None), P("gx", "gy", None)) + (P(),) * 7
    return jax.shard_map(
        per_device, mesh=mesh, in_specs=in_specs, out_specs=P("gx", "gy", None, None), check_vma=False
    )
```

```python
import functools
import math

import jax
import jax.numpy as jnp
from jax import lax
from jax.experimental import pallas as pl
from jax.experimental.pallas import tpu as pltpu
from jax.sharding import PartitionSpec as P

BF16 = jnp.bfloat16
F32 = jnp.float32
S = 64
DEPTH = 2
IN_VMEM = pl.BlockSpec(memory_space=pltpu.VMEM)
IN_HBM = pl.BlockSpec(memory_space=pltpu.HBM)


def dot(a, b):
    return jnp.dot(a, b, preferred_element_type=F32)


def dot_t(a, b):
    return lax.dot_general(a, b, (((1,), (1,)), ((), ())), preferred_element_type=F32)


def t_dot(a, b):
    return lax.dot_general(a, b, (((0,), (0,)), ((), ())), preferred_element_type=F32)


def in_hbm(array):
    return pltpu.with_memory_space_constraint(array, pltpu.HBM)


def params(mib):
    return pltpu.CompilerParams(vmem_limit_bytes=mib * 1024 * 1024)


def paired(ids):
    half = ids.shape[0] // 2
    return jnp.concatenate([ids[:half], ids[half:]], axis=1)


def pool_kernel(tile, f_ref, pm_ref, tm_ref, wq_ref, wk_ref, fv_ref, pv_ref, mv_ref, m_ref, pooled_ref, left_ref, right_ref, tv, wq, wk, sems):
    rows, span, chan = fv_ref.shape
    cy = span // tile
    small = [(tm_ref, tv), (wq_ref, wq), (wk_ref, wk), (pm_ref, pv_ref)]
    first = [pltpu.make_async_copy(src, dst, sems.at[rows + i]) for i, (src, dst) in enumerate(small)]
    beads_in = [pltpu.make_async_copy(f_ref.at[r], fv_ref.at[r], sems.at[r]) for r in range(rows)]
    for copy in first + beads_in:
        copy.start()
    block = lax.broadcasted_iota(jnp.int32, (18, 12 * tile), 1) // tile
    which = lax.broadcasted_iota(jnp.int32, (18, 12 * tile), 0)
    offset, second = which % 9, which // 9
    hit = (offset // 3 == block // 4) & (offset % 3 == block % 4 - second)
    pick = jnp.where(hit, 1 / math.sqrt(tile), 0.0).astype(BF16)
    for copy in first:
        copy.wait()
    m_ref[...] = (dot_t(wq[...], wk[...]) * (0.5 / math.sqrt(chan))).astype(BF16)
    mask = jnp.concatenate([tv[pl.ds(r, 9, stride=rows), :].astype(F32) for r in range(rows)], axis=1)
    even = lax.broadcasted_iota(jnp.int32, mask.shape, 1) % 2 == 0
    both = jnp.concatenate([jnp.where(even, mask, 0.0), jnp.where(even, 0.0, mask)], axis=0)
    mv_ref[...] = t_dot(both.astype(BF16), pick)

    node = lax.broadcasted_iota(jnp.int32, (S, 2 * tile), 0)
    order = [c for i in range(cy // 2) for c in (i, i + cy // 2)]
    total = jnp.zeros((S, chan), F32)
    for r in range(rows):
        pairs = paired(pv_ref[r])
        onehot = jnp.concatenate(
            [(jnp.broadcast_to(pairs[i : i + 1], node.shape) == node).astype(F32).astype(BF16) for i in range(cy // 2)],
            axis=1,
        )
        beads_in[r].wait()
        total += dot(onehot, jnp.concatenate([fv_ref[r, tile * c : tile * (c + 1)] for c in order], axis=0))
        left_ref[tile * r : tile * (r + 1)] = fv_ref[r, :tile]
        right_ref[tile * r : tile * (r + 1)] = fv_ref[r, span - tile :]
    pooled_ref[...] = (total * math.sqrt(S / (rows * span))).astype(BF16)


def pool(features, tile_mask, pool_map, w_query, w_key):
    cx, cy, tile, chan = features.shape
    span = cy * tile
    edge = pltpu.VMEM((cx * tile, chan), BF16)
    return pl.pallas_call(
        functools.partial(pool_kernel, tile),
        in_specs=[IN_HBM] * 5,
        out_specs=[IN_VMEM] * 7,
        out_shape=[
            pltpu.VMEM((cx, span, chan), BF16),
            pltpu.VMEM((cx, cy, tile), jnp.int32),
            pltpu.VMEM((cx * cy, 12 * tile), F32),
            pltpu.VMEM((chan, chan), BF16),
            pltpu.VMEM((S, chan), BF16),
            edge,
            edge,
        ],
        scratch_shapes=[
            pltpu.VMEM((9 * cx, cy), jnp.int32),
            pltpu.VMEM((chan, chan), BF16),
            pltpu.VMEM((chan, chan), BF16),
            pltpu.SemaphoreType.DMA((cx + 4,)),
        ],
        compiler_params=params(16),
        name="pool",
    )(
        in_hbm(features.reshape(cx, span, chan)),
        in_hbm(pool_map),
        in_hbm(jnp.transpose(tile_mask, (2, 0, 1)).reshape(9 * cx, cy)),
        in_hbm(w_query),
        in_hbm(w_key),
    )


def attend(tile, tasks):
    waiting = []

    def finish(task, weights):
        _, windows, _, store = task
        near = jnp.concatenate([window() for window in windows], axis=0)
        store(dot(jnp.concatenate(weights, axis=1), near).astype(BF16))

    for task in tasks:
        query, windows, masks, _ = task
        weights = []
        for r, window in enumerate(windows):
            half = dot_t(query, window()).astype(BF16)
            lanes = slice(4 * tile * r, 4 * tile * (r + 1))
            mask = jnp.concatenate([jnp.broadcast_to(masks(h, lanes), (tile, 4 * tile)) for h in (0, 1)], axis=0)
            weights.append((half * jnp.tanh(half) + half) * mask.astype(BF16))
        waiting.append((task, weights))
        if len(waiting) > DEPTH:
            finish(*waiting.pop(0))
    while waiting:
        finish(*waiting.pop(0))


def inner_tasks(refs, row, above, here, below):
    fv, pv, mv, m, o = refs
    _, span, chan = fv.shape
    cy, tile = pv.shape[1:]
    pairs = paired(pv[row])
    node = lax.broadcasted_iota(jnp.int32, (chan, 2 * tile), 0)
    for i in range(cy // 2):
        turned = (jnp.broadcast_to(pairs[i : i + 1], node.shape) == node).astype(F32).T.astype(BF16)
        o[row, tile * i : tile * (i + 1), chan:] = turned[:tile]
        o[row, span // 2 + tile * i : span // 2 + tile * (i + 1), chan:] = turned[tile:]
    queries = dot(here(2 * tile, span - 2 * tile), m[...]).astype(BF16)
    tasks = []
    for j in range(1, cy // 2 - 1):
        lo = 2 * tile * j

        def store(value, lo=lo):
            o[row, lo : lo + 2 * tile, :chan] = value

        tasks.append((
            queries[lo - 2 * tile : lo],
            [functools.partial(near, lo - tile, lo + 3 * tile) for near in (above, here, below)],
            lambda h, lanes, j=j: mv[pl.ds(row * cy + 2 * j + h, 1), lanes],
            store,
        ))
    return tasks


def rows_of(ref, row):
    return lambda lo, hi: ref[row, lo:hi]


def wide(tile, ref):
    return lambda lo, hi: ref[lo + tile : hi + tile]


def inner_kernel(first, count, fv, pv, mv, m, *rest):
    o = rest[-1]
    tile = pv.shape[2]
    refs = (fv, pv, mv, m, o)

    def body(row, many):
        tasks = []
        for k in range(many):
            tasks += inner_tasks(refs, row + k, rows_of(fv, row + k - 1), rows_of(fv, row + k), rows_of(fv, row + k + 1))
        attend(tile, tasks)

    if count // 2:

        @pl.loop(0, count // 2)
        def _(i):
            body(first + 2 * i, 2)

    if count % 2:
        body(first + count - 1, 1)


def ends_kernel(fv, pv, mv, m, out_in, above, below, o):
    tile = pv.shape[2]
    last = fv.shape[0] - 1
    refs = (fv, pv, mv, m, o)
    attend(
        tile,
        inner_tasks(refs, 0, wide(tile, above), rows_of(fv, 0), rows_of(fv, 1))
        + inner_tasks(refs, last, rows_of(fv, last - 1), rows_of(fv, last), wide(tile, below)),
    )


def sides_kernel(fv, pv, mv, m, out_in, above, below, left, right, *rest):
    o = rest[-1]
    rows, span, chan = fv.shape
    cy, tile = pv.shape[1:]
    side = 2 * tile
    tasks = []
    for row in range(rows):
        for j in (0, cy // 2 - 1):
            lo = side * j

            def window(r, j=j):
                if r in (-1, rows):
                    lo = 0 if j == 0 else span - 2 * tile
                    return (above if r < 0 else below)[lo : lo + 4 * tile]
                halo = (left if j == 0 else right)[tile * r : tile * (r + 1)]
                own = fv[r, : 3 * tile] if j == 0 else fv[r, span - 3 * tile :]
                return jnp.concatenate([halo, own] if j == 0 else [own, halo], axis=0)

            def store(value, row=row, lo=lo):
                o[row, lo : lo + side, :chan] = value

            tasks.append((
                dot(fv[row, lo : lo + side], m[...]).astype(BF16),
                [functools.partial(window, r) for r in (row - 1, row, row + 1)],
                lambda h, lanes, lo=row * cy + 2 * j: mv[lo + h : lo + h + 1, lanes],
                store,
            ))
    attend(tile, tasks)


def piece(kernel, rows_done, name, base, out, near=(), ties=()):
    fv, _, _, _ = base
    cx, span, chan = fv.shape
    done = [] if out is None else [out]
    return pl.pallas_call(
        kernel,
        in_specs=[IN_VMEM] * (4 + len(done) + len(near)) + [pl.BlockSpec(memory_space=pl.ANY)] * len(ties),
        out_specs=IN_VMEM,
        out_shape=pltpu.VMEM((cx, span, 2 * chan), BF16),
        input_output_aliases={4: 0} if done else {},
        compiler_params=params(16),
        cost_estimate=pl.CostEstimate(
            flops=int(rows_done * 1_200_000_000), bytes_accessed=1_000_000, transcendentals=0
        ),
        name=name,
    )(*base, *done, *near, *ties)


def final_kernel(nx, ny, n_blocks, *refs):
    blocks = refs[:n_blocks]
    readers_ref, wcq_ref, wck_ref, wcv_ref, wv_ref, o_ref, out_ref, mix, rows_out, sems = refs[n_blocks:]
    cx, span, chan = rows_out.shape
    nodes = jnp.concatenate([ref[...] for ref in blocks], axis=0)
    count = nodes.shape[0]
    mx, my = lax.axis_index("gx"), lax.axis_index("gy")
    block = lax.broadcasted_iota(jnp.int32, (readers_ref.shape[0], count), 1) // S
    rest = block // nx
    turn = (rest % (ny // 2)) * 2 + rest // (ny // 2)
    domain = ((block % nx) ^ mx) * ny + (turn ^ my)
    lane = lax.broadcasted_iota(jnp.int32, readers_ref.shape, 1)
    mine = jnp.sum(jnp.where(lane == mx * ny + my, readers_ref[...], 0), axis=1, keepdims=True)
    live = jnp.sum(jnp.where(domain == mine, 1.0, 0.0), axis=0, keepdims=True)
    query = dot(nodes[:S], wcq_ref[...]).astype(BF16)
    key = dot(nodes, wck_ref[...]).astype(BF16)
    value = dot(nodes, wcv_ref[...]).astype(BF16)
    half = dot_t(query, key) * (0.5 / math.sqrt(chan))
    weight = (half * jnp.tanh(half) + half).astype(BF16).astype(F32) * live
    mix[:chan] = wv_ref[...]
    mix[chan : chan + S] = (dot(weight.astype(BF16), value) / math.sqrt(S)).astype(BF16)
    mix[chan + S :] = jnp.zeros((chan - S, chan), BF16)

    def send(r):
        return pltpu.make_async_copy(rows_out.at[r], out_ref.at[r], sems.at[r])

    for r in range(cx):
        rows_out[r] = dot(o_ref[r], mix[...]).astype(BF16)
        send(r).start()
    for r in range(cx):
        send(r).wait()


def final(nx, ny, blocks, readers, w_cquery, w_ckey, w_cvalue, w_value, out):
    cx, span, wide = out.shape
    chan = wide // 2
    return pl.pallas_call(
        functools.partial(final_kernel, nx, ny, len(blocks)),
        in_specs=[IN_VMEM] * (len(blocks) + 6),
        out_specs=IN_HBM,
        out_shape=jax.ShapeDtypeStruct((cx, span, chan), BF16),
        scratch_shapes=[
            pltpu.VMEM((2 * chan, chan), BF16),
            pltpu.VMEM((cx, span, chan), BF16),
            pltpu.SemaphoreType.DMA((cx,)),
        ],
        compiler_params=params(16),
        name="final",
    )(*blocks, readers.T, w_cquery, w_ckey, w_cvalue, w_value, out)


def shift(array, axis, step):
    count = lax.axis_size(axis)
    return lax.ppermute(array, axis, [(i, i + step) for i in range(count) if 0 <= i + step < count])


def swap(array, axis, bits):
    return lax.ppermute(array, axis, [(i, i ^ bits) for i in range(lax.axis_size(axis))])


def join_kernel(count, *refs):
    parts, out = refs[:count], refs[-1]
    at = 0
    for part in parts:
        out[at : at + part.shape[0]] = part[...]
        at += part.shape[0]


def join(parts, ties):
    rows = sum(part.shape[0] for part in parts)
    return pl.pallas_call(
        functools.partial(join_kernel, len(parts)),
        in_specs=[IN_VMEM] * len(parts) + [pl.BlockSpec(memory_space=pl.ANY)] * len(ties),
        out_specs=IN_VMEM,
        out_shape=pltpu.VMEM((rows, parts[0].shape[1]), BF16),
        compiler_params=params(4),
        name="join",
    )(*parts, *ties)


def edge_rows_kernel(tile, fv_ref, left_ref, right_ref, up_ref, down_ref):
    rows, span, _ = fv_ref.shape
    for ref, r in ((up_ref, rows - 1), (down_ref, 0)):
        ref[:tile] = left_ref[tile * r : tile * (r + 1)]
        ref[tile : tile + span] = fv_ref[r]
        ref[tile + span :] = right_ref[tile * r : tile * (r + 1)]


def edge_rows(tile, fv, left, right):
    _, span, chan = fv.shape
    edge = pltpu.VMEM((span + 2 * tile, chan), BF16)
    return pl.pallas_call(
        functools.partial(edge_rows_kernel, tile),
        in_specs=[IN_VMEM] * 3,
        out_specs=[IN_VMEM] * 2,
        out_shape=[edge, edge],
        compiler_params=params(4),
        name="edge_rows",
    )(fv, left, right)


def per_device(features, tile_mask, pool_map, readers, w_query, w_key, w_value, w_cquery, w_ckey, w_cvalue):
    cx, cy, tile, chan = features.shape
    nx, ny = lax.axis_size("gx"), lax.axis_size("gy")
    *base, pooled, left_edge, right_edge = pool(features, tile_mask, pool_map, w_query, w_key)
    fv = base[0]

    def inner(first, count, out, ties):
        return piece(functools.partial(inner_kernel, first, count), 0.75 * count, f"inner_{first}", base, out, (), ties)

    cuts = [1, 1 + (cx - 2) * 4 // 14, 1 + (cx - 2) * 10 // 14, cx - 1]
    blocks = [pooled] + [swap(pooled, "gx", bits) for bits in range(1, nx)]
    left = shift(right_edge, "gy", 1)
    right = shift(left_edge, "gy", -1)
    out = inner(cuts[0], cuts[1] - cuts[0], None, ())
    part = join(blocks, (out,))
    blocks = [part] + [swap(part, "gy", bits) for bits in range(2, ny, 2)]
    up, down = edge_rows(tile, fv, left, right)
    above = shift(up, "gx", 1)
    below = shift(down, "gx", -1)
    out = inner(cuts[1], cuts[2] - cuts[1], out, (part, up))
    part = join(blocks, (out,))
    blocks = [part, swap(part, "gy", 1)]
    out = inner(cuts[2], cuts[3] - cuts[2], out, (part,))
    out = piece(ends_kernel, 1.5, "ends", base, out, (above, below))
    out = piece(sides_kernel, 4, "sides", base, out, (above, below, left, right))
    update = final(nx, ny, blocks, readers, w_cquery, w_ckey, w_cvalue, w_value, out)
    return update.reshape(features.shape)


def solution(mesh):
    in_specs = (P("gx", "gy", None, None), P("gx", "gy", None), P("gx", "gy", None)) + (P(),) * 7
    return jax.shard_map(
        per_device, mesh=mesh, in_specs=in_specs, out_specs=P("gx", "gy", None, None), check_vma=False
    )
```

```python
import functools
import math

import jax
import jax.numpy as jnp
from jax import lax
from jax.experimental import pallas as pl
from jax.experimental.pallas import tpu as pltpu
from jax.sharding import PartitionSpec as P

BF16 = jnp.bfloat16
F32 = jnp.float32
S = 64
DEPTH = 2
IN_VMEM = pl.BlockSpec(memory_space=pltpu.VMEM)
IN_HBM = pl.BlockSpec(memory_space=pltpu.HBM)


def dot(a, b):
    return jnp.dot(a, b, preferred_element_type=F32)


def dot_t(a, b):
    return lax.dot_general(a, b, (((1,), (1,)), ((), ())), preferred_element_type=F32)


def t_dot(a, b):
    return lax.dot_general(a, b, (((0,), (0,)), ((), ())), preferred_element_type=F32)


def in_hbm(array):
    return pltpu.with_memory_space_constraint(array, pltpu.HBM)


def params(mib):
    return pltpu.CompilerParams(vmem_limit_bytes=mib * 1024 * 1024)


def paired(ids):
    half = ids.shape[0] // 2
    return jnp.concatenate([ids[:half], ids[half:]], axis=1)


def pool_kernel(tile, nx, ny, f_ref, pm_ref, tm_ref, wq_ref, wk_ref, fv_ref, pv_ref, mv_ref, m_ref, pooled_ref, left_ref, right_ref, tv, wq, wk, sems):
    rows, span, chan = fv_ref.shape
    cy = span // tile
    small = [(tm_ref, tv), (wq_ref, wq), (wk_ref, wk), (pm_ref, pv_ref)]
    first = [pltpu.make_async_copy(src, dst, sems.at[rows + i]) for i, (src, dst) in enumerate(small)]
    beads_in = [pltpu.make_async_copy(f_ref.at[r], fv_ref.at[r], sems.at[r]) for r in range(rows)]
    for copy in first + beads_in:
        copy.start()
    block = lax.broadcasted_iota(jnp.int32, (18, 12 * tile), 1) // tile
    which = lax.broadcasted_iota(jnp.int32, (18, 12 * tile), 0)
    offset, second = which % 9, which // 9
    hit = (offset // 3 == block // 4) & (offset % 3 == block % 4 - second)
    pick = jnp.where(hit, 1 / math.sqrt(tile), 0.0).astype(BF16)
    for copy in first:
        copy.wait()
    m_ref[...] = (dot_t(wq[...], wk[...]) * (0.5 / math.sqrt(chan))).astype(BF16)
    mask = jnp.concatenate([tv[pl.ds(r, 9, stride=rows), :].astype(F32) for r in range(rows)], axis=1)
    lane = lax.broadcasted_iota(jnp.int32, mask.shape, 1)
    toward = lax.broadcasted_iota(jnp.int32, mask.shape, 0)
    mx, my = lax.axis_index("gx"), lax.axis_index("gy")
    outside = (toward // 3 == 0) & (lane // cy == jnp.where(mx == 0, 0, -1))
    outside |= (toward // 3 == 2) & (lane // cy == jnp.where(mx == nx - 1, rows - 1, -1))
    outside |= (toward % 3 == 0) & (lane % cy == jnp.where(my == 0, 0, -1))
    outside |= (toward % 3 == 2) & (lane % cy == jnp.where(my == ny - 1, cy - 1, -1))
    mask = jnp.where(outside, 0.0, mask)
    even = lane % 2 == 0
    both = jnp.concatenate([jnp.where(even, mask, 0.0), jnp.where(even, 0.0, mask)], axis=0)
    mv_ref[...] = t_dot(both.astype(BF16), pick)

    node = lax.broadcasted_iota(jnp.int32, (S, 2 * tile), 0)
    order = [c for i in range(cy // 2) for c in (i, i + cy // 2)]
    total = jnp.zeros((S, chan), F32)
    for r in range(rows):
        pairs = paired(pv_ref[r])
        onehot = jnp.concatenate(
            [(jnp.broadcast_to(pairs[i : i + 1], node.shape) == node).astype(F32).astype(BF16) for i in range(cy // 2)],
            axis=1,
        )
        beads_in[r].wait()
        total += dot(onehot, jnp.concatenate([fv_ref[r, tile * c : tile * (c + 1)] for c in order], axis=0))
        left_ref[tile * r : tile * (r + 1)] = fv_ref[r, :tile]
        right_ref[tile * r : tile * (r + 1)] = fv_ref[r, span - tile :]
    pooled_ref[...] = (total * math.sqrt(S / (rows * span))).astype(BF16)


def pool(nx, ny, features, tile_mask, pool_map, w_query, w_key):
    cx, cy, tile, chan = features.shape
    span = cy * tile
    edge = pltpu.VMEM((cx * tile, chan), BF16)
    return pl.pallas_call(
        functools.partial(pool_kernel, tile, nx, ny),
        in_specs=[IN_HBM] * 5,
        out_specs=[IN_VMEM] * 7,
        out_shape=[
            pltpu.VMEM((cx, span, chan), BF16),
            pltpu.VMEM((cx, cy, tile), jnp.int32),
            pltpu.VMEM((cx * cy, 12 * tile), F32),
            pltpu.VMEM((chan, chan), BF16),
            pltpu.VMEM((S, chan), BF16),
            edge,
            edge,
        ],
        scratch_shapes=[
            pltpu.VMEM((9 * cx, cy), jnp.int32),
            pltpu.VMEM((chan, chan), BF16),
            pltpu.VMEM((chan, chan), BF16),
            pltpu.SemaphoreType.DMA((cx + 4,)),
        ],
        compiler_params=params(16),
        name="pool",
    )(
        in_hbm(features.reshape(cx, span, chan)),
        in_hbm(pool_map),
        in_hbm(jnp.transpose(tile_mask, (2, 0, 1)).reshape(9 * cx, cy)),
        in_hbm(w_query),
        in_hbm(w_key),
    )


def attend(tile, tasks):
    waiting = []

    def finish(task, weights):
        _, windows, _, store = task
        near = jnp.concatenate([window() for window in windows], axis=0)
        store(dot(jnp.concatenate(weights, axis=1), near).astype(BF16))

    for task in tasks:
        query, windows, masks, _ = task
        weights = []
        for r, window in enumerate(windows):
            half = dot_t(query, window()).astype(BF16)
            lanes = slice(4 * tile * r, 4 * tile * (r + 1))
            mask = jnp.concatenate([jnp.broadcast_to(masks(h, lanes), (tile, 4 * tile)) for h in (0, 1)], axis=0)
            weights.append((half * jnp.tanh(half) + half) * mask.astype(BF16))
        waiting.append((task, weights))
        if len(waiting) > DEPTH:
            finish(*waiting.pop(0))
    while waiting:
        finish(*waiting.pop(0))


def row_tasks(refs, row, first, last, window):
    fv, pv, mv, m, o = refs
    chan = fv.shape[2]
    cy, tile = pv.shape[1:]
    side = 2 * tile
    queries = dot(fv[row, side * first : side * last], m[...]).astype(BF16)
    tasks = []
    for j in range(first, last):

        def store(value, lo=side * j):
            o[row, lo : lo + side, :chan] = value

        tasks.append((
            queries[side * (j - first) : side * (j - first + 1)],
            [functools.partial(window, r, j) for r in (row - 1, row, row + 1)],
            lambda h, lanes, j=j: mv[pl.ds(row * cy + 2 * j + h, 1), lanes],
            store,
        ))
    return tasks


def node_rows(refs, row):
    fv, pv, _, _, o = refs
    _, span, chan = fv.shape
    cy, tile = pv.shape[1:]
    pairs = paired(pv[row])
    node = lax.broadcasted_iota(jnp.int32, (chan, 2 * tile), 0)
    for i in range(cy // 2):
        turned = (jnp.broadcast_to(pairs[i : i + 1], node.shape) == node).astype(F32).T.astype(BF16)
        o[row, tile * i : tile * (i + 1), chan:] = turned[:tile]
        o[row, span // 2 + tile * i : span // 2 + tile * (i + 1), chan:] = turned[tile:]


def inner_kernel(first, count, fv, pv, mv, m, *rest):
    cy, tile = pv.shape[1:]
    refs = (fv, pv, mv, m, rest[-1])

    def window(r, j):
        return fv[r, tile * (2 * j - 1) : tile * (2 * j + 3)]

    def body(row, many):
        tasks = []
        for k in range(many):
            node_rows(refs, row + k)
            tasks += row_tasks(refs, row + k, 1, cy // 2 - 1, window)
        attend(tile, tasks)

    if count // 2:

        @pl.loop(0, count // 2)
        def _(i):
            body(first + 2 * i, 2)

    if count % 2:
        body(first + count - 1, 1)


def side_window(fv, tile, left, right):
    span = fv.shape[1]

    def window(r, j):
        if j == 0:
            return jnp.concatenate([left[tile * r : tile * (r + 1)], fv[r, : 3 * tile]], axis=0)
        if 2 * tile * (j + 1) == span:
            return jnp.concatenate([fv[r, span - 3 * tile :], right[tile * r : tile * (r + 1)]], axis=0)
        return fv[r, tile * (2 * j - 1) : tile * (2 * j + 3)]

    return window


def sides_kernel(fv, pv, mv, m, out_in, left, right, o):
    cy, tile = pv.shape[1:]
    refs = (fv, pv, mv, m, o)
    window = side_window(fv, tile, left, right)
    tasks = []
    for row in range(1, fv.shape[0] - 1):
        for j in (0, cy // 2 - 1):
            tasks += row_tasks(refs, row, j, j + 1, window)
    attend(tile, tasks)


def ends_kernel(fv, pv, mv, m, out_in, left, right, above, below, o):
    cy, tile = pv.shape[1:]
    rows = fv.shape[0]
    refs = (fv, pv, mv, m, o)
    near = side_window(fv, tile, left, right)

    def window(r, j):
        if r in (-1, rows):
            return (above if r < 0 else below)[2 * tile * j : 2 * tile * (j + 2)]
        return near(r, j)

    tasks = []
    for row in (0, rows - 1):
        node_rows(refs, row)
        tasks += row_tasks(refs, row, 0, cy // 2, window)
    attend(tile, tasks)


def piece(kernel, rows_done, name, base, out, near=(), ties=()):
    fv, _, _, _ = base
    cx, span, chan = fv.shape
    done = [] if out is None else [out]
    return pl.pallas_call(
        kernel,
        in_specs=[IN_VMEM] * (4 + len(done) + len(near)) + [pl.BlockSpec(memory_space=pl.ANY)] * len(ties),
        out_specs=IN_VMEM,
        out_shape=pltpu.VMEM((cx, span, 2 * chan), BF16),
        input_output_aliases={4: 0} if done else {},
        compiler_params=params(16),
        cost_estimate=pl.CostEstimate(
            flops=int(rows_done * 400_000_000), bytes_accessed=1_000_000, transcendentals=0
        ),
        name=name,
    )(*base, *done, *near, *ties)


def final_kernel(nx, ny, n_blocks, *refs):
    blocks = refs[:n_blocks]
    readers_ref, wcq_ref, wck_ref, wcv_ref, wv_ref, o_ref, out_ref, mix, rows_out, sems = refs[n_blocks:]
    cx, span, chan = rows_out.shape
    nodes = jnp.concatenate([ref[...] for ref in blocks], axis=0)
    count = nodes.shape[0]
    mx, my = lax.axis_index("gx"), lax.axis_index("gy")
    block = lax.broadcasted_iota(jnp.int32, (readers_ref.shape[0], count), 1) // S
    rest = block // nx
    turn = (rest % (ny // 2)) * 2 + rest // (ny // 2)
    domain = ((block % nx) ^ mx) * ny + (turn ^ my)
    lane = lax.broadcasted_iota(jnp.int32, readers_ref.shape, 1)
    mine = jnp.sum(jnp.where(lane == mx * ny + my, readers_ref[...], 0), axis=1, keepdims=True)
    live = jnp.sum(jnp.where(domain == mine, 1.0, 0.0), axis=0, keepdims=True)
    query = dot(nodes[:S], wcq_ref[...]).astype(BF16)
    key = dot(nodes, wck_ref[...]).astype(BF16)
    value = dot(nodes, wcv_ref[...]).astype(BF16)
    half = dot_t(query, key) * (0.5 / math.sqrt(chan))
    weight = (half * jnp.tanh(half) + half).astype(BF16).astype(F32) * live
    mix[:chan] = wv_ref[...]
    mix[chan : chan + S] = (dot(weight.astype(BF16), value) / math.sqrt(S)).astype(BF16)
    mix[chan + S :] = jnp.zeros((chan - S, chan), BF16)

    def send(r):
        return pltpu.make_async_copy(rows_out.at[r], out_ref.at[r], sems.at[r])

    for r in range(cx):
        rows_out[r] = dot(o_ref[r], mix[...]).astype(BF16)
        send(r).start()
    for r in range(cx):
        send(r).wait()


def final(nx, ny, blocks, readers, w_cquery, w_ckey, w_cvalue, w_value, out):
    cx, span, wide = out.shape
    chan = wide // 2
    return pl.pallas_call(
        functools.partial(final_kernel, nx, ny, len(blocks)),
        in_specs=[IN_VMEM] * (len(blocks) + 6),
        out_specs=IN_HBM,
        out_shape=jax.ShapeDtypeStruct((cx, span, chan), BF16),
        scratch_shapes=[
            pltpu.VMEM((2 * chan, chan), BF16),
            pltpu.VMEM((cx, span, chan), BF16),
            pltpu.SemaphoreType.DMA((cx,)),
        ],
        compiler_params=params(16),
        name="final",
    )(*blocks, readers.T, w_cquery, w_ckey, w_cvalue, w_value, out)


def shift(array, axis, step):
    count = lax.axis_size(axis)
    return lax.ppermute(array, axis, [(i, (i + step) % count) for i in range(count)])


def swap(array, axis, bits):
    return lax.ppermute(array, axis, [(i, i ^ bits) for i in range(lax.axis_size(axis))])


def join_kernel(count, *refs):
    parts, out = refs[:count], refs[-1]
    at = 0
    for part in parts:
        out[at : at + part.shape[0]] = part[...]
        at += part.shape[0]


def join(parts, ties):
    rows = sum(part.shape[0] for part in parts)
    return pl.pallas_call(
        functools.partial(join_kernel, len(parts)),
        in_specs=[IN_VMEM] * len(parts) + [pl.BlockSpec(memory_space=pl.ANY)] * len(ties),
        out_specs=IN_VMEM,
        out_shape=pltpu.VMEM((rows, parts[0].shape[1]), BF16),
        compiler_params=params(4),
        name="join",
    )(*parts, *ties)


def edge_rows_kernel(tile, fv_ref, left_ref, right_ref, up_ref, down_ref):
    rows, span, _ = fv_ref.shape
    for ref, r in ((up_ref, rows - 1), (down_ref, 0)):
        ref[:tile] = left_ref[tile * r : tile * (r + 1)]
        ref[tile : tile + span] = fv_ref[r]
        ref[tile + span :] = right_ref[tile * r : tile * (r + 1)]


def edge_rows(tile, fv, left, right):
    _, span, chan = fv.shape
    edge = pltpu.VMEM((span + 2 * tile, chan), BF16)
    return pl.pallas_call(
        functools.partial(edge_rows_kernel, tile),
        in_specs=[IN_VMEM] * 3,
        out_specs=[IN_VMEM] * 2,
        out_shape=[edge, edge],
        compiler_params=params(4),
        name="edge_rows",
    )(fv, left, right)


def per_device(features, tile_mask, pool_map, readers, w_query, w_key, w_value, w_cquery, w_ckey, w_cvalue):
    cx, cy, tile, chan = features.shape
    nx, ny = lax.axis_size("gx"), lax.axis_size("gy")
    *base, pooled, left_edge, right_edge = pool(nx, ny, features, tile_mask, pool_map, w_query, w_key)
    fv = base[0]

    def inner(first, count, out, ties):
        return piece(functools.partial(inner_kernel, first, count), 0.75 * count, f"inner_{first}", base, out, (), ties)

    cuts = [1, 1 + (cx - 2) * 4 // 14, 1 + (cx - 2) * 10 // 14, cx - 1]
    blocks = [pooled] + [swap(pooled, "gx", bits) for bits in range(1, nx)]
    left = shift(right_edge, "gy", 1)
    right = shift(left_edge, "gy", -1)
    out = inner(cuts[0], cuts[1] - cuts[0], None, ())
    part = join(blocks, (out,))
    blocks = [part] + [swap(part, "gy", bits) for bits in range(2, ny, 2)]
    up, down = edge_rows(tile, fv, left, right)
    above = shift(up, "gx", 1)
    below = shift(down, "gx", -1)
    out = inner(cuts[1], cuts[2] - cuts[1], out, (part, up))
    part = join(blocks, (out,))
    blocks = [part, swap(part, "gy", 1)]
    out = inner(cuts[2], cuts[3] - cuts[2], out, (part,))
    out = piece(sides_kernel, 3.5, "sides", base, out, (left, right))
    out = piece(ends_kernel, 2, "ends", base, out, (left, right, above, below))
    update = final(nx, ny, blocks, readers, w_cquery, w_ckey, w_cvalue, w_value, out)
    return update.reshape(features.shape)


def solution(mesh):
    in_specs = (P("gx", "gy", None, None), P("gx", "gy", None), P("gx", "gy", None)) + (P(),) * 7
    return jax.shard_map(
        per_device, mesh=mesh, in_specs=in_specs, out_specs=P("gx", "gy", None, None), check_vma=False
    )
```

```python
import functools
import math

import jax
import jax.numpy as jnp
from jax import lax
from jax.experimental import pallas as pl
from jax.experimental.pallas import tpu as pltpu
from jax.sharding import PartitionSpec as P

BF16 = jnp.bfloat16
F32 = jnp.float32
S = 64
DEPTH = 2
CUTS = (2, 6, 11)
IN_VMEM = pl.BlockSpec(memory_space=pltpu.VMEM)
IN_HBM = pl.BlockSpec(memory_space=pltpu.HBM)


def dot(a, b):
    return jnp.dot(a, b, preferred_element_type=F32)


def dot_t(a, b):
    return lax.dot_general(a, b, (((1,), (1,)), ((), ())), preferred_element_type=F32)


def t_dot(a, b):
    return lax.dot_general(a, b, (((0,), (0,)), ((), ())), preferred_element_type=F32)


def in_hbm(array):
    return pltpu.with_memory_space_constraint(array, pltpu.HBM)


def params(mib):
    return pltpu.CompilerParams(vmem_limit_bytes=mib * 1024 * 1024)


def paired(ids):
    half = ids.shape[0] // 2
    return jnp.concatenate([ids[:half], ids[half:]], axis=1)


def pool_kernel(tile, nx, ny, f_ref, pm_ref, tm_ref, wq_ref, wk_ref, fv_ref, pv_ref, mv_ref, m_ref, pooled_ref, tv, wq, wk, sems):
    rows, span, chan = fv_ref.shape
    cy = span // tile
    small = [(tm_ref, tv), (wq_ref, wq), (wk_ref, wk), (pm_ref, pv_ref)]
    first = [pltpu.make_async_copy(src, dst, sems.at[rows + i]) for i, (src, dst) in enumerate(small)]
    beads_in = [pltpu.make_async_copy(f_ref.at[r], fv_ref.at[r], sems.at[r]) for r in range(rows)]
    for copy in first + beads_in:
        copy.start()
    block = lax.broadcasted_iota(jnp.int32, (18, 12 * tile), 1) // tile
    which = lax.broadcasted_iota(jnp.int32, (18, 12 * tile), 0)
    offset, second = which % 9, which // 9
    hit = (offset // 3 == block // 4) & (offset % 3 == block % 4 - second)
    pick = jnp.where(hit, 1 / math.sqrt(tile), 0.0).astype(BF16)
    for copy in first:
        copy.wait()
    m_ref[...] = (dot_t(wq[...], wk[...]) * (0.5 / math.sqrt(chan))).astype(BF16)
    mask = jnp.concatenate([tv[pl.ds(r, 9, stride=rows), :].astype(F32) for r in range(rows)], axis=1)
    lane = lax.broadcasted_iota(jnp.int32, mask.shape, 1)
    toward = lax.broadcasted_iota(jnp.int32, mask.shape, 0)
    mx, my = lax.axis_index("gx"), lax.axis_index("gy")
    outside = (toward // 3 == 0) & (lane // cy == jnp.where(mx == 0, 0, -1))
    outside |= (toward // 3 == 2) & (lane // cy == jnp.where(mx == nx - 1, rows - 1, -1))
    outside |= (toward % 3 == 0) & (lane % cy == jnp.where(my == 0, 0, -1))
    outside |= (toward % 3 == 2) & (lane % cy == jnp.where(my == ny - 1, cy - 1, -1))
    mask = jnp.where(outside, 0.0, mask)
    even = lane % 2 == 0
    both = jnp.concatenate([jnp.where(even, mask, 0.0), jnp.where(even, 0.0, mask)], axis=0)
    mv_ref[...] = t_dot(both.astype(BF16), pick)

    node = lax.broadcasted_iota(jnp.int32, (S, 2 * tile), 0)
    order = [c for i in range(cy // 2) for c in (i, i + cy // 2)]
    total = jnp.zeros((S, chan), F32)
    for r in range(rows):
        pairs = paired(pv_ref[r])
        onehot = jnp.concatenate(
            [(jnp.broadcast_to(pairs[i : i + 1], node.shape) == node).astype(F32).astype(BF16) for i in range(cy // 2)],
            axis=1,
        )
        beads_in[r].wait()
        total += dot(onehot, jnp.concatenate([fv_ref[r, tile * c : tile * (c + 1)] for c in order], axis=0))
    pooled_ref[...] = (total * math.sqrt(S / (rows * span))).astype(BF16)


def pool(nx, ny, features, tile_mask, pool_map, w_query, w_key):
    cx, cy, tile, chan = features.shape
    span = cy * tile
    return pl.pallas_call(
        functools.partial(pool_kernel, tile, nx, ny),
        in_specs=[IN_HBM] * 5,
        out_specs=[IN_VMEM] * 5,
        out_shape=[
            pltpu.VMEM((cx, span, chan), BF16),
            pltpu.VMEM((cx, cy, tile), jnp.int32),
            pltpu.VMEM((cx * cy, 12 * tile), F32),
            pltpu.VMEM((chan, chan), BF16),
            pltpu.VMEM((S, chan), BF16),
        ],
        scratch_shapes=[
            pltpu.VMEM((9 * cx, cy), jnp.int32),
            pltpu.VMEM((chan, chan), BF16),
            pltpu.VMEM((chan, chan), BF16),
            pltpu.SemaphoreType.DMA((cx + 4,)),
        ],
        compiler_params=params(16),
        name="pool",
    )(
        in_hbm(features.reshape(cx, span, chan)),
        in_hbm(pool_map),
        in_hbm(jnp.transpose(tile_mask, (2, 0, 1)).reshape(9 * cx, cy)),
        in_hbm(w_query),
        in_hbm(w_key),
    )


def attend(tile, tasks):
    waiting = []

    def finish(task, weights):
        _, windows, _, store = task
        near = jnp.concatenate([window() for window in windows], axis=0)
        store(dot(jnp.concatenate(weights, axis=1), near).astype(BF16))

    for task in tasks:
        query, windows, masks, _ = task
        weights = []
        for r, window in enumerate(windows):
            half = dot_t(query, window())
            lanes = slice(4 * tile * r, 4 * tile * (r + 1))
            mask = jnp.concatenate([jnp.broadcast_to(masks(h, lanes), (tile, 4 * tile)) for h in (0, 1)], axis=0)
            weights.append((half * jnp.tanh(half) + half).astype(BF16) * mask.astype(BF16))
        waiting.append((task, weights))
        if len(waiting) > DEPTH:
            finish(*waiting.pop(0))
    while waiting:
        finish(*waiting.pop(0))


def row_tasks(refs, row, first, last, window):
    fv, pv, mv, m, o = refs
    chan = fv.shape[2]
    cy, tile = pv.shape[1:]
    side = 2 * tile
    queries = dot(fv[row, side * first : side * last], m[...]).astype(BF16)
    tasks = []
    for j in range(first, last):

        def store(value, lo=side * j):
            o[row, lo : lo + side, :chan] = value

        tasks.append((
            queries[side * (j - first) : side * (j - first + 1)],
            [functools.partial(window, r, j) for r in (row - 1, row, row + 1)],
            lambda h, lanes, lo=row * cy + 2 * j: mv[lo + h : lo + h + 1, lanes],
            store,
        ))
    return tasks


def node_rows(refs, row):
    fv, pv, _, _, o = refs
    _, span, chan = fv.shape
    cy, tile = pv.shape[1:]
    pairs = paired(pv[row])
    node = lax.broadcasted_iota(jnp.int32, (chan, 2 * tile), 0)
    for i in range(cy // 2):
        turned = (jnp.broadcast_to(pairs[i : i + 1], node.shape) == node).astype(F32).T.astype(BF16)
        o[row, tile * i : tile * (i + 1), chan:] = turned[:tile]
        o[row, span // 2 + tile * i : span // 2 + tile * (i + 1), chan:] = turned[tile:]


def inner_tasks(refs, rows):
    fv, pv = refs[:2]
    cy, tile = pv.shape[1:]

    def window(r, j):
        return fv[r, tile * (2 * j - 1) : tile * (2 * j + 3)]

    tasks = []
    for row in rows:
        node_rows(refs, row)
        tasks += row_tasks(refs, row, 1, cy // 2 - 1, window)
    return tasks


def opening_kernel(rows, fv, pv, mv, m, pooled_in, o, pooled, left, right):
    span = fv.shape[1]
    tile = pv.shape[2]
    pooled[...] = pooled_in[...]
    for r in range(fv.shape[0]):
        left[tile * r : tile * (r + 1)] = fv[r, :tile]
        right[tile * r : tile * (r + 1)] = fv[r, span - tile :]
    attend(tile, inner_tasks((fv, pv, mv, m, o), rows))


def inner_kernel(rows, fv, pv, mv, m, *rest):
    attend(pv.shape[2], inner_tasks((fv, pv, mv, m, rest[-1]), rows))


def side_window(fv, tile, left, right):
    span = fv.shape[1]

    def window(r, j):
        if j == 0:
            return jnp.concatenate([left[tile * r : tile * (r + 1)], fv[r, : 3 * tile]], axis=0)
        if 2 * tile * (j + 1) == span:
            return jnp.concatenate([fv[r, span - 3 * tile :], right[tile * r : tile * (r + 1)]], axis=0)
        return fv[r, tile * (2 * j - 1) : tile * (2 * j + 3)]

    return window


def sides_kernel(rows, fv, pv, mv, m, out_in, left, right, *rest):
    cy, tile = pv.shape[1:]
    refs = (fv, pv, mv, m, rest[-1])
    window = side_window(fv, tile, left, right)
    tasks = inner_tasks(refs, rows)
    for row in range(1, fv.shape[0] - 1):
        for j in (0, cy // 2 - 1):
            tasks += row_tasks(refs, row, j, j + 1, window)
    attend(tile, tasks)


def ends_kernel(fv, pv, mv, m, out_in, left, right, above, below, o):
    cy, tile = pv.shape[1:]
    rows = fv.shape[0]
    refs = (fv, pv, mv, m, o)
    near = side_window(fv, tile, left, right)

    def window(r, j):
        if r in (-1, rows):
            return (above if r < 0 else below)[2 * tile * j : 2 * tile * (j + 2)]
        return near(r, j)

    tasks = []
    for row in (0, rows - 1):
        node_rows(refs, row)
        tasks += row_tasks(refs, row, 0, cy // 2, window)
    attend(tile, tasks)


def estimate(rows):
    return pl.CostEstimate(flops=int(rows * 400_000_000), bytes_accessed=1_000_000, transcendentals=0)


def opening(rows, base, pooled):
    cx, span, chan = base[0].shape
    cy = base[1].shape[1]
    edge = pltpu.VMEM((cx * span // cy, chan), BF16)
    return pl.pallas_call(
        functools.partial(opening_kernel, rows),
        in_specs=[IN_VMEM] * 5,
        out_specs=[IN_VMEM] * 4,
        out_shape=[pltpu.VMEM((cx, span, 2 * chan), BF16), pltpu.VMEM(pooled.shape, BF16), edge, edge],
        compiler_params=params(16),
        cost_estimate=estimate(len(rows)),
        name="opening",
    )(*base, pooled)


def piece(kernel, rows_done, name, base, out, near=(), ties=()):
    return pl.pallas_call(
        kernel,
        in_specs=[IN_VMEM] * (5 + len(near)) + [pl.BlockSpec(memory_space=pl.ANY)] * len(ties),
        out_specs=IN_VMEM,
        out_shape=pltpu.VMEM(out.shape, BF16),
        input_output_aliases={4: 0},
        compiler_params=params(16),
        cost_estimate=estimate(rows_done),
        name=name,
    )(*base, out, *near, *ties)


def final_kernel(nx, ny, n_blocks, *refs):
    blocks = refs[:n_blocks]
    readers_ref, wcq_ref, wck_ref, wcv_ref, wv_ref, o_ref, out_ref, mix, rows_out, sems = refs[n_blocks:]
    cx, span, chan = rows_out.shape
    nodes = jnp.concatenate([ref[...] for ref in blocks], axis=0)
    count = nodes.shape[0]
    mx, my = lax.axis_index("gx"), lax.axis_index("gy")
    block = lax.broadcasted_iota(jnp.int32, (readers_ref.shape[0], count), 1) // S
    rest = block // nx
    turn = (rest % (ny // 2)) * 2 + rest // (ny // 2)
    domain = ((block % nx) ^ mx) * ny + (turn ^ my)
    lane = lax.broadcasted_iota(jnp.int32, readers_ref.shape, 1)
    mine = jnp.sum(jnp.where(lane == mx * ny + my, readers_ref[...], 0), axis=1, keepdims=True)
    live = jnp.sum(jnp.where(domain == mine, 1.0, 0.0), axis=0, keepdims=True)
    query = dot(nodes[:S], wcq_ref[...]).astype(BF16)
    key = dot(nodes, wck_ref[...]).astype(BF16)
    value = dot(nodes, wcv_ref[...]).astype(BF16)
    half = dot_t(query, key) * (0.5 / math.sqrt(chan))
    weight = (half * jnp.tanh(half) + half).astype(BF16).astype(F32) * live
    mix[:chan] = wv_ref[...]
    mix[chan : chan + S] = (dot(weight.astype(BF16), value) / math.sqrt(S)).astype(BF16)
    mix[chan + S :] = jnp.zeros((chan - S, chan), BF16)

    def send(r):
        return pltpu.make_async_copy(rows_out.at[r], out_ref.at[r], sems.at[r])

    for r in range(cx):
        rows_out[r] = dot(o_ref[r], mix[...]).astype(BF16)
        send(r).start()
    for r in range(cx):
        send(r).wait()


def final(nx, ny, blocks, readers, w_cquery, w_ckey, w_cvalue, w_value, out):
    cx, span, wide = out.shape
    chan = wide // 2
    return pl.pallas_call(
        functools.partial(final_kernel, nx, ny, len(blocks)),
        in_specs=[IN_VMEM] * (len(blocks) + 6),
        out_specs=IN_HBM,
        out_shape=jax.ShapeDtypeStruct((cx, span, chan), BF16),
        scratch_shapes=[
            pltpu.VMEM((2 * chan, chan), BF16),
            pltpu.VMEM((cx, span, chan), BF16),
            pltpu.SemaphoreType.DMA((cx,)),
        ],
        compiler_params=params(16),
        name="final",
    )(*blocks, readers.T, w_cquery, w_ckey, w_cvalue, w_value, out)


def shift(array, axis, step):
    count = lax.axis_size(axis)
    return lax.ppermute(array, axis, [(i, (i + step) % count) for i in range(count)])


def swap(array, axis, bits):
    return lax.ppermute(array, axis, [(i, i ^ bits) for i in range(lax.axis_size(axis))])


def join_kernel(count, *refs):
    parts, out = refs[:count], refs[-1]
    at = 0
    for part in parts:
        out[at : at + part.shape[0]] = part[...]
        at += part.shape[0]


def join(parts, ties):
    rows = sum(part.shape[0] for part in parts)
    return pl.pallas_call(
        functools.partial(join_kernel, len(parts)),
        in_specs=[IN_VMEM] * len(parts) + [pl.BlockSpec(memory_space=pl.ANY)] * len(ties),
        out_specs=IN_VMEM,
        out_shape=pltpu.VMEM((rows, parts[0].shape[1]), BF16),
        compiler_params=params(4),
        name="join",
    )(*parts, *ties)


def edge_rows_kernel(tile, fv_ref, left_ref, right_ref, *rest):
    up_ref, down_ref = rest[-2:]
    rows, span, _ = fv_ref.shape
    for ref, r in ((up_ref, rows - 1), (down_ref, 0)):
        ref[:tile] = left_ref[tile * r : tile * (r + 1)]
        ref[tile : tile + span] = fv_ref[r]
        ref[tile + span :] = right_ref[tile * r : tile * (r + 1)]


def edge_rows(tile, fv, left, right, ties):
    _, span, chan = fv.shape
    edge = pltpu.VMEM((span + 2 * tile, chan), BF16)
    return pl.pallas_call(
        functools.partial(edge_rows_kernel, tile),
        in_specs=[IN_VMEM] * 3 + [pl.BlockSpec(memory_space=pl.ANY)] * len(ties),
        out_specs=[IN_VMEM] * 2,
        out_shape=[edge, edge],
        compiler_params=params(4),
        name="edge_rows",
    )(fv, left, right, *ties)


def per_device(features, tile_mask, pool_map, readers, w_query, w_key, w_value, w_cquery, w_ckey, w_cvalue):
    cx, cy, tile, chan = features.shape
    nx, ny = lax.axis_size("gx"), lax.axis_size("gy")
    *base, pooled = pool(nx, ny, features, tile_mask, pool_map, w_query, w_key)
    fv = base[0]
    cuts = [1] + [1 + (cx - 2) * part // 14 for part in CUTS] + [cx - 1]
    rows = [range(lo, hi) for lo, hi in zip(cuts, cuts[1:])]
    out, pooled, left_edge, right_edge = opening(rows[0], base, pooled)
    left = shift(right_edge, "gy", 1)
    right = shift(left_edge, "gy", -1)
    blocks = [pooled] + [swap(pooled, "gx", bits) for bits in range(1, nx)]
    out = piece(functools.partial(inner_kernel, rows[1]), len(rows[1]), "inner", base, out, (), (pooled,))
    up, down = edge_rows(tile, fv, left, right, (out,))
    above = shift(up, "gx", 1)
    below = shift(down, "gx", -1)
    part = join(blocks, (out, up))
    blocks = [part] + [swap(part, "gy", bits) for bits in range(2, ny, 2)]
    out = piece(functools.partial(inner_kernel, rows[2]), len(rows[2]), "middle", base, out, (), (part, up))
    part = join(blocks, (out,))
    blocks = [part, swap(part, "gy", 1)]
    out = piece(functools.partial(sides_kernel, rows[3]), len(rows[3]) + 3.5, "sides", base, out, (left, right), (part,))
    out = piece(ends_kernel, 2, "ends", base, out, (left, right, above, below))
    update = final(nx, ny, blocks, readers, w_cquery, w_ckey, w_cvalue, w_value, out)
    return update.reshape(features.shape)


def solution(mesh):
    in_specs = (P("gx", "gy", None, None), P("gx", "gy", None), P("gx", "gy", None)) + (P(),) * 7
    return jax.shard_map(
        per_device, mesh=mesh, in_specs=in_specs, out_specs=P("gx", "gy", None, None), check_vma=False
    )
```

```python
import functools
import math

import jax
import jax.numpy as jnp
from jax import lax
from jax.experimental import pallas as pl
from jax.experimental.pallas import tpu as pltpu
from jax.sharding import PartitionSpec as P

BF16 = jnp.bfloat16
F32 = jnp.float32
S = 64
DEPTH = 2
CUTS = (4, 7, 10, 14)
IN_VMEM = pl.BlockSpec(memory_space=pltpu.VMEM)
IN_HBM = pl.BlockSpec(memory_space=pltpu.HBM)


def dot(a, b):
    return jnp.dot(a, b, preferred_element_type=F32)


def dot_t(a, b):
    return lax.dot_general(a, b, (((1,), (1,)), ((), ())), preferred_element_type=F32)


def t_dot(a, b):
    return lax.dot_general(a, b, (((0,), (0,)), ((), ())), preferred_element_type=F32)


def in_hbm(array):
    return pltpu.with_memory_space_constraint(array, pltpu.HBM)


def params(mib):
    return pltpu.CompilerParams(vmem_limit_bytes=mib * 1024 * 1024)


def paired(ids):
    half = ids.shape[0] // 2
    return jnp.concatenate([ids[:half], ids[half:]], axis=1)


def pool_kernel(tile, nx, ny, f_ref, pm_ref, tm_ref, wq_ref, wk_ref, fv_ref, pv_ref, mv_ref, m_ref, pooled_ref, left_ref, right_ref, tv, wq, wk, sems):
    rows, span, chan = fv_ref.shape
    cy = span // tile
    small = [(tm_ref, tv), (wq_ref, wq), (wk_ref, wk), (pm_ref, pv_ref)]
    first = [pltpu.make_async_copy(src, dst, sems.at[rows + i]) for i, (src, dst) in enumerate(small)]
    beads_in = [pltpu.make_async_copy(f_ref.at[r], fv_ref.at[r], sems.at[r]) for r in range(rows)]
    for copy in first + beads_in:
        copy.start()
    block = lax.broadcasted_iota(jnp.int32, (18, 12 * tile), 1) // tile
    which = lax.broadcasted_iota(jnp.int32, (18, 12 * tile), 0)
    offset, second = which % 9, which // 9
    hit = (offset // 3 == block // 4) & (offset % 3 == block % 4 - second)
    pick = jnp.where(hit, 1 / math.sqrt(tile), 0.0).astype(BF16)
    for copy in first:
        copy.wait()
    m_ref[...] = (dot_t(wq[...], wk[...]) * (0.5 / math.sqrt(chan))).astype(BF16)
    mask = jnp.concatenate([tv[pl.ds(r, 9, stride=rows), :].astype(F32) for r in range(rows)], axis=1)
    lane = lax.broadcasted_iota(jnp.int32, mask.shape, 1)
    toward = lax.broadcasted_iota(jnp.int32, mask.shape, 0)
    mx, my = lax.axis_index("gx"), lax.axis_index("gy")
    outside = (toward // 3 == 0) & (lane // cy == jnp.where(mx == 0, 0, -1))
    outside |= (toward // 3 == 2) & (lane // cy == jnp.where(mx == nx - 1, rows - 1, -1))
    outside |= (toward % 3 == 0) & (lane % cy == jnp.where(my == 0, 0, -1))
    outside |= (toward % 3 == 2) & (lane % cy == jnp.where(my == ny - 1, cy - 1, -1))
    mask = jnp.where(outside, 0.0, mask)
    even = lane % 2 == 0
    both = jnp.concatenate([jnp.where(even, mask, 0.0), jnp.where(even, 0.0, mask)], axis=0)
    mv_ref[...] = t_dot(both.astype(BF16), pick)

    node = lax.broadcasted_iota(jnp.int32, (S, 2 * tile), 0)
    order = [c for i in range(cy // 2) for c in (i, i + cy // 2)]
    total = jnp.zeros((S, chan), F32)
    for r in range(rows):
        pairs = paired(pv_ref[r])
        onehot = jnp.concatenate(
            [(jnp.broadcast_to(pairs[i : i + 1], node.shape) == node).astype(F32).astype(BF16) for i in range(cy // 2)],
            axis=1,
        )
        beads_in[r].wait()
        total += dot(onehot, jnp.concatenate([fv_ref[r, tile * c : tile * (c + 1)] for c in order], axis=0))
        left_ref[tile * r : tile * (r + 1)] = fv_ref[r, :tile]
        right_ref[tile * r : tile * (r + 1)] = fv_ref[r, span - tile :]
    pooled_ref[...] = (total * math.sqrt(S / (rows * span))).astype(BF16)


def pool(nx, ny, features, tile_mask, pool_map, w_query, w_key):
    cx, cy, tile, chan = features.shape
    span = cy * tile
    edge = pltpu.VMEM((cx * tile, chan), BF16)
    return pl.pallas_call(
        functools.partial(pool_kernel, tile, nx, ny),
        in_specs=[IN_HBM] * 5,
        out_specs=[IN_VMEM] * 7,
        out_shape=[
            pltpu.VMEM((cx, span, chan), BF16),
            pltpu.VMEM((cx, cy, tile), jnp.int32),
            pltpu.VMEM((cx * cy, 12 * tile), F32),
            pltpu.VMEM((chan, chan), BF16),
            pltpu.VMEM((S, chan), BF16),
            edge,
            edge,
        ],
        scratch_shapes=[
            pltpu.VMEM((9 * cx, cy), jnp.int32),
            pltpu.VMEM((chan, chan), BF16),
            pltpu.VMEM((chan, chan), BF16),
            pltpu.SemaphoreType.DMA((cx + 4,)),
        ],
        compiler_params=params(16),
        name="pool",
    )(
        in_hbm(features.reshape(cx, span, chan)),
        in_hbm(pool_map),
        in_hbm(jnp.transpose(tile_mask, (2, 0, 1)).reshape(9 * cx, cy)),
        in_hbm(w_query),
        in_hbm(w_key),
    )


def attend(tile, tasks):
    waiting = []

    def finish(task, weights):
        _, windows, _, store = task
        near = jnp.concatenate([window() for window in windows], axis=0)
        store(dot(jnp.concatenate(weights, axis=1), near).astype(BF16))

    for task in tasks:
        query, windows, masks, _ = task
        weights = []
        for r, window in enumerate(windows):
            half = dot_t(query, window())
            lanes = slice(4 * tile * r, 4 * tile * (r + 1))
            mask = jnp.concatenate([jnp.broadcast_to(masks(h, lanes), (tile, 4 * tile)) for h in (0, 1)], axis=0)
            weights.append((half * jnp.tanh(half) + half).astype(BF16) * mask.astype(BF16))
        waiting.append((task, weights))
        if len(waiting) > DEPTH:
            finish(*waiting.pop(0))
    while waiting:
        finish(*waiting.pop(0))


def row_tasks(refs, row, first, last, window):
    fv, pv, mv, m, o = refs
    chan = fv.shape[2]
    cy, tile = pv.shape[1:]
    side = 2 * tile
    queries = dot(fv[row, side * first : side * last], m[...]).astype(BF16)
    tasks = []
    for j in range(first, last):

        def store(value, lo=side * j):
            o[row, lo : lo + side, :chan] = value

        tasks.append((
            queries[side * (j - first) : side * (j - first + 1)],
            [functools.partial(window, r, j) for r in (row - 1, row, row + 1)],
            lambda h, lanes, lo=row * cy + 2 * j: mv[lo + h : lo + h + 1, lanes],
            store,
        ))
    return tasks


def node_rows(refs, row):
    fv, pv, _, _, o = refs
    _, span, chan = fv.shape
    cy, tile = pv.shape[1:]
    pairs = paired(pv[row])
    node = lax.broadcasted_iota(jnp.int32, (chan, 2 * tile), 0)
    for i in range(cy // 2):
        turned = (jnp.broadcast_to(pairs[i : i + 1], node.shape) == node).astype(F32).T.astype(BF16)
        o[row, tile * i : tile * (i + 1), chan:] = turned[:tile]
        o[row, span // 2 + tile * i : span // 2 + tile * (i + 1), chan:] = turned[tile:]


def inner_tasks(refs, rows):
    fv, pv = refs[:2]
    cy, tile = pv.shape[1:]

    def window(r, j):
        return fv[r, tile * (2 * j - 1) : tile * (2 * j + 3)]

    tasks = []
    for row in rows:
        node_rows(refs, row)
        tasks += row_tasks(refs, row, 1, cy // 2 - 1, window)
    return tasks


def inner_kernel(rows, fv, pv, mv, m, *rest):
    attend(pv.shape[2], inner_tasks((fv, pv, mv, m, rest[-1]), rows))


def side_window(fv, tile, left, right):
    span = fv.shape[1]

    def window(r, j):
        if j == 0:
            return jnp.concatenate([left[tile * r : tile * (r + 1)], fv[r, : 3 * tile]], axis=0)
        if 2 * tile * (j + 1) == span:
            return jnp.concatenate([fv[r, span - 3 * tile :], right[tile * r : tile * (r + 1)]], axis=0)
        return fv[r, tile * (2 * j - 1) : tile * (2 * j + 3)]

    return window


def sides_kernel(rows, fv, pv, mv, m, out_in, left, right, *rest):
    cy, tile = pv.shape[1:]
    refs = (fv, pv, mv, m, rest[-1])
    window = side_window(fv, tile, left, right)
    tasks = inner_tasks(refs, rows)
    for row in range(1, fv.shape[0] - 1):
        for j in (0, cy // 2 - 1):
            tasks += row_tasks(refs, row, j, j + 1, window)
    attend(tile, tasks)


def ends_kernel(fv, pv, mv, m, out_in, left, right, above, below, *rest):
    cy, tile = pv.shape[1:]
    rows = fv.shape[0]
    refs = (fv, pv, mv, m, rest[-1])
    near = side_window(fv, tile, left, right)

    def window(r, j):
        if r in (-1, rows):
            return (above if r < 0 else below)[2 * tile * j : 2 * tile * (j + 2)]
        return near(r, j)

    tasks = []
    for row in (0, rows - 1):
        node_rows(refs, row)
        tasks += row_tasks(refs, row, 0, cy // 2, window)
    attend(tile, tasks)


def estimate(rows):
    return pl.CostEstimate(flops=int(rows * 400_000_000), bytes_accessed=1_000_000, transcendentals=0)


def piece(kernel, rows_done, name, base, out, near=(), ties=()):
    cx, span, chan = base[0].shape
    done = [] if out is None else [out]
    return pl.pallas_call(
        kernel,
        in_specs=[IN_VMEM] * (4 + len(done) + len(near)) + [pl.BlockSpec(memory_space=pl.ANY)] * len(ties),
        out_specs=IN_VMEM,
        out_shape=pltpu.VMEM((cx, span, 2 * chan), BF16),
        input_output_aliases={4: 0} if done else {},
        compiler_params=params(16),
        cost_estimate=estimate(rows_done),
        name=name,
    )(*base, *done, *near, *ties)


def final_kernel(nx, ny, n_blocks, *refs):
    blocks = refs[:n_blocks]
    readers_ref, wcq_ref, wck_ref, wcv_ref, wv_ref, o_ref, out_ref, mix, rows_out, sems = refs[n_blocks:]
    cx, span, chan = rows_out.shape
    nodes = jnp.concatenate([ref[...] for ref in blocks], axis=0)
    count = nodes.shape[0]
    mx, my = lax.axis_index("gx"), lax.axis_index("gy")
    block = lax.broadcasted_iota(jnp.int32, (readers_ref.shape[0], count), 1) // S
    rest = block // nx
    turn = (rest % (ny // 2)) * 2 + rest // (ny // 2)
    domain = ((block % nx) ^ mx) * ny + (turn ^ my)
    lane = lax.broadcasted_iota(jnp.int32, readers_ref.shape, 1)
    mine = jnp.sum(jnp.where(lane == mx * ny + my, readers_ref[...], 0), axis=1, keepdims=True)
    live = jnp.sum(jnp.where(domain == mine, 1.0, 0.0), axis=0, keepdims=True)
    query = dot(nodes[:S], wcq_ref[...]).astype(BF16)
    key = dot(nodes, wck_ref[...]).astype(BF16)
    value = dot(nodes, wcv_ref[...]).astype(BF16)
    half = dot_t(query, key) * (0.5 / math.sqrt(chan))
    weight = (half * jnp.tanh(half) + half).astype(BF16).astype(F32) * live
    mix[:chan] = wv_ref[...]
    mix[chan : chan + S] = (dot(weight.astype(BF16), value) / math.sqrt(S)).astype(BF16)
    mix[chan + S :] = jnp.zeros((chan - S, chan), BF16)

    def send(r):
        return pltpu.make_async_copy(rows_out.at[r], out_ref.at[r], sems.at[r])

    for r in range(cx):
        rows_out[r] = dot(o_ref[r], mix[...]).astype(BF16)
        send(r).start()
    for r in range(cx):
        send(r).wait()


def final(nx, ny, blocks, readers, w_cquery, w_ckey, w_cvalue, w_value, out):
    cx, span, wide = out.shape
    chan = wide // 2
    return pl.pallas_call(
        functools.partial(final_kernel, nx, ny, len(blocks)),
        in_specs=[IN_VMEM] * (len(blocks) + 6),
        out_specs=IN_HBM,
        out_shape=jax.ShapeDtypeStruct((cx, span, chan), BF16),
        scratch_shapes=[
            pltpu.VMEM((2 * chan, chan), BF16),
            pltpu.VMEM((cx, span, chan), BF16),
            pltpu.SemaphoreType.DMA((cx,)),
        ],
        compiler_params=params(16),
        name="final",
    )(*blocks, readers.T, w_cquery, w_ckey, w_cvalue, w_value, out)


def shift(array, axis, step):
    count = lax.axis_size(axis)
    return lax.ppermute(array, axis, [(i, (i + step) % count) for i in range(count)])


def swap(array, axis, bits):
    return lax.ppermute(array, axis, [(i, i ^ bits) for i in range(lax.axis_size(axis))])


def join_kernel(count, *refs):
    parts, out = refs[:count], refs[-1]
    at = 0
    for part in parts:
        out[at : at + part.shape[0]] = part[...]
        at += part.shape[0]


def join(parts, ties):
    rows = sum(part.shape[0] for part in parts)
    return pl.pallas_call(
        functools.partial(join_kernel, len(parts)),
        in_specs=[IN_VMEM] * len(parts) + [pl.BlockSpec(memory_space=pl.ANY)] * len(ties),
        out_specs=IN_VMEM,
        out_shape=pltpu.VMEM((rows, parts[0].shape[1]), BF16),
        compiler_params=params(4),
        name="join",
    )(*parts, *ties)


def edge_rows_kernel(tile, fv_ref, left_ref, right_ref, *rest):
    up_ref, down_ref = rest[-2:]
    rows, span, _ = fv_ref.shape
    for ref, r in ((up_ref, rows - 1), (down_ref, 0)):
        ref[:tile] = left_ref[tile * r : tile * (r + 1)]
        ref[tile : tile + span] = fv_ref[r]
        ref[tile + span :] = right_ref[tile * r : tile * (r + 1)]


def edge_rows(tile, fv, left, right, ties):
    _, span, chan = fv.shape
    edge = pltpu.VMEM((span + 2 * tile, chan), BF16)
    return pl.pallas_call(
        functools.partial(edge_rows_kernel, tile),
        in_specs=[IN_VMEM] * 3 + [pl.BlockSpec(memory_space=pl.ANY)] * len(ties),
        out_specs=[IN_VMEM] * 2,
        out_shape=[edge, edge],
        compiler_params=params(4),
        name="edge_rows",
    )(fv, left, right, *ties)


def per_device(features, tile_mask, pool_map, readers, w_query, w_key, w_value, w_cquery, w_ckey, w_cvalue):
    cx, cy, tile, chan = features.shape
    nx, ny = lax.axis_size("gx"), lax.axis_size("gy")
    *base, pooled, left_edge, right_edge = pool(nx, ny, features, tile_mask, pool_map, w_query, w_key)
    fv = base[0]
    cuts = [1] + [1 + (cx - 2) * part // 14 for part in CUTS] + [cx - 1]
    rows = [range(lo, hi) for lo, hi in zip(cuts, cuts[1:])]
    steps = [("gx", 1 << b) for b in range(nx.bit_length() - 1)]
    steps += [("gy", 1 << b) for b in range(1, ny.bit_length() - 1)] + [("gy", 1)]
    left = shift(right_edge, "gy", 1)
    right = shift(left_edge, "gy", -1)
    out, first, ties = None, pooled, (pooled,)
    for step, (axis, bit) in enumerate(steps):
        second = swap(first, axis, bit)
        if step == 1:
            up, down = edge_rows(tile, fv, left, right, (out,))
            above = shift(up, "gx", 1)
            below = shift(down, "gx", -1)
            ties += (up,)
        if step == len(steps) - 1:
            break
        if step < len(rows) - 1:
            kernel = functools.partial(inner_kernel, rows[step])
            out = piece(kernel, len(rows[step]), f"inner_{step}", base, out, (), ties)
        first = join((first, second), (out,))
        ties = (first,)
    out = piece(ends_kernel, 2, "ends", base, out, (left, right, above, below), ties)
    out = piece(functools.partial(sides_kernel, rows[-1]), len(rows[-1]) + 3.5, "sides", base, out, (left, right))
    update = final(nx, ny, (first, second), readers, w_cquery, w_ckey, w_cvalue, w_value, out)
    return update.reshape(features.shape)


def solution(mesh):
    in_specs = (P("gx", "gy", None, None), P("gx", "gy", None), P("gx", "gy", None)) + (P(),) * 7
    return jax.shard_map(
        per_device, mesh=mesh, in_specs=in_specs, out_specs=P("gx", "gy", None, None), check_vma=False
    )
```

```python
import functools
import math

import jax
import jax.numpy as jnp
from jax import lax
from jax.experimental import pallas as pl
from jax.experimental.pallas import tpu as pltpu
from jax.sharding import PartitionSpec as P

BF16 = jnp.bfloat16
F32 = jnp.float32
S = 64
DEPTH = 2
CUTS = (4, 7, 9, 12)
IN_VMEM = pl.BlockSpec(memory_space=pltpu.VMEM)
IN_HBM = pl.BlockSpec(memory_space=pltpu.HBM)


def dot(a, b):
    return jnp.dot(a, b, preferred_element_type=F32)


def dot_t(a, b):
    return lax.dot_general(a, b, (((1,), (1,)), ((), ())), preferred_element_type=F32)


def t_dot(a, b):
    return lax.dot_general(a, b, (((0,), (0,)), ((), ())), preferred_element_type=F32)


def in_hbm(array):
    return pltpu.with_memory_space_constraint(array, pltpu.HBM)


def params(mib):
    return pltpu.CompilerParams(vmem_limit_bytes=mib * 1024 * 1024)


def paired(ids):
    half = ids.shape[0] // 2
    return jnp.concatenate([ids[:half], ids[half:]], axis=1)


def opening_kernel(tile, nx, ny, f_ref, tm_ref, wq_ref, wk_ref, mv_ref, m_ref, left_ref, right_ref, tv, wq, wk, sems):
    rows, span, chan = f_ref.shape
    cy = span // tile
    first = [pltpu.make_async_copy(src, dst, sems.at[i]) for i, (src, dst) in enumerate([(tm_ref, tv), (wq_ref, wq), (wk_ref, wk)])]
    columns = []
    for r in range(rows):
        for k, (ref, lo) in enumerate(((left_ref, 0), (right_ref, span - tile))):
            there = ref.at[pl.ds(tile * r, tile)]
            columns.append(pltpu.make_async_copy(f_ref.at[r, pl.ds(lo, tile)], there, sems.at[3 + 2 * r + k]))
    for copy in first + columns:
        copy.start()
    block = lax.broadcasted_iota(jnp.int32, (18, 12 * tile), 1) // tile
    which = lax.broadcasted_iota(jnp.int32, (18, 12 * tile), 0)
    offset, second = which % 9, which // 9
    hit = (offset // 3 == block // 4) & (offset % 3 == block % 4 - second)
    pick = jnp.where(hit, 1 / math.sqrt(tile), 0.0).astype(BF16)
    for copy in first:
        copy.wait()
    m_ref[...] = (dot_t(wq[...], wk[...]) * (0.5 / math.sqrt(chan))).astype(BF16)
    mask = jnp.concatenate([tv[pl.ds(r, 9, stride=rows), :].astype(F32) for r in range(rows)], axis=1)
    lane = lax.broadcasted_iota(jnp.int32, mask.shape, 1)
    toward = lax.broadcasted_iota(jnp.int32, mask.shape, 0)
    mx, my = lax.axis_index("gx"), lax.axis_index("gy")
    outside = (toward // 3 == 0) & (lane // cy == jnp.where(mx == 0, 0, -1))
    outside |= (toward // 3 == 2) & (lane // cy == jnp.where(mx == nx - 1, rows - 1, -1))
    outside |= (toward % 3 == 0) & (lane % cy == jnp.where(my == 0, 0, -1))
    outside |= (toward % 3 == 2) & (lane % cy == jnp.where(my == ny - 1, cy - 1, -1))
    mask = jnp.where(outside, 0.0, mask)
    even = lane % 2 == 0
    both = jnp.concatenate([jnp.where(even, mask, 0.0), jnp.where(even, 0.0, mask)], axis=0)
    mv_ref[...] = t_dot(both.astype(BF16), pick)
    for copy in columns:
        copy.wait()


def opening(nx, ny, features, tile_mask, w_query, w_key):
    cx, cy, tile, chan = features.shape
    edge = pltpu.VMEM((cx * tile, chan), BF16)
    return pl.pallas_call(
        functools.partial(opening_kernel, tile, nx, ny),
        in_specs=[IN_HBM] * 4,
        out_specs=[IN_VMEM] * 4,
        out_shape=[pltpu.VMEM((cx * cy, 12 * tile), F32), pltpu.VMEM((chan, chan), BF16), edge, edge],
        scratch_shapes=[
            pltpu.VMEM((9 * cx, cy), jnp.int32),
            pltpu.VMEM((chan, chan), BF16),
            pltpu.VMEM((chan, chan), BF16),
            pltpu.SemaphoreType.DMA((3 + 2 * cx,)),
        ],
        compiler_params=params(8),
        name="opening",
    )(
        in_hbm(features.reshape(cx, cy * tile, chan)),
        in_hbm(jnp.transpose(tile_mask, (2, 0, 1)).reshape(9 * cx, cy)),
        in_hbm(w_query),
        in_hbm(w_key),
    )


def pool_kernel(tile, f_ref, pm_ref, tie, fv_ref, pv_ref, pooled_ref, sems):
    rows, span, chan = fv_ref.shape
    cy = span // tile
    ids_in = pltpu.make_async_copy(pm_ref, pv_ref, sems.at[rows])
    beads_in = [pltpu.make_async_copy(f_ref.at[r], fv_ref.at[r], sems.at[r]) for r in range(rows)]
    for copy in [ids_in] + beads_in:
        copy.start()
    node = lax.broadcasted_iota(jnp.int32, (S, 2 * tile), 0)
    order = [c for i in range(cy // 2) for c in (i, i + cy // 2)]
    total = jnp.zeros((S, chan), F32)
    ids_in.wait()
    for r in range(rows):
        pairs = paired(pv_ref[r])
        onehot = jnp.concatenate(
            [(jnp.broadcast_to(pairs[i : i + 1], node.shape) == node).astype(F32).astype(BF16) for i in range(cy // 2)],
            axis=1,
        )
        beads_in[r].wait()
        total += dot(onehot, jnp.concatenate([fv_ref[r, tile * c : tile * (c + 1)] for c in order], axis=0))
    pooled_ref[...] = (total * math.sqrt(S / (rows * span))).astype(BF16)


def pool(features, pool_map, tie):
    cx, cy, tile, chan = features.shape
    span = cy * tile
    return pl.pallas_call(
        functools.partial(pool_kernel, tile),
        in_specs=[IN_HBM] * 2 + [pl.BlockSpec(memory_space=pl.ANY)],
        out_specs=[IN_VMEM] * 3,
        out_shape=[
            pltpu.VMEM((cx, span, chan), BF16),
            pltpu.VMEM((cx, cy, tile), jnp.int32),
            pltpu.VMEM((S, chan), BF16),
        ],
        scratch_shapes=[pltpu.SemaphoreType.DMA((cx + 1,))],
        compiler_params=params(8),
        cost_estimate=estimate(4),
        name="pool",
    )(in_hbm(features.reshape(cx, span, chan)), in_hbm(pool_map), tie)


def attend(tile, tasks):
    waiting = []

    def finish(task, weights):
        _, windows, _, store = task
        near = jnp.concatenate([window() for window in windows], axis=0)
        store(dot(jnp.concatenate(weights, axis=1), near).astype(BF16))

    for task in tasks:
        query, windows, masks, _ = task
        weights = []
        for r, window in enumerate(windows):
            half = dot_t(query, window())
            lanes = slice(4 * tile * r, 4 * tile * (r + 1))
            mask = jnp.concatenate([jnp.broadcast_to(masks(h, lanes), (tile, 4 * tile)) for h in (0, 1)], axis=0)
            weights.append((half * jnp.tanh(half) + half).astype(BF16) * mask.astype(BF16))
        waiting.append((task, weights))
        if len(waiting) > DEPTH:
            finish(*waiting.pop(0))
    while waiting:
        finish(*waiting.pop(0))


def row_tasks(refs, row, first, last, window):
    fv, pv, mv, m, o = refs
    chan = fv.shape[2]
    cy, tile = pv.shape[1:]
    side = 2 * tile
    queries = dot(fv[row, side * first : side * last], m[...]).astype(BF16)
    tasks = []
    for j in range(first, last):

        def store(value, lo=side * j):
            o[row, lo : lo + side, :chan] = value

        tasks.append((
            queries[side * (j - first) : side * (j - first + 1)],
            [functools.partial(window, r, j) for r in (row - 1, row, row + 1)],
            lambda h, lanes, lo=row * cy + 2 * j: mv[lo + h : lo + h + 1, lanes],
            store,
        ))
    return tasks


def node_rows(refs, row):
    fv, pv, _, _, o = refs
    _, span, chan = fv.shape
    cy, tile = pv.shape[1:]
    pairs = paired(pv[row])
    node = lax.broadcasted_iota(jnp.int32, (chan, 2 * tile), 0)
    for i in range(cy // 2):
        turned = (jnp.broadcast_to(pairs[i : i + 1], node.shape) == node).astype(F32).T.astype(BF16)
        o[row, tile * i : tile * (i + 1), chan:] = turned[:tile]
        o[row, span // 2 + tile * i : span // 2 + tile * (i + 1), chan:] = turned[tile:]


def inner_tasks(refs, rows):
    fv, pv = refs[:2]
    cy, tile = pv.shape[1:]

    def window(r, j):
        return fv[r, tile * (2 * j - 1) : tile * (2 * j + 3)]

    tasks = []
    for row in rows:
        node_rows(refs, row)
        tasks += row_tasks(refs, row, 1, cy // 2 - 1, window)
    return tasks


def inner_kernel(rows, fv, pv, mv, m, *rest):
    attend(pv.shape[2], inner_tasks((fv, pv, mv, m, rest[-1]), rows))


def side_window(fv, tile, left, right):
    span = fv.shape[1]

    def window(r, j):
        if j == 0:
            return jnp.concatenate([left[tile * r : tile * (r + 1)], fv[r, : 3 * tile]], axis=0)
        if 2 * tile * (j + 1) == span:
            return jnp.concatenate([fv[r, span - 3 * tile :], right[tile * r : tile * (r + 1)]], axis=0)
        return fv[r, tile * (2 * j - 1) : tile * (2 * j + 3)]

    return window


def sides_kernel(rows, fv, pv, mv, m, out_in, left, right, *rest):
    cy, tile = pv.shape[1:]
    refs = (fv, pv, mv, m, rest[-1])
    window = side_window(fv, tile, left, right)
    tasks = inner_tasks(refs, rows)
    for row in range(1, fv.shape[0] - 1):
        for j in (0, cy // 2 - 1):
            tasks += row_tasks(refs, row, j, j + 1, window)
    attend(tile, tasks)


def ends_kernel(fv, pv, mv, m, out_in, left, right, above, below, *rest):
    cy, tile = pv.shape[1:]
    rows = fv.shape[0]
    refs = (fv, pv, mv, m, rest[-1])
    near = side_window(fv, tile, left, right)

    def window(r, j):
        if r in (-1, rows):
            return (above if r < 0 else below)[2 * tile * j : 2 * tile * (j + 2)]
        return near(r, j)

    tasks = []
    for row in (0, rows - 1):
        node_rows(refs, row)
        tasks += row_tasks(refs, row, 0, cy // 2, window)
    attend(tile, tasks)


def estimate(rows):
    return pl.CostEstimate(flops=int(rows * 400_000_000), bytes_accessed=1_000_000, transcendentals=0)


def piece(kernel, rows_done, name, base, out, near=(), ties=()):
    cx, span, chan = base[0].shape
    done = [] if out is None else [out]
    return pl.pallas_call(
        kernel,
        in_specs=[IN_VMEM] * (4 + len(done) + len(near)) + [pl.BlockSpec(memory_space=pl.ANY)] * len(ties),
        out_specs=IN_VMEM,
        out_shape=pltpu.VMEM((cx, span, 2 * chan), BF16),
        input_output_aliases={4: 0} if done else {},
        compiler_params=params(16),
        cost_estimate=estimate(rows_done),
        name=name,
    )(*base, *done, *near, *ties)


def final_kernel(nx, ny, n_blocks, *refs):
    blocks = refs[:n_blocks]
    readers_ref, wcq_ref, wck_ref, wcv_ref, wv_ref, o_ref, out_ref, mix, rows_out, sems = refs[n_blocks:]
    cx, span, chan = rows_out.shape
    nodes = jnp.concatenate([ref[...] for ref in blocks], axis=0)
    count = nodes.shape[0]
    mx, my = lax.axis_index("gx"), lax.axis_index("gy")
    block = lax.broadcasted_iota(jnp.int32, (readers_ref.shape[0], count), 1) // S
    rest = block // nx
    turn = (rest % (ny // 2)) * 2 + rest // (ny // 2)
    domain = ((block % nx) ^ mx) * ny + (turn ^ my)
    lane = lax.broadcasted_iota(jnp.int32, readers_ref.shape, 1)
    mine = jnp.sum(jnp.where(lane == mx * ny + my, readers_ref[...], 0), axis=1, keepdims=True)
    live = jnp.sum(jnp.where(domain == mine, 1.0, 0.0), axis=0, keepdims=True)
    query = dot(nodes[:S], wcq_ref[...]).astype(BF16)
    key = dot(nodes, wck_ref[...]).astype(BF16)
    value = dot(nodes, wcv_ref[...]).astype(BF16)
    half = dot_t(query, key) * (0.5 / math.sqrt(chan))
    weight = (half * jnp.tanh(half) + half).astype(BF16).astype(F32) * live
    mix[:chan] = wv_ref[...]
    mix[chan : chan + S] = (dot(weight.astype(BF16), value) / math.sqrt(S)).astype(BF16)
    mix[chan + S :] = jnp.zeros((chan - S, chan), BF16)

    def send(r):
        return pltpu.make_async_copy(rows_out.at[r], out_ref.at[r], sems.at[r])

    for r in range(cx):
        rows_out[r] = dot(o_ref[r], mix[...]).astype(BF16)
        send(r).start()
    for r in range(cx):
        send(r).wait()


def final(nx, ny, blocks, readers, w_cquery, w_ckey, w_cvalue, w_value, out):
    cx, span, wide = out.shape
    chan = wide // 2
    return pl.pallas_call(
        functools.partial(final_kernel, nx, ny, len(blocks)),
        in_specs=[IN_VMEM] * (len(blocks) + 6),
        out_specs=IN_HBM,
        out_shape=jax.ShapeDtypeStruct((cx, span, chan), BF16),
        scratch_shapes=[
            pltpu.VMEM((2 * chan, chan), BF16),
            pltpu.VMEM((cx, span, chan), BF16),
            pltpu.SemaphoreType.DMA((cx,)),
        ],
        compiler_params=params(16),
        name="final",
    )(*blocks, readers.T, w_cquery, w_ckey, w_cvalue, w_value, out)


def shift(array, axis, step):
    count = lax.axis_size(axis)
    return lax.ppermute(array, axis, [(i, (i + step) % count) for i in range(count)])


def swap(array, axis, bits):
    return lax.ppermute(array, axis, [(i, i ^ bits) for i in range(lax.axis_size(axis))])


def join_kernel(count, *refs):
    parts, out = refs[:count], refs[-1]
    at = 0
    for part in parts:
        out[at : at + part.shape[0]] = part[...]
        at += part.shape[0]


def join(parts, ties):
    rows = sum(part.shape[0] for part in parts)
    return pl.pallas_call(
        functools.partial(join_kernel, len(parts)),
        in_specs=[IN_VMEM] * len(parts) + [pl.BlockSpec(memory_space=pl.ANY)] * len(ties),
        out_specs=IN_VMEM,
        out_shape=pltpu.VMEM((rows, parts[0].shape[1]), BF16),
        compiler_params=params(4),
        name="join",
    )(*parts, *ties)


def edge_rows_kernel(tile, fv_ref, left_ref, right_ref, *rest):
    up_ref, down_ref = rest[-2:]
    rows, span, _ = fv_ref.shape
    for ref, r in ((up_ref, rows - 1), (down_ref, 0)):
        ref[:tile] = left_ref[tile * r : tile * (r + 1)]
        ref[tile : tile + span] = fv_ref[r]
        ref[tile + span :] = right_ref[tile * r : tile * (r + 1)]


def edge_rows(tile, fv, left, right, ties):
    _, span, chan = fv.shape
    edge = pltpu.VMEM((span + 2 * tile, chan), BF16)
    return pl.pallas_call(
        functools.partial(edge_rows_kernel, tile),
        in_specs=[IN_VMEM] * 3 + [pl.BlockSpec(memory_space=pl.ANY)] * len(ties),
        out_specs=[IN_VMEM] * 2,
        out_shape=[edge, edge],
        compiler_params=params(4),
        name="edge_rows",
    )(fv, left, right, *ties)


def per_device(features, tile_mask, pool_map, readers, w_query, w_key, w_value, w_cquery, w_ckey, w_cvalue):
    cx, cy, tile, chan = features.shape
    nx, ny = lax.axis_size("gx"), lax.axis_size("gy")
    mv, m, left_edge, right_edge = opening(nx, ny, features, tile_mask, w_query, w_key)
    left = shift(right_edge, "gy", 1)
    right = shift(left_edge, "gy", -1)
    fv, pv, pooled = pool(features, pool_map, right_edge)
    base = (fv, pv, mv, m)
    cuts = [1] + [1 + (cx - 2) * part // 14 for part in CUTS] + [cx - 1]
    rows = [range(lo, hi) for lo, hi in zip(cuts, cuts[1:])]
    steps = [("gx", 1 << b) for b in range(nx.bit_length() - 1)]
    steps += [("gy", 1 << b) for b in range(1, ny.bit_length() - 1)] + [("gy", 1)]
    up, down = edge_rows(tile, fv, left, right, (pooled,))
    above = shift(up, "gx", 1)
    below = shift(down, "gx", -1)
    out, first, ties = None, pooled, (pooled, up)
    for step, (axis, bit) in enumerate(steps):
        second = swap(first, axis, bit)
        if step == len(steps) - 1:
            break
        if step < len(rows) - 1:
            kernel = functools.partial(inner_kernel, rows[step])
            out = piece(kernel, len(rows[step]), f"inner_{step}", base, out, (), ties)
        first = join((first, second), (out,))
        ties = (first,)
    out = piece(ends_kernel, 2, "ends", base, out, (left, right, above, below), ties)
    out = piece(functools.partial(sides_kernel, rows[-1]), len(rows[-1]) + 3.5, "sides", base, out, (left, right))
    update = final(nx, ny, (first, second), readers, w_cquery, w_ckey, w_cvalue, w_value, out)
    return update.reshape(features.shape)


def solution(mesh):
    in_specs = (P("gx", "gy", None, None), P("gx", "gy", None), P("gx", "gy", None)) + (P(),) * 7
    return jax.shard_map(
        per_device, mesh=mesh, in_specs=in_specs, out_specs=P("gx", "gy", None, None), check_vma=False
    )
```

```python
import functools
import math

import jax
import jax.numpy as jnp
from jax import lax
from jax.experimental import pallas as pl
from jax.experimental.pallas import tpu as pltpu
from jax.sharding import PartitionSpec as P

BF16 = jnp.bfloat16
F32 = jnp.float32
S = 64
DEPTH = 2
CUTS = (4, 6, 9, 13)
IN_VMEM = pl.BlockSpec(memory_space=pltpu.VMEM)
IN_HBM = pl.BlockSpec(memory_space=pltpu.HBM)


def dot(a, b):
    return jnp.dot(a, b, preferred_element_type=F32)


def dot_t(a, b):
    return lax.dot_general(a, b, (((1,), (1,)), ((), ())), preferred_element_type=F32)


def t_dot(a, b):
    return lax.dot_general(a, b, (((0,), (0,)), ((), ())), preferred_element_type=F32)


def in_hbm(array):
    return pltpu.with_memory_space_constraint(array, pltpu.HBM)


def params(mib):
    return pltpu.CompilerParams(vmem_limit_bytes=mib * 1024 * 1024)


def paired(ids):
    half = ids.shape[0] // 2
    return jnp.concatenate([ids[:half], ids[half:]], axis=1)


def pool_kernel(tile, nx, ny, f_ref, pm_ref, tm_ref, wq_ref, wk_ref, fv_ref, pv_ref, mv_ref, m_ref, pooled_ref, left_ref, right_ref, tv, wq, wk, sems):
    rows, span, chan = fv_ref.shape
    cy = span // tile
    small = [(tm_ref, tv), (wq_ref, wq), (wk_ref, wk), (pm_ref, pv_ref)]
    first = [pltpu.make_async_copy(src, dst, sems.at[rows + i]) for i, (src, dst) in enumerate(small)]
    beads_in = [pltpu.make_async_copy(f_ref.at[r], fv_ref.at[r], sems.at[r]) for r in range(rows)]
    for copy in first + beads_in:
        copy.start()
    block = lax.broadcasted_iota(jnp.int32, (18, 12 * tile), 1) // tile
    which = lax.broadcasted_iota(jnp.int32, (18, 12 * tile), 0)
    offset, second = which % 9, which // 9
    hit = (offset // 3 == block // 4) & (offset % 3 == block % 4 - second)
    pick = jnp.where(hit, 1 / math.sqrt(tile), 0.0).astype(BF16)
    for copy in first:
        copy.wait()
    m_ref[...] = (dot_t(wq[...], wk[...]) * (0.5 / math.sqrt(chan))).astype(BF16)
    mask = jnp.concatenate([tv[pl.ds(r, 9, stride=rows), :].astype(F32) for r in range(rows)], axis=1)
    lane = lax.broadcasted_iota(jnp.int32, mask.shape, 1)
    toward = lax.broadcasted_iota(jnp.int32, mask.shape, 0)
    mx, my = lax.axis_index("gx"), lax.axis_index("gy")
    outside = (toward // 3 == 0) & (lane // cy == jnp.where(mx == 0, 0, -1))
    outside |= (toward // 3 == 2) & (lane // cy == jnp.where(mx == nx - 1, rows - 1, -1))
    outside |= (toward % 3 == 0) & (lane % cy == jnp.where(my == 0, 0, -1))
    outside |= (toward % 3 == 2) & (lane % cy == jnp.where(my == ny - 1, cy - 1, -1))
    mask = jnp.where(outside, 0.0, mask)
    even = lane % 2 == 0
    both = jnp.concatenate([jnp.where(even, mask, 0.0), jnp.where(even, 0.0, mask)], axis=0)
    mv_ref[...] = t_dot(both.astype(BF16), pick)

    node = lax.broadcasted_iota(jnp.int32, (S, 2 * tile), 0)
    order = [c for i in range(cy // 2) for c in (i, i + cy // 2)]
    total = jnp.zeros((S, chan), F32)
    for r in range(rows):
        pairs = paired(pv_ref[r])
        onehot = jnp.concatenate(
            [(jnp.broadcast_to(pairs[i : i + 1], node.shape) == node).astype(F32).astype(BF16) for i in range(cy // 2)],
            axis=1,
        )
        beads_in[r].wait()
        total += dot(onehot, jnp.concatenate([fv_ref[r, tile * c : tile * (c + 1)] for c in order], axis=0))
        left_ref[tile * r : tile * (r + 1)] = fv_ref[r, :tile]
        right_ref[tile * r : tile * (r + 1)] = fv_ref[r, span - tile :]
    pooled_ref[...] = (total * math.sqrt(S / (rows * span))).astype(BF16)


def pool(nx, ny, features, tile_mask, pool_map, w_query, w_key):
    cx, cy, tile, chan = features.shape
    span = cy * tile
    edge = pltpu.VMEM((cx * tile, chan), BF16)
    return pl.pallas_call(
        functools.partial(pool_kernel, tile, nx, ny),
        in_specs=[IN_HBM] * 5,
        out_specs=[IN_VMEM] * 7,
        out_shape=[
            pltpu.VMEM((cx, span, chan), BF16),
            pltpu.VMEM((cx, cy, tile), jnp.int32),
            pltpu.VMEM((cx * cy, 12 * tile), F32),
            pltpu.VMEM((chan, chan), BF16),
            pltpu.VMEM((S, chan), BF16),
            edge,
            edge,
        ],
        scratch_shapes=[
            pltpu.VMEM((9 * cx, cy), jnp.int32),
            pltpu.VMEM((chan, chan), BF16),
            pltpu.VMEM((chan, chan), BF16),
            pltpu.SemaphoreType.DMA((cx + 4,)),
        ],
        compiler_params=params(16),
        name="pool",
    )(
        in_hbm(features.reshape(cx, span, chan)),
        in_hbm(pool_map),
        in_hbm(jnp.transpose(tile_mask, (2, 0, 1)).reshape(9 * cx, cy)),
        in_hbm(w_query),
        in_hbm(w_key),
    )


def attend(tile, tasks):
    waiting = []

    def finish(task, weights):
        _, windows, _, store = task
        near = jnp.concatenate([window() for window in windows], axis=0)
        store(dot(jnp.concatenate(weights, axis=1), near).astype(BF16))

    for task in tasks:
        query, windows, masks, _ = task
        weights = []
        for r, window in enumerate(windows):
            half = dot_t(query, window())
            lanes = slice(4 * tile * r, 4 * tile * (r + 1))
            mask = jnp.concatenate([jnp.broadcast_to(masks(h, lanes), (tile, 4 * tile)) for h in (0, 1)], axis=0)
            weights.append((half * jnp.tanh(half) + half).astype(BF16) * mask.astype(BF16))
        waiting.append((task, weights))
        if len(waiting) > DEPTH:
            finish(*waiting.pop(0))
    while waiting:
        finish(*waiting.pop(0))


def row_tasks(refs, row, first, last, window):
    fv, pv, mv, m, o = refs
    chan = fv.shape[2]
    cy, tile = pv.shape[1:]
    side = 2 * tile
    queries = dot(fv[row, side * first : side * last], m[...]).astype(BF16)
    tasks = []
    for j in range(first, last):

        def store(value, lo=side * j):
            o[row, lo : lo + side, :chan] = value

        tasks.append((
            queries[side * (j - first) : side * (j - first + 1)],
            [functools.partial(window, r, j) for r in (row - 1, row, row + 1)],
            lambda h, lanes, lo=row * cy + 2 * j: mv[lo + h : lo + h + 1, lanes],
            store,
        ))
    return tasks


def node_rows(refs, row):
    fv, pv, _, _, o = refs
    _, span, chan = fv.shape
    cy, tile = pv.shape[1:]
    pairs = paired(pv[row])
    node = lax.broadcasted_iota(jnp.int32, (chan, 2 * tile), 0)
    for i in range(cy // 2):
        turned = (jnp.broadcast_to(pairs[i : i + 1], node.shape) == node).astype(F32).T.astype(BF16)
        o[row, tile * i : tile * (i + 1), chan:] = turned[:tile]
        o[row, span // 2 + tile * i : span // 2 + tile * (i + 1), chan:] = turned[tile:]


def inner_tasks(refs, rows):
    fv, pv = refs[:2]
    cy, tile = pv.shape[1:]

    def window(r, j):
        return fv[r, tile * (2 * j - 1) : tile * (2 * j + 3)]

    tasks = []
    for row in rows:
        node_rows(refs, row)
        tasks += row_tasks(refs, row, 1, cy // 2 - 1, window)
    return tasks


def inner_kernel(rows, fv, pv, mv, m, *rest):
    attend(pv.shape[2], inner_tasks((fv, pv, mv, m, rest[-1]), rows))


def side_window(fv, tile, left, right):
    span = fv.shape[1]

    def window(r, j):
        if j == 0:
            return jnp.concatenate([left[tile * r : tile * (r + 1)], fv[r, : 3 * tile]], axis=0)
        if 2 * tile * (j + 1) == span:
            return jnp.concatenate([fv[r, span - 3 * tile :], right[tile * r : tile * (r + 1)]], axis=0)
        return fv[r, tile * (2 * j - 1) : tile * (2 * j + 3)]

    return window


def sides_kernel(rows, fv, pv, mv, m, out_in, left, right, *rest):
    cy, tile = pv.shape[1:]
    refs = (fv, pv, mv, m, rest[-1])
    window = side_window(fv, tile, left, right)
    tasks = inner_tasks(refs, rows)
    for row in range(1, fv.shape[0] - 1):
        for j in (0, cy // 2 - 1):
            tasks += row_tasks(refs, row, j, j + 1, window)
    attend(tile, tasks)


def ends_kernel(fv, pv, mv, m, out_in, left, right, paired_row, other_row, *rest):
    *_, o, above, below = rest
    cy, tile = pv.shape[1:]
    rows = fv.shape[0]
    refs = (fv, pv, mv, m, o)
    near = side_window(fv, tile, left, right)
    odd = lax.axis_index("gx") % 2 == 1

    @pl.when(odd)
    def _():
        above[...] = paired_row[...]
        below[...] = other_row[...]

    @pl.when(jnp.logical_not(odd))
    def _():
        above[...] = other_row[...]
        below[...] = paired_row[...]

    def window(r, j):
        if r in (-1, rows):
            return (above if r < 0 else below)[2 * tile * j : 2 * tile * (j + 2)]
        return near(r, j)

    tasks = []
    for row in (0, rows - 1):
        node_rows(refs, row)
        tasks += row_tasks(refs, row, 0, cy // 2, window)
    attend(tile, tasks)


def estimate(rows):
    return pl.CostEstimate(flops=int(rows * 400_000_000), bytes_accessed=1_000_000, transcendentals=0)


def piece(kernel, rows_done, name, base, out, near=(), ties=(), scratch=()):
    cx, span, chan = base[0].shape
    done = [] if out is None else [out]
    return pl.pallas_call(
        kernel,
        in_specs=[IN_VMEM] * (4 + len(done) + len(near)) + [pl.BlockSpec(memory_space=pl.ANY)] * len(ties),
        out_specs=IN_VMEM,
        out_shape=pltpu.VMEM((cx, span, 2 * chan), BF16),
        scratch_shapes=list(scratch),
        input_output_aliases={4: 0} if done else {},
        compiler_params=params(16),
        cost_estimate=estimate(rows_done),
        name=name,
    )(*base, *done, *near, *ties)


def final_kernel(nx, ny, n_blocks, *refs):
    blocks = refs[:n_blocks]
    readers_ref, wcq_ref, wck_ref, wcv_ref, wv_ref, o_ref, out_ref, mix, rows_out, sems = refs[n_blocks:]
    cx, span, chan = rows_out.shape
    nodes = jnp.concatenate([ref[...] for ref in blocks], axis=0)
    count = nodes.shape[0]
    mx, my = lax.axis_index("gx"), lax.axis_index("gy")
    block = lax.broadcasted_iota(jnp.int32, (readers_ref.shape[0], count), 1) // S
    rest = block // nx
    turn = (rest % (ny // 2)) * 2 + rest // (ny // 2)
    domain = ((block % nx) ^ mx) * ny + (turn ^ my)
    lane = lax.broadcasted_iota(jnp.int32, readers_ref.shape, 1)
    mine = jnp.sum(jnp.where(lane == mx * ny + my, readers_ref[...], 0), axis=1, keepdims=True)
    live = jnp.sum(jnp.where(domain == mine, 1.0, 0.0), axis=0, keepdims=True)
    query = dot(nodes[:S], wcq_ref[...]).astype(BF16)
    key = dot(nodes, wck_ref[...]).astype(BF16)
    value = dot(nodes, wcv_ref[...]).astype(BF16)
    half = dot_t(query, key) * (0.5 / math.sqrt(chan))
    weight = (half * jnp.tanh(half) + half).astype(BF16).astype(F32) * live
    mix[:chan] = wv_ref[...]
    mix[chan : chan + S] = (dot(weight.astype(BF16), value) / math.sqrt(S)).astype(BF16)
    mix[chan + S :] = jnp.zeros((chan - S, chan), BF16)

    def send(r):
        return pltpu.make_async_copy(rows_out.at[r], out_ref.at[r], sems.at[r])

    for r in range(cx):
        rows_out[r] = dot(o_ref[r], mix[...]).astype(BF16)
        send(r).start()
    for r in range(cx):
        send(r).wait()


def final(nx, ny, blocks, readers, w_cquery, w_ckey, w_cvalue, w_value, out):
    cx, span, wide = out.shape
    chan = wide // 2
    return pl.pallas_call(
        functools.partial(final_kernel, nx, ny, len(blocks)),
        in_specs=[IN_VMEM] * (len(blocks) + 6),
        out_specs=IN_HBM,
        out_shape=jax.ShapeDtypeStruct((cx, span, chan), BF16),
        scratch_shapes=[
            pltpu.VMEM((2 * chan, chan), BF16),
            pltpu.VMEM((cx, span, chan), BF16),
            pltpu.SemaphoreType.DMA((cx,)),
        ],
        compiler_params=params(16),
        name="final",
    )(*blocks, readers.T, w_cquery, w_ckey, w_cvalue, w_value, out)


def shift(array, axis, step):
    count = lax.axis_size(axis)
    return lax.ppermute(array, axis, [(i, (i + step) % count) for i in range(count)])


def swap(array, axis, bits):
    return lax.ppermute(array, axis, [(i, i ^ bits) for i in range(lax.axis_size(axis))])


def join_kernel(count, *refs):
    parts, out = refs[:count], refs[-1]
    at = 0
    for part in parts:
        out[at : at + part.shape[0]] = part[...]
        at += part.shape[0]


def join(parts, ties):
    rows = sum(part.shape[0] for part in parts)
    return pl.pallas_call(
        functools.partial(join_kernel, len(parts)),
        in_specs=[IN_VMEM] * len(parts) + [pl.BlockSpec(memory_space=pl.ANY)] * len(ties),
        out_specs=IN_VMEM,
        out_shape=pltpu.VMEM((rows, parts[0].shape[1]), BF16),
        compiler_params=params(4),
        name="join",
    )(*parts, *ties)


def edge_rows_kernel(tile, fv_ref, left_ref, right_ref, *rest):
    to_refs = rest[-2:]
    rows, span, _ = fv_ref.shape
    odd = lax.axis_index("gx") % 2
    for ref, low in ((to_refs[0], odd), (to_refs[1], 1 - odd)):
        r = (1 - low) * (rows - 1)
        corner = pl.ds(pl.multiple_of(tile * r, tile), tile)
        ref[:tile] = left_ref[corner]
        ref[tile : tile + span] = fv_ref[r]
        ref[tile + span :] = right_ref[corner]


def edge_rows(tile, fv, left, right, ties):
    _, span, chan = fv.shape
    edge = pltpu.VMEM((span + 2 * tile, chan), BF16)
    return pl.pallas_call(
        functools.partial(edge_rows_kernel, tile),
        in_specs=[IN_VMEM] * 3 + [pl.BlockSpec(memory_space=pl.ANY)] * len(ties),
        out_specs=[IN_VMEM] * 2,
        out_shape=[edge, edge],
        compiler_params=params(4),
        name="edge_rows",
    )(fv, left, right, *ties)


def swap_across(array, nx, ny):
    moves = []
    for x in range(nx):
        for y in range(ny):
            near = x + 1 if x % 2 else x - 1
            there = near * ny + y if 0 <= near < nx else x * ny + (y ^ 1)
            moves.append((x * ny + y, there))
    return lax.ppermute(array, ("gx", "gy"), moves)


def per_device(features, tile_mask, pool_map, readers, w_query, w_key, w_value, w_cquery, w_ckey, w_cvalue):
    cx, cy, tile, chan = features.shape
    nx, ny = lax.axis_size("gx"), lax.axis_size("gy")
    *base, pooled, left_edge, right_edge = pool(nx, ny, features, tile_mask, pool_map, w_query, w_key)
    fv = base[0]
    cuts = [1] + [1 + (cx - 2) * part // 14 for part in CUTS] + [cx - 1]
    rows = [range(lo, hi) for lo, hi in zip(cuts, cuts[1:])]
    steps = [("gx", 1 << b) for b in range(nx.bit_length() - 1)]
    steps += [("gy", 1 << b) for b in range(1, ny.bit_length() - 1)] + [("gy", 1)]
    left = shift(right_edge, "gy", 1)
    right = shift(left_edge, "gy", -1)
    out, first, ties = None, pooled, (pooled,)
    for step, (axis, bit) in enumerate(steps):
        second = swap(first, axis, bit)
        if step == 1:
            inward, outward = edge_rows(tile, fv, left, right, (out,))
            paired_row = swap(inward, "gx", 1)
            other_row = swap_across(outward, nx, ny)
            ties += (inward,)
        if step == len(steps) - 1:
            break
        if step < len(rows) - 1:
            kernel = functools.partial(inner_kernel, rows[step])
            out = piece(kernel, len(rows[step]), f"inner_{step}", base, out, (), ties)
        first = join((first, second), (out,))
        ties = (first,)
    out = piece(ends_kernel, 2, "ends", base, out, (left, right, paired_row, other_row), ties, [pltpu.VMEM(inward.shape, BF16)] * 2)
    out = piece(functools.partial(sides_kernel, rows[-1]), len(rows[-1]) + 3.5, "sides", base, out, (left, right))
    update = final(nx, ny, (first, second), readers, w_cquery, w_ckey, w_cvalue, w_value, out)
    return update.reshape(features.shape)


def solution(mesh):
    in_specs = (P("gx", "gy", None, None), P("gx", "gy", None), P("gx", "gy", None)) + (P(),) * 7
    return jax.shard_map(
        per_device, mesh=mesh, in_specs=in_specs, out_specs=P("gx", "gy", None, None), check_vma=False
    )
```

```python
import functools
import math

import jax
import jax.numpy as jnp
from jax import lax
from jax.experimental import pallas as pl
from jax.experimental.pallas import tpu as pltpu
from jax.sharding import PartitionSpec as P

BF16 = jnp.bfloat16
F32 = jnp.float32
S = 64
DEPTH = 2
CUTS = (4, 6, 9, 13)
IN_VMEM = pl.BlockSpec(memory_space=pltpu.VMEM)
IN_HBM = pl.BlockSpec(memory_space=pltpu.HBM)


def dot(a, b):
    return jnp.dot(a, b, preferred_element_type=F32)


def dot_t(a, b):
    return lax.dot_general(a, b, (((1,), (1,)), ((), ())), preferred_element_type=F32)


def t_dot(a, b):
    return lax.dot_general(a, b, (((0,), (0,)), ((), ())), preferred_element_type=F32)


def in_hbm(array):
    return pltpu.with_memory_space_constraint(array, pltpu.HBM)


def params(mib):
    return pltpu.CompilerParams(vmem_limit_bytes=mib * 1024 * 1024)


def paired(ids):
    half = ids.shape[0] // 2
    return jnp.concatenate([ids[:half], ids[half:]], axis=1)


def pool_kernel(tile, nx, ny, f_ref, pm_ref, tm_ref, wq_ref, wk_ref, fv_ref, pv_ref, mv_ref, m_ref, pooled_ref, inward_ref, outward_ref, tv, wq, wk, sems):
    rows, span, chan = fv_ref.shape
    cy = span // tile
    small = [(tm_ref, tv), (wq_ref, wq), (wk_ref, wk), (pm_ref, pv_ref)]
    first = [pltpu.make_async_copy(src, dst, sems.at[rows + i]) for i, (src, dst) in enumerate(small)]
    beads_in = [pltpu.make_async_copy(f_ref.at[r], fv_ref.at[r], sems.at[r]) for r in range(rows)]
    for copy in first + beads_in:
        copy.start()
    block = lax.broadcasted_iota(jnp.int32, (18, 12 * tile), 1) // tile
    which = lax.broadcasted_iota(jnp.int32, (18, 12 * tile), 0)
    offset, second = which % 9, which // 9
    hit = (offset // 3 == block // 4) & (offset % 3 == block % 4 - second)
    pick = jnp.where(hit, 1 / math.sqrt(tile), 0.0).astype(BF16)
    for copy in first:
        copy.wait()
    m_ref[...] = (dot_t(wq[...], wk[...]) * (0.5 / math.sqrt(chan))).astype(BF16)
    mask = jnp.concatenate([tv[pl.ds(r, 9, stride=rows), :].astype(F32) for r in range(rows)], axis=1)
    lane = lax.broadcasted_iota(jnp.int32, mask.shape, 1)
    toward = lax.broadcasted_iota(jnp.int32, mask.shape, 0)
    mx, my = lax.axis_index("gx"), lax.axis_index("gy")
    outside = (toward // 3 == 0) & (lane // cy == jnp.where(mx == 0, 0, -1))
    outside |= (toward // 3 == 2) & (lane // cy == jnp.where(mx == nx - 1, rows - 1, -1))
    outside |= (toward % 3 == 0) & (lane % cy == jnp.where(my == 0, 0, -1))
    outside |= (toward % 3 == 2) & (lane % cy == jnp.where(my == ny - 1, cy - 1, -1))
    mask = jnp.where(outside, 0.0, mask)
    even = lane % 2 == 0
    both = jnp.concatenate([jnp.where(even, mask, 0.0), jnp.where(even, 0.0, mask)], axis=0)
    mv_ref[...] = t_dot(both.astype(BF16), pick)

    node = lax.broadcasted_iota(jnp.int32, (S, 2 * tile), 0)
    order = [c for i in range(cy // 2) for c in (i, i + cy // 2)]
    total = jnp.zeros((S, chan), F32)
    for r in range(rows):
        pairs = paired(pv_ref[r])
        onehot = jnp.concatenate(
            [(jnp.broadcast_to(pairs[i : i + 1], node.shape) == node).astype(F32).astype(BF16) for i in range(cy // 2)],
            axis=1,
        )
        beads_in[r].wait()
        total += dot(onehot, jnp.concatenate([fv_ref[r, tile * c : tile * (c + 1)] for c in order], axis=0))
        for ref, low in ((inward_ref, my % 2), (outward_ref, 1 - my % 2)):
            column = pl.ds(pl.multiple_of((1 - low) * (span - tile), tile), tile)
            ref[tile * r : tile * (r + 1)] = fv_ref[r, column]
    pooled_ref[...] = (total * math.sqrt(S / (rows * span))).astype(BF16)


def pool(nx, ny, features, tile_mask, pool_map, w_query, w_key):
    cx, cy, tile, chan = features.shape
    span = cy * tile
    edge = pltpu.VMEM((cx * tile, chan), BF16)
    return pl.pallas_call(
        functools.partial(pool_kernel, tile, nx, ny),
        in_specs=[IN_HBM] * 5,
        out_specs=[IN_VMEM] * 7,
        out_shape=[
            pltpu.VMEM((cx, span, chan), BF16),
            pltpu.VMEM((cx, cy, tile), jnp.int32),
            pltpu.VMEM((cx * cy, 12 * tile), F32),
            pltpu.VMEM((chan, chan), BF16),
            pltpu.VMEM((S, chan), BF16),
            edge,
            edge,
        ],
        scratch_shapes=[
            pltpu.VMEM((9 * cx, cy), jnp.int32),
            pltpu.VMEM((chan, chan), BF16),
            pltpu.VMEM((chan, chan), BF16),
            pltpu.SemaphoreType.DMA((cx + 4,)),
        ],
        compiler_params=params(16),
        name="pool",
    )(
        in_hbm(features.reshape(cx, span, chan)),
        in_hbm(pool_map),
        in_hbm(jnp.transpose(tile_mask, (2, 0, 1)).reshape(9 * cx, cy)),
        in_hbm(w_query),
        in_hbm(w_key),
    )


def attend(tile, tasks):
    waiting = []

    def finish(task, weights):
        _, windows, _, store = task
        near = jnp.concatenate([window() for window in windows], axis=0)
        store(dot(jnp.concatenate(weights, axis=1), near).astype(BF16))

    for task in tasks:
        query, windows, masks, _ = task
        weights = []
        for r, window in enumerate(windows):
            half = dot_t(query, window())
            lanes = slice(4 * tile * r, 4 * tile * (r + 1))
            mask = jnp.concatenate([jnp.broadcast_to(masks(h, lanes), (tile, 4 * tile)) for h in (0, 1)], axis=0)
            weights.append((half * jnp.tanh(half) + half).astype(BF16) * mask.astype(BF16))
        waiting.append((task, weights))
        if len(waiting) > DEPTH:
            finish(*waiting.pop(0))
    while waiting:
        finish(*waiting.pop(0))


def row_tasks(refs, row, first, last, window):
    fv, pv, mv, m, o = refs
    chan = fv.shape[2]
    cy, tile = pv.shape[1:]
    side = 2 * tile
    queries = dot(fv[row, side * first : side * last], m[...]).astype(BF16)
    tasks = []
    for j in range(first, last):

        def store(value, lo=side * j):
            o[row, lo : lo + side, :chan] = value

        tasks.append((
            queries[side * (j - first) : side * (j - first + 1)],
            [functools.partial(window, r, j) for r in (row - 1, row, row + 1)],
            lambda h, lanes, lo=row * cy + 2 * j: mv[lo + h : lo + h + 1, lanes],
            store,
        ))
    return tasks


def node_rows(refs, row):
    fv, pv, _, _, o = refs
    _, span, chan = fv.shape
    cy, tile = pv.shape[1:]
    pairs = paired(pv[row])
    node = lax.broadcasted_iota(jnp.int32, (chan, 2 * tile), 0)
    for i in range(cy // 2):
        turned = (jnp.broadcast_to(pairs[i : i + 1], node.shape) == node).astype(F32).T.astype(BF16)
        o[row, tile * i : tile * (i + 1), chan:] = turned[:tile]
        o[row, span // 2 + tile * i : span // 2 + tile * (i + 1), chan:] = turned[tile:]


def inner_tasks(refs, rows):
    fv, pv = refs[:2]
    cy, tile = pv.shape[1:]

    def window(r, j):
        return fv[r, tile * (2 * j - 1) : tile * (2 * j + 3)]

    tasks = []
    for row in rows:
        node_rows(refs, row)
        tasks += row_tasks(refs, row, 1, cy // 2 - 1, window)
    return tasks


def inner_kernel(rows, fv, pv, mv, m, *rest):
    attend(pv.shape[2], inner_tasks((fv, pv, mv, m, rest[-1]), rows))


def side_window(fv, tile, left, right):
    span = fv.shape[1]

    def window(r, j):
        if j == 0:
            return jnp.concatenate([left[tile * r : tile * (r + 1)], fv[r, : 3 * tile]], axis=0)
        if 2 * tile * (j + 1) == span:
            return jnp.concatenate([fv[r, span - 3 * tile :], right[tile * r : tile * (r + 1)]], axis=0)
        return fv[r, tile * (2 * j - 1) : tile * (2 * j + 3)]

    return window


def sides_kernel(rows, fv, pv, mv, m, out_in, left, right, *rest):
    cy, tile = pv.shape[1:]
    refs = (fv, pv, mv, m, rest[-1])
    window = side_window(fv, tile, left, right)
    tasks = inner_tasks(refs, rows)
    for row in range(1, fv.shape[0] - 1):
        for j in (0, cy // 2 - 1):
            tasks += row_tasks(refs, row, j, j + 1, window)
    attend(tile, tasks)


def ends_kernel(fv, pv, mv, m, out_in, left, right, paired_row, other_row, *rest):
    *_, o, above, below = rest
    cy, tile = pv.shape[1:]
    rows = fv.shape[0]
    refs = (fv, pv, mv, m, o)
    near = side_window(fv, tile, left, right)
    odd = lax.axis_index("gx") % 2 == 1

    @pl.when(odd)
    def _():
        above[...] = paired_row[...]
        below[...] = other_row[...]

    @pl.when(jnp.logical_not(odd))
    def _():
        above[...] = other_row[...]
        below[...] = paired_row[...]

    def window(r, j):
        if r in (-1, rows):
            return (above if r < 0 else below)[2 * tile * j : 2 * tile * (j + 2)]
        return near(r, j)

    tasks = []
    for row in (0, rows - 1):
        node_rows(refs, row)
        tasks += row_tasks(refs, row, 0, cy // 2, window)
    attend(tile, tasks)


def estimate(rows):
    return pl.CostEstimate(flops=int(rows * 400_000_000), bytes_accessed=1_000_000, transcendentals=0)


def piece(kernel, rows_done, name, base, out, near=(), ties=(), scratch=()):
    cx, span, chan = base[0].shape
    done = [] if out is None else [out]
    return pl.pallas_call(
        kernel,
        in_specs=[IN_VMEM] * (4 + len(done) + len(near)) + [pl.BlockSpec(memory_space=pl.ANY)] * len(ties),
        out_specs=IN_VMEM,
        out_shape=pltpu.VMEM((cx, span, 2 * chan), BF16),
        scratch_shapes=list(scratch),
        input_output_aliases={4: 0} if done else {},
        compiler_params=params(16),
        cost_estimate=estimate(rows_done),
        name=name,
    )(*base, *done, *near, *ties)


def final_kernel(nx, ny, n_blocks, *refs):
    blocks = refs[:n_blocks]
    readers_ref, wcq_ref, wck_ref, wcv_ref, wv_ref, o_ref, out_ref, mix, rows_out, sems = refs[n_blocks:]
    cx, span, chan = rows_out.shape
    nodes = jnp.concatenate([ref[...] for ref in blocks], axis=0)
    count = nodes.shape[0]
    mx, my = lax.axis_index("gx"), lax.axis_index("gy")
    block = lax.broadcasted_iota(jnp.int32, (readers_ref.shape[0], count), 1) // S
    rest = block // nx
    turn = (rest % (ny // 2)) * 2 + rest // (ny // 2)
    domain = ((block % nx) ^ mx) * ny + (turn ^ my)
    lane = lax.broadcasted_iota(jnp.int32, readers_ref.shape, 1)
    mine = jnp.sum(jnp.where(lane == mx * ny + my, readers_ref[...], 0), axis=1, keepdims=True)
    live = jnp.sum(jnp.where(domain == mine, 1.0, 0.0), axis=0, keepdims=True)
    query = dot(nodes[:S], wcq_ref[...]).astype(BF16)
    key = dot(nodes, wck_ref[...]).astype(BF16)
    value = dot(nodes, wcv_ref[...]).astype(BF16)
    half = dot_t(query, key) * (0.5 / math.sqrt(chan))
    weight = (half * jnp.tanh(half) + half).astype(BF16).astype(F32) * live
    mix[:chan] = wv_ref[...]
    mix[chan : chan + S] = (dot(weight.astype(BF16), value) / math.sqrt(S)).astype(BF16)
    mix[chan + S :] = jnp.zeros((chan - S, chan), BF16)

    def send(r):
        return pltpu.make_async_copy(rows_out.at[r], out_ref.at[r], sems.at[r])

    for r in range(cx):
        rows_out[r] = dot(o_ref[r], mix[...]).astype(BF16)
        send(r).start()
    for r in range(cx):
        send(r).wait()


def final(nx, ny, blocks, readers, w_cquery, w_ckey, w_cvalue, w_value, out):
    cx, span, wide = out.shape
    chan = wide // 2
    return pl.pallas_call(
        functools.partial(final_kernel, nx, ny, len(blocks)),
        in_specs=[IN_VMEM] * (len(blocks) + 6),
        out_specs=IN_HBM,
        out_shape=jax.ShapeDtypeStruct((cx, span, chan), BF16),
        scratch_shapes=[
            pltpu.VMEM((2 * chan, chan), BF16),
            pltpu.VMEM((cx, span, chan), BF16),
            pltpu.SemaphoreType.DMA((cx,)),
        ],
        compiler_params=params(16),
        name="final",
    )(*blocks, readers.T, w_cquery, w_ckey, w_cvalue, w_value, out)


def swap(array, axis, bits):
    return lax.ppermute(array, axis, [(i, i ^ bits) for i in range(lax.axis_size(axis))])


def join_kernel(count, *refs):
    parts, out = refs[:count], refs[-1]
    at = 0
    for part in parts:
        out[at : at + part.shape[0]] = part[...]
        at += part.shape[0]


def join(parts, ties):
    rows = sum(part.shape[0] for part in parts)
    return pl.pallas_call(
        functools.partial(join_kernel, len(parts)),
        in_specs=[IN_VMEM] * len(parts) + [pl.BlockSpec(memory_space=pl.ANY)] * len(ties),
        out_specs=IN_VMEM,
        out_shape=pltpu.VMEM((rows, parts[0].shape[1]), BF16),
        compiler_params=params(4),
        name="join",
    )(*parts, *ties)


def edge_rows_kernel(tile, fv_ref, paired_ref, other_ref, *rest):
    left_ref, right_ref, inward_ref, outward_ref = rest[-4:]
    rows, span, _ = fv_ref.shape

    @pl.when(lax.axis_index("gy") % 2 == 1)
    def _():
        left_ref[...] = paired_ref[...]
        right_ref[...] = other_ref[...]

    @pl.when(lax.axis_index("gy") % 2 == 0)
    def _():
        left_ref[...] = other_ref[...]
        right_ref[...] = paired_ref[...]

    odd = lax.axis_index("gx") % 2
    for ref, low in ((inward_ref, odd), (outward_ref, 1 - odd)):
        r = (1 - low) * (rows - 1)
        corner = pl.ds(pl.multiple_of(tile * r, tile), tile)
        ref[:tile] = left_ref[corner]
        ref[tile : tile + span] = fv_ref[r]
        ref[tile + span :] = right_ref[corner]


def edge_rows(tile, fv, paired_column, other_column, ties):
    rows, span, chan = fv.shape
    column = pltpu.VMEM((rows * tile, chan), BF16)
    edge = pltpu.VMEM((span + 2 * tile, chan), BF16)
    return pl.pallas_call(
        functools.partial(edge_rows_kernel, tile),
        in_specs=[IN_VMEM] * 3 + [pl.BlockSpec(memory_space=pl.ANY)] * len(ties),
        out_specs=[IN_VMEM] * 4,
        out_shape=[column, column, edge, edge],
        compiler_params=params(4),
        name="edge_rows",
    )(fv, paired_column, other_column, *ties)


def swap_across(array, axis, nx, ny):
    moves = []
    for x in range(nx):
        for y in range(ny):
            if axis == "gx":
                near = x + 1 if x % 2 else x - 1
                there = near * ny + y if 0 <= near < nx else x * ny + (y ^ 1)
            else:
                near = y + 1 if y % 2 else y - 1
                there = x * ny + near if 0 <= near < ny else (x ^ 1) * ny + y
            moves.append((x * ny + y, there))
    return lax.ppermute(array, ("gx", "gy"), moves)


def per_device(features, tile_mask, pool_map, readers, w_query, w_key, w_value, w_cquery, w_ckey, w_cvalue):
    cx, cy, tile, chan = features.shape
    nx, ny = lax.axis_size("gx"), lax.axis_size("gy")
    *base, pooled, inward, outward = pool(nx, ny, features, tile_mask, pool_map, w_query, w_key)
    fv = base[0]
    cuts = [1] + [1 + (cx - 2) * part // 14 for part in CUTS] + [cx - 1]
    rows = [range(lo, hi) for lo, hi in zip(cuts, cuts[1:])]
    steps = [("gx", 1 << b) for b in range(nx.bit_length() - 1)]
    steps += [("gy", 1 << b) for b in range(1, ny.bit_length() - 1)] + [("gy", 1)]
    paired_column = swap(inward, "gy", 1)
    other_column = swap_across(outward, "gy", nx, ny)
    out, first, ties = None, pooled, (pooled,)
    for step, (axis, bit) in enumerate(steps):
        second = swap(first, axis, bit)
        if step == 2:
            left, right, inward, outward = edge_rows(tile, fv, paired_column, other_column, (out, first))
            paired_row = swap(inward, "gx", 1)
            other_row = swap_across(outward, "gx", nx, ny)
            ties += (inward,)
        if step == len(steps) - 1:
            break
        if step < len(rows) - 1:
            kernel = functools.partial(inner_kernel, rows[step])
            out = piece(kernel, len(rows[step]), f"inner_{step}", base, out, (), ties)
        first = join((first, second), (out,))
        ties = (first,)
    out = piece(functools.partial(sides_kernel, rows[-1]), len(rows[-1]) + 3.5, "sides", base, out, (left, right), ties)
    out = piece(ends_kernel, 2, "ends", base, out, (left, right, paired_row, other_row), (), [pltpu.VMEM(inward.shape, BF16)] * 2)
    update = final(nx, ny, (first, second), readers, w_cquery, w_ckey, w_cvalue, w_value, out)
    return update.reshape(features.shape)


def solution(mesh):
    in_specs = (P("gx", "gy", None, None), P("gx", "gy", None), P("gx", "gy", None)) + (P(),) * 7
    return jax.shard_map(
        per_device, mesh=mesh, in_specs=in_specs, out_specs=P("gx", "gy", None, None), check_vma=False
    )
```

```python
import functools
import math

import jax
import jax.numpy as jnp
from jax import lax
from jax.experimental import pallas as pl
from jax.experimental.pallas import tpu as pltpu
from jax.sharding import PartitionSpec as P

BF16 = jnp.bfloat16
F32 = jnp.float32
S = 64
DEPTH = 2
CUTS = (4, 7, 10, 14)
IN_VMEM = pl.BlockSpec(memory_space=pltpu.VMEM)
IN_HBM = pl.BlockSpec(memory_space=pltpu.HBM)


def dot(a, b):
    return jnp.dot(a, b, preferred_element_type=F32)


def dot_t(a, b):
    return lax.dot_general(a, b, (((1,), (1,)), ((), ())), preferred_element_type=F32)


def t_dot(a, b):
    return lax.dot_general(a, b, (((0,), (0,)), ((), ())), preferred_element_type=F32)


def in_hbm(array):
    return pltpu.with_memory_space_constraint(array, pltpu.HBM)


def params(mib):
    return pltpu.CompilerParams(vmem_limit_bytes=mib * 1024 * 1024)


def paired(ids):
    half = ids.shape[0] // 2
    return jnp.concatenate([ids[:half], ids[half:]], axis=1)


def pool_kernel(tile, nx, ny, f_ref, pm_ref, tm_ref, wq_ref, wk_ref, fv_ref, pv_ref, mv_ref, m_ref, pooled_ref, inward_ref, outward_ref, tv, wq, wk, sems):
    rows, span, chan = fv_ref.shape
    cy = span // tile
    small = [(tm_ref, tv), (wq_ref, wq), (wk_ref, wk), (pm_ref, pv_ref)]
    first = [pltpu.make_async_copy(src, dst, sems.at[rows + i]) for i, (src, dst) in enumerate(small)]
    beads_in = [pltpu.make_async_copy(f_ref.at[r], fv_ref.at[r], sems.at[r]) for r in range(rows)]
    for copy in first + beads_in:
        copy.start()
    block = lax.broadcasted_iota(jnp.int32, (18, 12 * tile), 1) // tile
    which = lax.broadcasted_iota(jnp.int32, (18, 12 * tile), 0)
    offset, second = which % 9, which // 9
    hit = (offset // 3 == block // 4) & (offset % 3 == block % 4 - second)
    pick = jnp.where(hit, 1 / math.sqrt(tile), 0.0).astype(BF16)
    for copy in first:
        copy.wait()
    m_ref[...] = (dot_t(wq[...], wk[...]) * (0.5 / math.sqrt(chan))).astype(BF16)
    mask = jnp.concatenate([tv[pl.ds(r, 9, stride=rows), :].astype(F32) for r in range(rows)], axis=1)
    lane = lax.broadcasted_iota(jnp.int32, mask.shape, 1)
    toward = lax.broadcasted_iota(jnp.int32, mask.shape, 0)
    mx, my = lax.axis_index("gx"), lax.axis_index("gy")
    outside = (toward // 3 == 0) & (lane // cy == jnp.where(mx == 0, 0, -1))
    outside |= (toward // 3 == 2) & (lane // cy == jnp.where(mx == nx - 1, rows - 1, -1))
    outside |= (toward % 3 == 0) & (lane % cy == jnp.where(my == 0, 0, -1))
    outside |= (toward % 3 == 2) & (lane % cy == jnp.where(my == ny - 1, cy - 1, -1))
    mask = jnp.where(outside, 0.0, mask)
    even = lane % 2 == 0
    both = jnp.concatenate([jnp.where(even, mask, 0.0), jnp.where(even, 0.0, mask)], axis=0)
    mv_ref[...] = t_dot(both.astype(BF16), pick)

    node = lax.broadcasted_iota(jnp.int32, (S, 2 * tile), 0)
    order = [c for i in range(cy // 2) for c in (i, i + cy // 2)]
    total = jnp.zeros((S, chan), F32)
    for low in range(0, rows, 8):
        group = range(low, min(low + 8, rows))
        hot, beads = [], []
        for r in group:
            pairs = paired(pv_ref[r])
            hot += [
                (jnp.broadcast_to(pairs[i : i + 1], node.shape) == node).astype(F32).astype(BF16) for i in range(cy // 2)
            ]
        for r in group:
            beads_in[r].wait()
        for r in group:
            beads += [fv_ref[r, tile * c : tile * (c + 1)] for c in order]
        total += dot(jnp.concatenate(hot, axis=1), jnp.concatenate(beads, axis=0))
        for r in group:
            for ref, low_side in ((inward_ref, my % 2), (outward_ref, 1 - my % 2)):
                column = pl.ds(pl.multiple_of((1 - low_side) * (span - tile), tile), tile)
                ref[tile * r : tile * (r + 1)] = fv_ref[r, column]
    pooled_ref[...] = (total * math.sqrt(S / (rows * span))).astype(BF16)


def pool(nx, ny, features, tile_mask, pool_map, w_query, w_key):
    cx, cy, tile, chan = features.shape
    span = cy * tile
    edge = pltpu.VMEM((cx * tile, chan), BF16)
    return pl.pallas_call(
        functools.partial(pool_kernel, tile, nx, ny),
        in_specs=[IN_HBM] * 5,
        out_specs=[IN_VMEM] * 7,
        out_shape=[
            pltpu.VMEM((cx, span, chan), BF16),
            pltpu.VMEM((cx, cy, tile), jnp.int32),
            pltpu.VMEM((cx * cy, 12 * tile), F32),
            pltpu.VMEM((chan, chan), BF16),
            pltpu.VMEM((S, chan), BF16),
            edge,
            edge,
        ],
        scratch_shapes=[
            pltpu.VMEM((9 * cx, cy), jnp.int32),
            pltpu.VMEM((chan, chan), BF16),
            pltpu.VMEM((chan, chan), BF16),
            pltpu.SemaphoreType.DMA((cx + 4,)),
        ],
        compiler_params=params(16),
        name="pool",
    )(
        in_hbm(features.reshape(cx, span, chan)),
        in_hbm(pool_map),
        in_hbm(jnp.transpose(tile_mask, (2, 0, 1)).reshape(9 * cx, cy)),
        in_hbm(w_query),
        in_hbm(w_key),
    )


def attend(tile, tasks):
    waiting = []

    def finish(task, weights):
        _, windows, _, store = task
        near = jnp.concatenate([window() for window in windows], axis=0)
        store(dot(jnp.concatenate(weights, axis=1), near).astype(BF16))

    for task in tasks:
        query, windows, masks, _ = task
        weights = []
        for r, window in enumerate(windows):
            half = dot_t(query, window())
            lanes = slice(4 * tile * r, 4 * tile * (r + 1))
            mask = jnp.concatenate([jnp.broadcast_to(masks(h, lanes), (tile, 4 * tile)) for h in (0, 1)], axis=0)
            weights.append((half * jnp.tanh(half) + half).astype(BF16) * mask.astype(BF16))
        waiting.append((task, weights))
        if len(waiting) > DEPTH:
            finish(*waiting.pop(0))
    while waiting:
        finish(*waiting.pop(0))


def row_tasks(refs, row, first, last, window):
    fv, pv, mv, m, o = refs
    chan = fv.shape[2]
    cy, tile = pv.shape[1:]
    side = 2 * tile
    queries = dot(fv[row, side * first : side * last], m[...]).astype(BF16)
    tasks = []
    for j in range(first, last):

        def store(value, lo=side * j):
            o[row, lo : lo + side, :chan] = value

        tasks.append((
            queries[side * (j - first) : side * (j - first + 1)],
            [functools.partial(window, r, j) for r in (row - 1, row, row + 1)],
            lambda h, lanes, lo=row * cy + 2 * j: mv[lo + h : lo + h + 1, lanes],
            store,
        ))
    return tasks


def node_rows(refs, row):
    fv, pv, _, _, o = refs
    _, span, chan = fv.shape
    cy, tile = pv.shape[1:]
    pairs = paired(pv[row])
    node = lax.broadcasted_iota(jnp.int32, (chan, 2 * tile), 0)
    for i in range(cy // 2):
        turned = (jnp.broadcast_to(pairs[i : i + 1], node.shape) == node).astype(F32).T.astype(BF16)
        o[row, tile * i : tile * (i + 1), chan:] = turned[:tile]
        o[row, span // 2 + tile * i : span // 2 + tile * (i + 1), chan:] = turned[tile:]


def inner_tasks(refs, rows):
    fv, pv = refs[:2]
    cy, tile = pv.shape[1:]

    def window(r, j):
        return fv[r, tile * (2 * j - 1) : tile * (2 * j + 3)]

    tasks = []
    for row in rows:
        node_rows(refs, row)
        tasks += row_tasks(refs, row, 1, cy // 2 - 1, window)
    return tasks


def inner_kernel(rows, fv, pv, mv, m, *rest):
    attend(pv.shape[2], inner_tasks((fv, pv, mv, m, rest[-1]), rows))


def side_window(fv, tile, left, right):
    span = fv.shape[1]

    def window(r, j):
        if j == 0:
            return jnp.concatenate([left[tile * r : tile * (r + 1)], fv[r, : 3 * tile]], axis=0)
        if 2 * tile * (j + 1) == span:
            return jnp.concatenate([fv[r, span - 3 * tile :], right[tile * r : tile * (r + 1)]], axis=0)
        return fv[r, tile * (2 * j - 1) : tile * (2 * j + 3)]

    return window


def sides_kernel(rows, fv, pv, mv, m, out_in, left, right, *rest):
    cy, tile = pv.shape[1:]
    refs = (fv, pv, mv, m, rest[-1])
    window = side_window(fv, tile, left, right)
    tasks = inner_tasks(refs, rows)
    for row in range(1, fv.shape[0] - 1):
        for j in (0, cy // 2 - 1):
            tasks += row_tasks(refs, row, j, j + 1, window)
    attend(tile, tasks)


def ends_kernel(fv, pv, mv, m, out_in, left, right, paired_row, other_row, *rest):
    *_, o, above, below = rest
    cy, tile = pv.shape[1:]
    rows = fv.shape[0]
    refs = (fv, pv, mv, m, o)
    near = side_window(fv, tile, left, right)
    odd = lax.axis_index("gx") % 2 == 1

    @pl.when(odd)
    def _():
        above[...] = paired_row[...]
        below[...] = other_row[...]

    @pl.when(jnp.logical_not(odd))
    def _():
        above[...] = other_row[...]
        below[...] = paired_row[...]

    def window(r, j):
        if r in (-1, rows):
            return (above if r < 0 else below)[2 * tile * j : 2 * tile * (j + 2)]
        return near(r, j)

    tasks = []
    for row in (0, rows - 1):
        node_rows(refs, row)
        tasks += row_tasks(refs, row, 0, cy // 2, window)
    attend(tile, tasks)


def estimate(rows):
    return pl.CostEstimate(flops=int(rows * 400_000_000), bytes_accessed=1_000_000, transcendentals=0)


def piece(kernel, rows_done, name, base, out, near=(), ties=(), scratch=()):
    cx, span, chan = base[0].shape
    done = [] if out is None else [out]
    return pl.pallas_call(
        kernel,
        in_specs=[IN_VMEM] * (4 + len(done) + len(near)) + [pl.BlockSpec(memory_space=pl.ANY)] * len(ties),
        out_specs=IN_VMEM,
        out_shape=pltpu.VMEM((cx, span, 2 * chan), BF16),
        scratch_shapes=list(scratch),
        input_output_aliases={4: 0} if done else {},
        compiler_params=params(16),
        cost_estimate=estimate(rows_done),
        name=name,
    )(*base, *done, *near, *ties)


def final_kernel(nx, ny, n_blocks, *refs):
    blocks = refs[:n_blocks]
    readers_ref, wcq_ref, wck_ref, wcv_ref, wv_ref, o_ref, out_ref, mix, rows_out, sems = refs[n_blocks:]
    cx, span, chan = rows_out.shape
    nodes = jnp.concatenate([ref[...] for ref in blocks], axis=0)
    count = nodes.shape[0]
    mx, my = lax.axis_index("gx"), lax.axis_index("gy")
    block = lax.broadcasted_iota(jnp.int32, (readers_ref.shape[0], count), 1) // S
    rest = block // nx
    turn = (rest % (ny // 2)) * 2 + rest // (ny // 2)
    domain = ((block % nx) ^ mx) * ny + (turn ^ my)
    lane = lax.broadcasted_iota(jnp.int32, readers_ref.shape, 1)
    mine = jnp.sum(jnp.where(lane == mx * ny + my, readers_ref[...], 0), axis=1, keepdims=True)
    live = jnp.sum(jnp.where(domain == mine, 1.0, 0.0), axis=0, keepdims=True)
    query = dot(nodes[:S], wcq_ref[...]).astype(BF16)
    key = dot(nodes, wck_ref[...]).astype(BF16)
    value = dot(nodes, wcv_ref[...]).astype(BF16)
    half = dot_t(query, key) * (0.5 / math.sqrt(chan))
    weight = (half * jnp.tanh(half) + half).astype(BF16).astype(F32) * live
    mix[:chan] = wv_ref[...]
    mix[chan : chan + S] = (dot(weight.astype(BF16), value) / math.sqrt(S)).astype(BF16)
    mix[chan + S :] = jnp.zeros((chan - S, chan), BF16)

    def send(r):
        return pltpu.make_async_copy(rows_out.at[r], out_ref.at[r], sems.at[r])

    for r in range(cx):
        rows_out[r] = dot(o_ref[r], mix[...]).astype(BF16)
        send(r).start()
    for r in range(cx):
        send(r).wait()


def final(nx, ny, blocks, readers, w_cquery, w_ckey, w_cvalue, w_value, out):
    cx, span, wide = out.shape
    chan = wide // 2
    return pl.pallas_call(
        functools.partial(final_kernel, nx, ny, len(blocks)),
        in_specs=[IN_VMEM] * (len(blocks) + 6),
        out_specs=IN_HBM,
        out_shape=jax.ShapeDtypeStruct((cx, span, chan), BF16),
        scratch_shapes=[
            pltpu.VMEM((2 * chan, chan), BF16),
            pltpu.VMEM((cx, span, chan), BF16),
            pltpu.SemaphoreType.DMA((cx,)),
        ],
        compiler_params=params(16),
        name="final",
    )(*blocks, readers.T, w_cquery, w_ckey, w_cvalue, w_value, out)


def swap(array, axis, bits):
    return lax.ppermute(array, axis, [(i, i ^ bits) for i in range(lax.axis_size(axis))])


def join_kernel(count, *refs):
    parts, out = refs[:count], refs[-1]
    at = 0
    for part in parts:
        out[at : at + part.shape[0]] = part[...]
        at += part.shape[0]


def join(parts, ties):
    rows = sum(part.shape[0] for part in parts)
    return pl.pallas_call(
        functools.partial(join_kernel, len(parts)),
        in_specs=[IN_VMEM] * len(parts) + [pl.BlockSpec(memory_space=pl.ANY)] * len(ties),
        out_specs=IN_VMEM,
        out_shape=pltpu.VMEM((rows, parts[0].shape[1]), BF16),
        compiler_params=params(4),
        name="join",
    )(*parts, *ties)


def edge_rows_kernel(tile, fv_ref, paired_ref, other_ref, *rest):
    left_ref, right_ref, inward_ref, outward_ref = rest[-4:]
    rows, span, _ = fv_ref.shape

    @pl.when(lax.axis_index("gy") % 2 == 1)
    def _():
        left_ref[...] = paired_ref[...]
        right_ref[...] = other_ref[...]

    @pl.when(lax.axis_index("gy") % 2 == 0)
    def _():
        left_ref[...] = other_ref[...]
        right_ref[...] = paired_ref[...]

    odd = lax.axis_index("gx") % 2
    for ref, low in ((inward_ref, odd), (outward_ref, 1 - odd)):
        r = (1 - low) * (rows - 1)
        corner = pl.ds(pl.multiple_of(tile * r, tile), tile)
        ref[:tile] = left_ref[corner]
        ref[tile : tile + span] = fv_ref[r]
        ref[tile + span :] = right_ref[corner]


def edge_rows(tile, fv, paired_column, other_column, ties):
    rows, span, chan = fv.shape
    column = pltpu.VMEM((rows * tile, chan), BF16)
    edge = pltpu.VMEM((span + 2 * tile, chan), BF16)
    return pl.pallas_call(
        functools.partial(edge_rows_kernel, tile),
        in_specs=[IN_VMEM] * 3 + [pl.BlockSpec(memory_space=pl.ANY)] * len(ties),
        out_specs=[IN_VMEM] * 4,
        out_shape=[column, column, edge, edge],
        compiler_params=params(4),
        name="edge_rows",
    )(fv, paired_column, other_column, *ties)


def swap_across(array, axis, nx, ny):
    moves = []
    for x in range(nx):
        for y in range(ny):
            if axis == "gx":
                near = x + 1 if x % 2 else x - 1
                there = near * ny + y if 0 <= near < nx else x * ny + (y ^ 1)
            else:
                near = y + 1 if y % 2 else y - 1
                there = x * ny + near if 0 <= near < ny else (x ^ 1) * ny + y
            moves.append((x * ny + y, there))
    return lax.ppermute(array, ("gx", "gy"), moves)


def per_device(features, tile_mask, pool_map, readers, w_query, w_key, w_value, w_cquery, w_ckey, w_cvalue):
    cx, cy, tile, chan = features.shape
    nx, ny = lax.axis_size("gx"), lax.axis_size("gy")
    *base, pooled, inward, outward = pool(nx, ny, features, tile_mask, pool_map, w_query, w_key)
    fv = base[0]
    cuts = [1] + [1 + (cx - 2) * part // 14 for part in CUTS] + [cx - 1]
    rows = [range(lo, hi) for lo, hi in zip(cuts, cuts[1:])]
    steps = [("gx", 1 << b) for b in range(nx.bit_length() - 1)]
    steps += [("gy", 1 << b) for b in range(1, ny.bit_length() - 1)] + [("gy", 1)]
    paired_column = swap(inward, "gy", 1)
    other_column = swap_across(outward, "gy", nx, ny)
    out, first, ties = None, pooled, (pooled,)
    for step, (axis, bit) in enumerate(steps):
        second = swap(first, axis, bit)
        if step == 2:
            left, right, inward, outward = edge_rows(tile, fv, paired_column, other_column, (out, first))
            paired_row = swap(inward, "gx", 1)
            other_row = swap_across(outward, "gx", nx, ny)
            ties += (inward,)
        if step == len(steps) - 1:
            break
        if step < len(rows) - 1:
            kernel = functools.partial(inner_kernel, rows[step])
            out = piece(kernel, len(rows[step]), f"inner_{step}", base, out, (), ties)
        first = join((first, second), (out,))
        ties = (first,)
    out = piece(functools.partial(sides_kernel, rows[-1]), len(rows[-1]) + 3.5, "sides", base, out, (left, right), ties)
    out = piece(ends_kernel, 2, "ends", base, out, (left, right, paired_row, other_row), (), [pltpu.VMEM(inward.shape, BF16)] * 2)
    update = final(nx, ny, (first, second), readers, w_cquery, w_ckey, w_cvalue, w_value, out)
    return update.reshape(features.shape)


def solution(mesh):
    in_specs = (P("gx", "gy", None, None), P("gx", "gy", None), P("gx", "gy", None)) + (P(),) * 7
    return jax.shard_map(
        per_device, mesh=mesh, in_specs=in_specs, out_specs=P("gx", "gy", None, None), check_vma=False
    )
```

```python
import functools
import math

import jax
import jax.numpy as jnp
from jax import lax
from jax.experimental import pallas as pl
from jax.experimental.pallas import tpu as pltpu
from jax.sharding import PartitionSpec as P

BF16 = jnp.bfloat16
F32 = jnp.float32
S = 64
DEPTH = 2
CUTS = (3, 6, 9, 12)
IN_VMEM = pl.BlockSpec(memory_space=pltpu.VMEM)
IN_HBM = pl.BlockSpec(memory_space=pltpu.HBM)


def dot(a, b):
    return jnp.dot(a, b, preferred_element_type=F32)


def dot_t(a, b):
    return lax.dot_general(a, b, (((1,), (1,)), ((), ())), preferred_element_type=F32)


def t_dot(a, b):
    return lax.dot_general(a, b, (((0,), (0,)), ((), ())), preferred_element_type=F32)


def in_hbm(array):
    return pltpu.with_memory_space_constraint(array, pltpu.HBM)


def params(mib):
    return pltpu.CompilerParams(vmem_limit_bytes=mib * 1024 * 1024)


def paired(ids):
    half = ids.shape[0] // 2
    return jnp.concatenate([ids[:half], ids[half:]], axis=1)


def pool_kernel(tile, nx, ny, f_ref, pm_ref, tm_ref, wq_ref, wk_ref, fv_ref, pv_ref, mv_ref, m_ref, pooled_ref, inward_ref, outward_ref, tv, wq, wk, sems):
    rows, span, chan = fv_ref.shape
    cy = span // tile
    small = [(tm_ref, tv), (wq_ref, wq), (wk_ref, wk), (pm_ref, pv_ref)]
    first = [pltpu.make_async_copy(src, dst, sems.at[rows + i]) for i, (src, dst) in enumerate(small)]
    beads_in = [pltpu.make_async_copy(f_ref.at[r], fv_ref.at[r], sems.at[r]) for r in range(rows)]
    for copy in first + beads_in:
        copy.start()
    block = lax.broadcasted_iota(jnp.int32, (18, 12 * tile), 1) // tile
    which = lax.broadcasted_iota(jnp.int32, (18, 12 * tile), 0)
    offset, second = which % 9, which // 9
    hit = (offset // 3 == block // 4) & (offset % 3 == block % 4 - second)
    pick = jnp.where(hit, 1 / math.sqrt(tile), 0.0).astype(BF16)
    for copy in first:
        copy.wait()
    m_ref[...] = (dot_t(wq[...], wk[...]) * (0.5 / math.sqrt(chan))).astype(BF16)
    mask = jnp.concatenate([tv[pl.ds(r, 9, stride=rows), :].astype(F32) for r in range(rows)], axis=1)
    lane = lax.broadcasted_iota(jnp.int32, mask.shape, 1)
    toward = lax.broadcasted_iota(jnp.int32, mask.shape, 0)
    mx, my = lax.axis_index("gx"), lax.axis_index("gy")
    outside = (toward // 3 == 0) & (lane // cy == jnp.where(mx == 0, 0, -1))
    outside |= (toward // 3 == 2) & (lane // cy == jnp.where(mx == nx - 1, rows - 1, -1))
    outside |= (toward % 3 == 0) & (lane % cy == jnp.where(my == 0, 0, -1))
    outside |= (toward % 3 == 2) & (lane % cy == jnp.where(my == ny - 1, cy - 1, -1))
    mask = jnp.where(outside, 0.0, mask)
    even = lane % 2 == 0
    both = jnp.concatenate([jnp.where(even, mask, 0.0), jnp.where(even, 0.0, mask)], axis=0)
    mv_ref[...] = t_dot(both.astype(BF16), pick)

    node = lax.broadcasted_iota(jnp.int32, (S, 2 * tile), 0)
    order = [c for i in range(cy // 2) for c in (i, i + cy // 2)]
    total = jnp.zeros((S, chan), F32)
    for low in range(0, rows, 8):
        group = range(low, min(low + 8, rows))
        hot, beads = [], []
        for r in group:
            pairs = paired(pv_ref[r])
            hot += [
                (jnp.broadcast_to(pairs[i : i + 1], node.shape) == node).astype(F32).astype(BF16) for i in range(cy // 2)
            ]
        for r in group:
            beads_in[r].wait()
        for r in group:
            beads += [fv_ref[r, tile * c : tile * (c + 1)] for c in order]
        total += dot(jnp.concatenate(hot, axis=1), jnp.concatenate(beads, axis=0))
        for r in group:
            for ref, low_side in ((inward_ref, my % 2), (outward_ref, 1 - my % 2)):
                column = pl.ds(pl.multiple_of((1 - low_side) * (span - tile), tile), tile)
                ref[tile * r : tile * (r + 1)] = fv_ref[r, column]
    pooled = (total * math.sqrt(S / (rows * span))).astype(BF16)
    pooled_ref[...] = pooled
    inward_ref[tile * rows :] = pooled


def pool(nx, ny, features, tile_mask, pool_map, w_query, w_key):
    cx, cy, tile, chan = features.shape
    span = cy * tile
    return pl.pallas_call(
        functools.partial(pool_kernel, tile, nx, ny),
        in_specs=[IN_HBM] * 5,
        out_specs=[IN_VMEM] * 7,
        out_shape=[
            pltpu.VMEM((cx, span, chan), BF16),
            pltpu.VMEM((cx, cy, tile), jnp.int32),
            pltpu.VMEM((cx * cy, 12 * tile), F32),
            pltpu.VMEM((chan, chan), BF16),
            pltpu.VMEM((S, chan), BF16),
            pltpu.VMEM((cx * tile + S, chan), BF16),
            pltpu.VMEM((cx * tile, chan), BF16),
        ],
        scratch_shapes=[
            pltpu.VMEM((9 * cx, cy), jnp.int32),
            pltpu.VMEM((chan, chan), BF16),
            pltpu.VMEM((chan, chan), BF16),
            pltpu.SemaphoreType.DMA((cx + 4,)),
        ],
        compiler_params=params(16),
        name="pool",
    )(
        in_hbm(features.reshape(cx, span, chan)),
        in_hbm(pool_map),
        in_hbm(jnp.transpose(tile_mask, (2, 0, 1)).reshape(9 * cx, cy)),
        in_hbm(w_query),
        in_hbm(w_key),
    )


def attend(tile, tasks):
    waiting = []

    def finish(task, weights):
        _, windows, _, store = task
        near = jnp.concatenate([window() for window in windows], axis=0)
        store(dot(jnp.concatenate(weights, axis=1), near).astype(BF16))

    for task in tasks:
        query, windows, masks, _ = task
        weights = []
        for r, window in enumerate(windows):
            half = dot_t(query, window())
            lanes = slice(4 * tile * r, 4 * tile * (r + 1))
            mask = jnp.concatenate([jnp.broadcast_to(masks(h, lanes), (tile, 4 * tile)) for h in (0, 1)], axis=0)
            weights.append((half * jnp.tanh(half) + half).astype(BF16) * mask.astype(BF16))
        waiting.append((task, weights))
        if len(waiting) > DEPTH:
            finish(*waiting.pop(0))
    while waiting:
        finish(*waiting.pop(0))


def row_tasks(refs, row, first, last, window):
    fv, pv, mv, m, o = refs
    chan = fv.shape[2]
    cy, tile = pv.shape[1:]
    side = 2 * tile
    queries = dot(fv[row, side * first : side * last], m[...]).astype(BF16)
    tasks = []
    for j in range(first, last):

        def store(value, lo=side * j):
            o[row, lo : lo + side, :chan] = value

        tasks.append((
            queries[side * (j - first) : side * (j - first + 1)],
            [functools.partial(window, r, j) for r in (row - 1, row, row + 1)],
            lambda h, lanes, lo=row * cy + 2 * j: mv[lo + h : lo + h + 1, lanes],
            store,
        ))
    return tasks


def node_rows(refs, row):
    fv, pv, _, _, o = refs
    _, span, chan = fv.shape
    cy, tile = pv.shape[1:]
    pairs = paired(pv[row])
    node = lax.broadcasted_iota(jnp.int32, (chan, 2 * tile), 0)
    for i in range(cy // 2):
        turned = (jnp.broadcast_to(pairs[i : i + 1], node.shape) == node).astype(F32).T.astype(BF16)
        o[row, tile * i : tile * (i + 1), chan:] = turned[:tile]
        o[row, span // 2 + tile * i : span // 2 + tile * (i + 1), chan:] = turned[tile:]


def inner_tasks(refs, rows):
    fv, pv = refs[:2]
    cy, tile = pv.shape[1:]

    def window(r, j):
        return fv[r, tile * (2 * j - 1) : tile * (2 * j + 3)]

    tasks = []
    for row in rows:
        node_rows(refs, row)
        tasks += row_tasks(refs, row, 1, cy // 2 - 1, window)
    return tasks


def inner_kernel(rows, fv, pv, mv, m, *rest):
    attend(pv.shape[2], inner_tasks((fv, pv, mv, m, rest[-1]), rows))


def side_window(fv, tile, left, right):
    span = fv.shape[1]

    def window(r, j):
        if j == 0:
            return jnp.concatenate([left[tile * r : tile * (r + 1)], fv[r, : 3 * tile]], axis=0)
        if 2 * tile * (j + 1) == span:
            return jnp.concatenate([fv[r, span - 3 * tile :], right[tile * r : tile * (r + 1)]], axis=0)
        return fv[r, tile * (2 * j - 1) : tile * (2 * j + 3)]

    return window


def sides_kernel(rows, fv, pv, mv, m, out_in, left, right, *rest):
    cy, tile = pv.shape[1:]
    refs = (fv, pv, mv, m, rest[-1])
    window = side_window(fv, tile, left, right)
    tasks = inner_tasks(refs, rows)
    for row in range(1, fv.shape[0] - 1):
        for j in (0, cy // 2 - 1):
            tasks += row_tasks(refs, row, j, j + 1, window)
    attend(tile, tasks)


def ends_kernel(fv, pv, mv, m, out_in, left, right, paired_row, other_row, *rest):
    *_, o, above, below = rest
    cy, tile = pv.shape[1:]
    rows = fv.shape[0]
    refs = (fv, pv, mv, m, o)
    near = side_window(fv, tile, left, right)
    odd = lax.axis_index("gx") % 2 == 1

    @pl.when(odd)
    def _():
        above[...] = paired_row[...]
        below[...] = other_row[...]

    @pl.when(jnp.logical_not(odd))
    def _():
        above[...] = other_row[...]
        below[...] = paired_row[...]

    def window(r, j):
        if r in (-1, rows):
            return (above if r < 0 else below)[2 * tile * j : 2 * tile * (j + 2)]
        return near(r, j)

    tasks = []
    for row in (0, rows - 1):
        node_rows(refs, row)
        tasks += row_tasks(refs, row, 0, cy // 2, window)
    attend(tile, tasks)


def estimate(rows):
    return pl.CostEstimate(flops=int(rows * 400_000_000), bytes_accessed=1_000_000, transcendentals=0)


def piece(kernel, rows_done, name, base, out, near=(), ties=(), scratch=()):
    cx, span, chan = base[0].shape
    done = [] if out is None else [out]
    return pl.pallas_call(
        kernel,
        in_specs=[IN_VMEM] * (4 + len(done) + len(near)) + [pl.BlockSpec(memory_space=pl.ANY)] * len(ties),
        out_specs=IN_VMEM,
        out_shape=pltpu.VMEM((cx, span, 2 * chan), BF16),
        scratch_shapes=list(scratch),
        input_output_aliases={4: 0} if done else {},
        compiler_params=params(16),
        cost_estimate=estimate(rows_done),
        name=name,
    )(*base, *done, *near, *ties)


def final_kernel(nx, ny, n_blocks, *refs):
    blocks = refs[:n_blocks]
    readers_ref, wcq_ref, wck_ref, wcv_ref, wv_ref, o_ref, out_ref, mix, rows_out, sems = refs[n_blocks:]
    cx, span, chan = rows_out.shape
    nodes = jnp.concatenate([ref[...] for ref in blocks], axis=0)
    count = nodes.shape[0]
    mx, my = lax.axis_index("gx"), lax.axis_index("gy")
    block = lax.broadcasted_iota(jnp.int32, (readers_ref.shape[0], count), 1) // S
    turn = block // (2 * nx) * 2 + block % 2
    domain = ((block // 2 % nx) ^ mx) * ny + (turn ^ my)
    lane = lax.broadcasted_iota(jnp.int32, readers_ref.shape, 1)
    mine = jnp.sum(jnp.where(lane == mx * ny + my, readers_ref[...], 0), axis=1, keepdims=True)
    live = jnp.sum(jnp.where(domain == mine, 1.0, 0.0), axis=0, keepdims=True)
    query = dot(nodes[:S], wcq_ref[...]).astype(BF16)
    key = dot(nodes, wck_ref[...]).astype(BF16)
    value = dot(nodes, wcv_ref[...]).astype(BF16)
    half = dot_t(query, key) * (0.5 / math.sqrt(chan))
    weight = (half * jnp.tanh(half) + half).astype(BF16).astype(F32) * live
    mix[:chan] = wv_ref[...]
    mix[chan : chan + S] = (dot(weight.astype(BF16), value) / math.sqrt(S)).astype(BF16)
    mix[chan + S :] = jnp.zeros((chan - S, chan), BF16)

    def send(r):
        return pltpu.make_async_copy(rows_out.at[r], out_ref.at[r], sems.at[r])

    for r in range(cx):
        rows_out[r] = dot(o_ref[r], mix[...]).astype(BF16)
        send(r).start()
    for r in range(cx):
        send(r).wait()


def final(nx, ny, blocks, readers, w_cquery, w_ckey, w_cvalue, w_value, out):
    cx, span, wide = out.shape
    chan = wide // 2
    return pl.pallas_call(
        functools.partial(final_kernel, nx, ny, len(blocks)),
        in_specs=[IN_VMEM] * (len(blocks) + 6),
        out_specs=IN_HBM,
        out_shape=jax.ShapeDtypeStruct((cx, span, chan), BF16),
        scratch_shapes=[
            pltpu.VMEM((2 * chan, chan), BF16),
            pltpu.VMEM((cx, span, chan), BF16),
            pltpu.SemaphoreType.DMA((cx,)),
        ],
        compiler_params=params(16),
        name="final",
    )(*blocks, readers.T, w_cquery, w_ckey, w_cvalue, w_value, out)


def swap(array, axis, bits):
    return lax.ppermute(array, axis, [(i, i ^ bits) for i in range(lax.axis_size(axis))])


def join_kernel(size, *refs):
    first_ref, second_ref, *_, out_ref = refs
    out_ref[:size] = first_ref[...]
    out_ref[size:] = second_ref[second_ref.shape[0] - size :]


def join(first, second, ties):
    size, chan = first.shape
    return pl.pallas_call(
        functools.partial(join_kernel, size),
        in_specs=[IN_VMEM] * 2 + [pl.BlockSpec(memory_space=pl.ANY)] * len(ties),
        out_specs=IN_VMEM,
        out_shape=pltpu.VMEM((2 * size, chan), BF16),
        compiler_params=params(4),
        name="join",
    )(first, second, *ties)


def edge_rows_kernel(tile, fv_ref, paired_ref, other_ref, *rest):
    left_ref, right_ref, inward_ref, outward_ref = rest[-4:]
    rows, span, _ = fv_ref.shape

    @pl.when(lax.axis_index("gy") % 2 == 1)
    def _():
        left_ref[...] = paired_ref[: rows * tile]
        right_ref[...] = other_ref[...]

    @pl.when(lax.axis_index("gy") % 2 == 0)
    def _():
        left_ref[...] = other_ref[...]
        right_ref[...] = paired_ref[: rows * tile]

    odd = lax.axis_index("gx") % 2
    for ref, low in ((inward_ref, odd), (outward_ref, 1 - odd)):
        r = (1 - low) * (rows - 1)
        corner = pl.ds(pl.multiple_of(tile * r, tile), tile)
        ref[:tile] = left_ref[corner]
        ref[tile : tile + span] = fv_ref[r]
        ref[tile + span :] = right_ref[corner]


def edge_rows(tile, fv, paired_column, other_column, ties):
    rows, span, chan = fv.shape
    column = pltpu.VMEM((rows * tile, chan), BF16)
    edge = pltpu.VMEM((span + 2 * tile, chan), BF16)
    return pl.pallas_call(
        functools.partial(edge_rows_kernel, tile),
        in_specs=[IN_VMEM] * 3 + [pl.BlockSpec(memory_space=pl.ANY)] * len(ties),
        out_specs=[IN_VMEM] * 4,
        out_shape=[column, column, edge, edge],
        compiler_params=params(4),
        name="edge_rows",
    )(fv, paired_column, other_column, *ties)


def swap_across(array, axis, nx, ny):
    moves = []
    for x in range(nx):
        for y in range(ny):
            if axis == "gx":
                near = x + 1 if x % 2 else x - 1
                there = near * ny + y if 0 <= near < nx else x * ny + (y ^ 1)
            else:
                near = y + 1 if y % 2 else y - 1
                there = x * ny + near if 0 <= near < ny else (x ^ 1) * ny + y
            moves.append((x * ny + y, there))
    return lax.ppermute(array, ("gx", "gy"), moves)


def per_device(features, tile_mask, pool_map, readers, w_query, w_key, w_value, w_cquery, w_ckey, w_cvalue):
    cx, cy, tile, chan = features.shape
    nx, ny = lax.axis_size("gx"), lax.axis_size("gy")
    *base, pooled, inward, outward = pool(nx, ny, features, tile_mask, pool_map, w_query, w_key)
    fv = base[0]
    cuts = [1] + [1 + (cx - 2) * part // 14 for part in CUTS] + [cx - 1]
    rows = [range(lo, hi) for lo, hi in zip(cuts, cuts[1:])]
    steps = [("gx", 1 << b) for b in range(nx.bit_length() - 1)]
    steps += [("gy", 1 << b) for b in range(1, ny.bit_length() - 1)]
    paired_column = swap(inward, "gy", 1)
    other_column = swap_across(outward, "gy", nx, ny)
    out = piece(functools.partial(inner_kernel, rows[0]), len(rows[0]), "inner_0", base, None, (), (pooled,))
    first = join(pooled, paired_column, (out,))
    ties = (first,)
    for step, (axis, bit) in enumerate(steps):
        second = swap(first, axis, bit)
        if step == 2:
            left, right, inward, outward = edge_rows(tile, fv, paired_column, other_column, (out, first))
            paired_row = swap(inward, "gx", 1)
            other_row = swap_across(outward, "gx", nx, ny)
            ties += (inward,)
        if step == len(steps) - 1:
            break
        if step + 1 < len(rows) - 1:
            kernel = functools.partial(inner_kernel, rows[step + 1])
            out = piece(kernel, len(rows[step + 1]), f"inner_{step + 1}", base, out, (), ties)
        first = join(first, second, (out,))
        ties = (first,)
    out = piece(functools.partial(sides_kernel, rows[-1]), len(rows[-1]) + 3.5, "sides", base, out, (left, right), ties)
    out = piece(ends_kernel, 2, "ends", base, out, (left, right, paired_row, other_row), (), [pltpu.VMEM(inward.shape, BF16)] * 2)
    update = final(nx, ny, (first, second), readers, w_cquery, w_ckey, w_cvalue, w_value, out)
    return update.reshape(features.shape)


def solution(mesh):
    in_specs = (P("gx", "gy", None, None), P("gx", "gy", None), P("gx", "gy", None)) + (P(),) * 7
    return jax.shard_map(
        per_device, mesh=mesh, in_specs=in_specs, out_specs=P("gx", "gy", None, None), check_vma=False
    )
```

```python
import functools
import math

import jax
import jax.numpy as jnp
from jax import lax
from jax.experimental import pallas as pl
from jax.experimental.pallas import tpu as pltpu
from jax.sharding import PartitionSpec as P

BF16 = jnp.bfloat16
F32 = jnp.float32
S = 64
DEPTH = 2
CUTS = (4, 7, 10, 14)
IN_VMEM = pl.BlockSpec(memory_space=pltpu.VMEM)
IN_HBM = pl.BlockSpec(memory_space=pltpu.HBM)


def dot(a, b):
    return jnp.dot(a, b, preferred_element_type=F32)


def dot_t(a, b):
    return lax.dot_general(a, b, (((1,), (1,)), ((), ())), preferred_element_type=F32)


def t_dot(a, b):
    return lax.dot_general(a, b, (((0,), (0,)), ((), ())), preferred_element_type=F32)


def in_hbm(array):
    return pltpu.with_memory_space_constraint(array, pltpu.HBM)


def params(mib):
    return pltpu.CompilerParams(vmem_limit_bytes=mib * 1024 * 1024)


def paired(ids):
    half = ids.shape[0] // 2
    return jnp.concatenate([ids[:half], ids[half:]], axis=1)


def pool_kernel(tile, nx, ny, f_ref, pm_ref, tm_ref, wq_ref, wk_ref, fv_ref, pv_ref, mv_ref, m_ref, pooled_ref, inward_ref, outward_ref, tv, wq, wk, sems):
    rows, span, chan = fv_ref.shape
    cy = span // tile
    small = [(tm_ref, tv), (wq_ref, wq), (wk_ref, wk), (pm_ref, pv_ref)]
    first = [pltpu.make_async_copy(src, dst, sems.at[rows + i]) for i, (src, dst) in enumerate(small)]
    beads_in = [pltpu.make_async_copy(f_ref.at[r], fv_ref.at[r], sems.at[r]) for r in range(rows)]
    for copy in first + beads_in:
        copy.start()
    block = lax.broadcasted_iota(jnp.int32, (18, 12 * tile), 1) // tile
    which = lax.broadcasted_iota(jnp.int32, (18, 12 * tile), 0)
    offset, second = which % 9, which // 9
    hit = (offset // 3 == block // 4) & (offset % 3 == block % 4 - second)
    pick = jnp.where(hit, 1 / math.sqrt(tile), 0.0).astype(BF16)
    for copy in first:
        copy.wait()
    m_ref[...] = (dot_t(wq[...], wk[...]) * (0.5 / math.sqrt(chan))).astype(BF16)
    mask = jnp.concatenate([tv[pl.ds(r, 9, stride=rows), :].astype(F32) for r in range(rows)], axis=1)
    lane = lax.broadcasted_iota(jnp.int32, mask.shape, 1)
    toward = lax.broadcasted_iota(jnp.int32, mask.shape, 0)
    mx, my = lax.axis_index("gx"), lax.axis_index("gy")
    outside = (toward // 3 == 0) & (lane // cy == jnp.where(mx == 0, 0, -1))
    outside |= (toward // 3 == 2) & (lane // cy == jnp.where(mx == nx - 1, rows - 1, -1))
    outside |= (toward % 3 == 0) & (lane % cy == jnp.where(my == 0, 0, -1))
    outside |= (toward % 3 == 2) & (lane % cy == jnp.where(my == ny - 1, cy - 1, -1))
    mask = jnp.where(outside, 0.0, mask)
    even = lane % 2 == 0
    both = jnp.concatenate([jnp.where(even, mask, 0.0), jnp.where(even, 0.0, mask)], axis=0)
    mv_ref[...] = t_dot(both.astype(BF16), pick)

    node = lax.broadcasted_iota(jnp.int32, (S, 2 * tile), 0)
    order = [c for i in range(cy // 2) for c in (i, i + cy // 2)]
    total = jnp.zeros((S, chan), F32)
    for low in range(0, rows, 8):
        group = range(low, min(low + 8, rows))
        hot, beads = [], []
        for r in group:
            pairs = paired(pv_ref[r])
            hot += [
                (jnp.broadcast_to(pairs[i : i + 1], node.shape) == node).astype(F32).astype(BF16) for i in range(cy // 2)
            ]
        for r in group:
            beads_in[r].wait()
        for r in group:
            beads += [fv_ref[r, tile * c : tile * (c + 1)] for c in order]
        total += dot(jnp.concatenate(hot, axis=1), jnp.concatenate(beads, axis=0))
        for r in group:
            for ref, low_side in ((inward_ref, my % 2), (outward_ref, 1 - my % 2)):
                column = pl.ds(pl.multiple_of((1 - low_side) * (span - tile), tile), tile)
                ref[tile * r : tile * (r + 1)] = fv_ref[r, column]
    pooled_ref[...] = (total * math.sqrt(S / (rows * span))).astype(BF16)


def pool(nx, ny, features, tile_mask, pool_map, w_query, w_key):
    cx, cy, tile, chan = features.shape
    span = cy * tile
    edge = pltpu.VMEM((cx * tile, chan), BF16)
    return pl.pallas_call(
        functools.partial(pool_kernel, tile, nx, ny),
        in_specs=[IN_HBM] * 5,
        out_specs=[IN_VMEM] * 7,
        out_shape=[
            pltpu.VMEM((cx, span, chan), BF16),
            pltpu.VMEM((cx, cy, tile), jnp.int32),
            pltpu.VMEM((cx * cy, 12 * tile), F32),
            pltpu.VMEM((chan, chan), BF16),
            pltpu.VMEM((S, chan), BF16),
            edge,
            edge,
        ],
        scratch_shapes=[
            pltpu.VMEM((9 * cx, cy), jnp.int32),
            pltpu.VMEM((chan, chan), BF16),
            pltpu.VMEM((chan, chan), BF16),
            pltpu.SemaphoreType.DMA((cx + 4,)),
        ],
        compiler_params=params(16),
        name="pool",
    )(
        in_hbm(features.reshape(cx, span, chan)),
        in_hbm(pool_map),
        in_hbm(jnp.transpose(tile_mask, (2, 0, 1)).reshape(9 * cx, cy)),
        in_hbm(w_query),
        in_hbm(w_key),
    )


def attend(tile, tasks):
    waiting = []

    def finish(task, weights):
        _, windows, _, store = task
        near = jnp.concatenate([window() for window in windows], axis=0)
        store(dot(jnp.concatenate(weights, axis=1), near).astype(BF16))

    for task in tasks:
        query, windows, masks, _ = task
        weights = []
        for r, window in enumerate(windows):
            half = dot_t(query, window())
            lanes = slice(4 * tile * r, 4 * tile * (r + 1))
            mask = jnp.concatenate([jnp.broadcast_to(masks(h, lanes), (tile, 4 * tile)) for h in (0, 1)], axis=0)
            weights.append((half * jnp.tanh(half) + half).astype(BF16) * mask.astype(BF16))
        waiting.append((task, weights))
        if len(waiting) > DEPTH:
            finish(*waiting.pop(0))
    while waiting:
        finish(*waiting.pop(0))


def row_tasks(refs, row, first, last, window):
    fv, pv, mv, m, o = refs
    chan = fv.shape[2]
    cy, tile = pv.shape[1:]
    side = 2 * tile
    queries = dot(fv[row, side * first : side * last], m[...]).astype(BF16)
    tasks = []
    for j in range(first, last):

        def store(value, lo=side * j):
            o[row, lo : lo + side, :chan] = value

        tasks.append((
            queries[side * (j - first) : side * (j - first + 1)],
            [functools.partial(window, r, j) for r in (row - 1, row, row + 1)],
            lambda h, lanes, lo=row * cy + 2 * j: mv[lo + h : lo + h + 1, lanes],
            store,
        ))
    return tasks


def node_rows(refs, row):
    fv, pv, _, _, o = refs
    _, span, chan = fv.shape
    cy, tile = pv.shape[1:]
    pairs = paired(pv[row])
    node = lax.broadcasted_iota(jnp.int32, (chan, 2 * tile), 0)
    for i in range(cy // 2):
        turned = (jnp.broadcast_to(pairs[i : i + 1], node.shape) == node).astype(F32).T.astype(BF16)
        o[row, tile * i : tile * (i + 1), chan:] = turned[:tile]
        o[row, span // 2 + tile * i : span // 2 + tile * (i + 1), chan:] = turned[tile:]


def inner_tasks(refs, rows):
    fv, pv = refs[:2]
    cy, tile = pv.shape[1:]

    def window(r, j):
        return fv[r, tile * (2 * j - 1) : tile * (2 * j + 3)]

    tasks = []
    for row in rows:
        node_rows(refs, row)
        tasks += row_tasks(refs, row, 1, cy // 2 - 1, window)
    return tasks


def inner_kernel(rows, fv, pv, mv, m, *rest):
    attend(pv.shape[2], inner_tasks((fv, pv, mv, m, rest[-1]), rows))


def side_window(fv, tile, left, right):
    span = fv.shape[1]

    def window(r, j):
        if j == 0:
            return jnp.concatenate([left[tile * r : tile * (r + 1)], fv[r, : 3 * tile]], axis=0)
        if 2 * tile * (j + 1) == span:
            return jnp.concatenate([fv[r, span - 3 * tile :], right[tile * r : tile * (r + 1)]], axis=0)
        return fv[r, tile * (2 * j - 1) : tile * (2 * j + 3)]

    return window


def sides_kernel(rows, fv, pv, mv, m, out_in, left, right, *rest):
    cy, tile = pv.shape[1:]
    refs = (fv, pv, mv, m, rest[-1])
    window = side_window(fv, tile, left, right)
    tasks = inner_tasks(refs, rows)
    for row in range(1, fv.shape[0] - 1):
        for j in (0, cy // 2 - 1):
            tasks += row_tasks(refs, row, j, j + 1, window)
    attend(tile, tasks)


def ends_kernel(nx, ny, fv, pv, mv, m, out_in, left, right, paired_row, other_row, *rest):
    first, second, *weights, o, mix, above, below = rest
    cy, tile = pv.shape[1:]
    rows = fv.shape[0]
    refs = (fv, pv, mv, m, o)
    near = side_window(fv, tile, left, right)
    odd = lax.axis_index("gx") % 2 == 1

    @pl.when(odd)
    def _():
        above[...] = paired_row[...]
        below[...] = other_row[...]

    @pl.when(jnp.logical_not(odd))
    def _():
        above[...] = other_row[...]
        below[...] = paired_row[...]

    def window(r, j):
        if r in (-1, rows):
            return (above if r < 0 else below)[2 * tile * j : 2 * tile * (j + 2)]
        return near(r, j)

    coarse(nx, ny, (first, second), *weights, mix)
    tasks = []
    for row in (0, rows - 1):
        node_rows(refs, row)
        tasks += row_tasks(refs, row, 0, cy // 2, window)
    attend(tile, tasks)


def estimate(rows):
    return pl.CostEstimate(flops=int(rows * 400_000_000), bytes_accessed=1_000_000, transcendentals=0)


def piece(kernel, rows_done, name, base, out, near=(), ties=()):
    cx, span, chan = base[0].shape
    done = [] if out is None else [out]
    return pl.pallas_call(
        kernel,
        in_specs=[IN_VMEM] * (4 + len(done) + len(near)) + [pl.BlockSpec(memory_space=pl.ANY)] * len(ties),
        out_specs=IN_VMEM,
        out_shape=pltpu.VMEM((cx, span, 2 * chan), BF16),
        input_output_aliases={4: 0} if done else {},
        compiler_params=params(16),
        cost_estimate=estimate(rows_done),
        name=name,
    )(*base, *done, *near, *ties)


def coarse(nx, ny, blocks, readers_ref, wcq_ref, wck_ref, wcv_ref, wv_ref, mix):
    nodes = jnp.concatenate([ref[...] for ref in blocks], axis=0)
    count, chan = nodes.shape
    mx, my = lax.axis_index("gx"), lax.axis_index("gy")
    block = lax.broadcasted_iota(jnp.int32, (readers_ref.shape[0], count), 1) // S
    rest = block // nx
    turn = (rest % (ny // 2)) * 2 + rest // (ny // 2)
    domain = ((block % nx) ^ mx) * ny + (turn ^ my)
    lane = lax.broadcasted_iota(jnp.int32, readers_ref.shape, 1)
    mine = jnp.sum(jnp.where(lane == mx * ny + my, readers_ref[...], 0), axis=1, keepdims=True)
    live = jnp.sum(jnp.where(domain == mine, 1.0, 0.0), axis=0, keepdims=True)
    query = dot(nodes[:S], wcq_ref[...]).astype(BF16)
    key = dot(nodes, wck_ref[...]).astype(BF16)
    value = dot(nodes, wcv_ref[...]).astype(BF16)
    half = dot_t(query, key) * (0.5 / math.sqrt(chan))
    weight = (half * jnp.tanh(half) + half).astype(BF16).astype(F32) * live
    mix[:chan] = wv_ref[...]
    mix[chan : chan + S] = (dot(weight.astype(BF16), value) / math.sqrt(S)).astype(BF16)
    mix[chan + S :] = jnp.zeros((chan - S, chan), BF16)


def ends(nx, ny, base, out, halos, blocks, readers, w_cquery, w_ckey, w_cvalue, w_value):
    chan = base[0].shape[2]
    operands = (*base, out, *halos, *blocks, readers.T, w_cquery, w_ckey, w_cvalue, w_value)
    return pl.pallas_call(
        functools.partial(ends_kernel, nx, ny),
        in_specs=[IN_VMEM] * len(operands),
        out_specs=[IN_VMEM] * 2,
        out_shape=[pltpu.VMEM(out.shape, BF16), pltpu.VMEM((2 * chan, chan), BF16)],
        scratch_shapes=[pltpu.VMEM(halos[-1].shape, BF16)] * 2,
        input_output_aliases={4: 0},
        compiler_params=params(16),
        cost_estimate=estimate(2),
        name="ends",
    )(*operands)


def final_kernel(o_ref, mix, out_ref, rows_out, sems):
    rows = rows_out.shape[0]

    def send(r):
        return pltpu.make_async_copy(rows_out.at[r], out_ref.at[r], sems.at[r])

    for r in range(rows):
        rows_out[r] = dot(o_ref[r], mix[...]).astype(BF16)
        send(r).start()
    for r in range(rows):
        send(r).wait()


def final(out, mix):
    cx, span, wide = out.shape
    chan = wide // 2
    return pl.pallas_call(
        final_kernel,
        in_specs=[IN_VMEM] * 2,
        out_specs=IN_HBM,
        out_shape=jax.ShapeDtypeStruct((cx, span, chan), BF16),
        scratch_shapes=[pltpu.VMEM((cx, span, chan), BF16), pltpu.SemaphoreType.DMA((cx,))],
        compiler_params=params(16),
        name="final",
    )(out, mix)


def swap(array, axis, bits):
    return lax.ppermute(array, axis, [(i, i ^ bits) for i in range(lax.axis_size(axis))])


def join_kernel(count, *refs):
    parts, out = refs[:count], refs[-1]
    at = 0
    for part in parts:
        out[at : at + part.shape[0]] = part[...]
        at += part.shape[0]


def join(parts, ties):
    rows = sum(part.shape[0] for part in parts)
    return pl.pallas_call(
        functools.partial(join_kernel, len(parts)),
        in_specs=[IN_VMEM] * len(parts) + [pl.BlockSpec(memory_space=pl.ANY)] * len(ties),
        out_specs=IN_VMEM,
        out_shape=pltpu.VMEM((rows, parts[0].shape[1]), BF16),
        compiler_params=params(4),
        name="join",
    )(*parts, *ties)


def edge_rows_kernel(tile, fv_ref, paired_ref, other_ref, *rest):
    left_ref, right_ref, inward_ref, outward_ref = rest[-4:]
    rows, span, _ = fv_ref.shape

    @pl.when(lax.axis_index("gy") % 2 == 1)
    def _():
        left_ref[...] = paired_ref[...]
        right_ref[...] = other_ref[...]

    @pl.when(lax.axis_index("gy") % 2 == 0)
    def _():
        left_ref[...] = other_ref[...]
        right_ref[...] = paired_ref[...]

    odd = lax.axis_index("gx") % 2
    for ref, low in ((inward_ref, odd), (outward_ref, 1 - odd)):
        r = (1 - low) * (rows - 1)
        corner = pl.ds(pl.multiple_of(tile * r, tile), tile)
        ref[:tile] = left_ref[corner]
        ref[tile : tile + span] = fv_ref[r]
        ref[tile + span :] = right_ref[corner]


def edge_rows(tile, fv, paired_column, other_column, ties):
    rows, span, chan = fv.shape
    column = pltpu.VMEM((rows * tile, chan), BF16)
    edge = pltpu.VMEM((span + 2 * tile, chan), BF16)
    return pl.pallas_call(
        functools.partial(edge_rows_kernel, tile),
        in_specs=[IN_VMEM] * 3 + [pl.BlockSpec(memory_space=pl.ANY)] * len(ties),
        out_specs=[IN_VMEM] * 4,
        out_shape=[column, column, edge, edge],
        compiler_params=params(4),
        name="edge_rows",
    )(fv, paired_column, other_column, *ties)


def swap_across(array, axis, nx, ny):
    moves = []
    for x in range(nx):
        for y in range(ny):
            if axis == "gx":
                near = x + 1 if x % 2 else x - 1
                there = near * ny + y if 0 <= near < nx else x * ny + (y ^ 1)
            else:
                near = y + 1 if y % 2 else y - 1
                there = x * ny + near if 0 <= near < ny else (x ^ 1) * ny + y
            moves.append((x * ny + y, there))
    return lax.ppermute(array, ("gx", "gy"), moves)


def per_device(features, tile_mask, pool_map, readers, w_query, w_key, w_value, w_cquery, w_ckey, w_cvalue):
    cx, cy, tile, chan = features.shape
    nx, ny = lax.axis_size("gx"), lax.axis_size("gy")
    *base, pooled, inward, outward = pool(nx, ny, features, tile_mask, pool_map, w_query, w_key)
    fv = base[0]
    cuts = [1] + [1 + (cx - 2) * part // 14 for part in CUTS] + [cx - 1]
    rows = [range(lo, hi) for lo, hi in zip(cuts, cuts[1:])]
    steps = [("gx", 1 << b) for b in range(nx.bit_length() - 1)]
    steps += [("gy", 1 << b) for b in range(1, ny.bit_length() - 1)] + [("gy", 1)]
    paired_column = swap(inward, "gy", 1)
    other_column = swap_across(outward, "gy", nx, ny)
    out, first, ties = None, pooled, (pooled,)
    for step, (axis, bit) in enumerate(steps):
        second = swap(first, axis, bit)
        if step == 2:
            left, right, inward, outward = edge_rows(tile, fv, paired_column, other_column, (out, first))
            paired_row = swap(inward, "gx", 1)
            other_row = swap_across(outward, "gx", nx, ny)
            ties += (inward,)
        if step == len(steps) - 1:
            break
        if step < len(rows) - 1:
            kernel = functools.partial(inner_kernel, rows[step])
            out = piece(kernel, len(rows[step]), f"inner_{step}", base, out, (), ties)
        first = join((first, second), (out,))
        ties = (first,)
    out = piece(functools.partial(sides_kernel, rows[-1]), len(rows[-1]) + 3.5, "sides", base, out, (left, right), ties)
    halos = (left, right, paired_row, other_row)
    out, mix = ends(nx, ny, base, out, halos, (first, second), readers, w_cquery, w_ckey, w_cvalue, w_value)
    update = final(out, mix)
    return update.reshape(features.shape)


def solution(mesh):
    in_specs = (P("gx", "gy", None, None), P("gx", "gy", None), P("gx", "gy", None)) + (P(),) * 7
    return jax.shard_map(
        per_device, mesh=mesh, in_specs=in_specs, out_specs=P("gx", "gy", None, None), check_vma=False
    )
```

```python
import functools
import math

import jax
import jax.numpy as jnp
from jax import lax
from jax.experimental import pallas as pl
from jax.experimental.pallas import tpu as pltpu
from jax.sharding import PartitionSpec as P

BF16 = jnp.bfloat16
F32 = jnp.float32
S = 64
DEPTH = 2
CUTS = (4, 7, 10, 14)
IN_VMEM = pl.BlockSpec(memory_space=pltpu.VMEM)
IN_HBM = pl.BlockSpec(memory_space=pltpu.HBM)


def dot(a, b):
    return jnp.dot(a, b, preferred_element_type=F32)


def dot_t(a, b):
    return lax.dot_general(a, b, (((1,), (1,)), ((), ())), preferred_element_type=F32)


def t_dot(a, b):
    return lax.dot_general(a, b, (((0,), (0,)), ((), ())), preferred_element_type=F32)


def in_hbm(array):
    return pltpu.with_memory_space_constraint(array, pltpu.HBM)


def params(mib):
    return pltpu.CompilerParams(vmem_limit_bytes=mib * 1024 * 1024)


def paired(ids):
    half = ids.shape[0] // 2
    return jnp.concatenate([ids[:half], ids[half:]], axis=1)


def pool_kernel(tile, nx, ny, f_ref, pm_ref, tm_ref, wq_ref, wk_ref, fv_ref, pv_ref, mv_ref, m_ref, pooled_ref, inward_ref, outward_ref, tv, wq, wk, sems):
    rows, span, chan = fv_ref.shape
    cy = span // tile
    small = [(tm_ref, tv), (wq_ref, wq), (wk_ref, wk), (pm_ref, pv_ref)]
    first = [pltpu.make_async_copy(src, dst, sems.at[rows + i]) for i, (src, dst) in enumerate(small)]
    beads_in = [pltpu.make_async_copy(f_ref.at[r], fv_ref.at[r], sems.at[r]) for r in range(rows)]
    for copy in first + beads_in:
        copy.start()
    block = lax.broadcasted_iota(jnp.int32, (18, 12 * tile), 1) // tile
    which = lax.broadcasted_iota(jnp.int32, (18, 12 * tile), 0)
    offset, second = which % 9, which // 9
    hit = (offset // 3 == block // 4) & (offset % 3 == block % 4 - second)
    pick = jnp.where(hit, 1 / math.sqrt(tile), 0.0).astype(BF16)
    for copy in first:
        copy.wait()
    m_ref[...] = (dot_t(wq[...], wk[...]) * (0.5 / math.sqrt(chan))).astype(BF16)
    mask = jnp.concatenate([tv[pl.ds(r, 9, stride=rows), :].astype(F32) for r in range(rows)], axis=1)
    lane = lax.broadcasted_iota(jnp.int32, mask.shape, 1)
    toward = lax.broadcasted_iota(jnp.int32, mask.shape, 0)
    mx, my = lax.axis_index("gx"), lax.axis_index("gy")
    outside = (toward // 3 == 0) & (lane // cy == jnp.where(mx == 0, 0, -1))
    outside |= (toward // 3 == 2) & (lane // cy == jnp.where(mx == nx - 1, rows - 1, -1))
    outside |= (toward % 3 == 0) & (lane % cy == jnp.where(my == 0, 0, -1))
    outside |= (toward % 3 == 2) & (lane % cy == jnp.where(my == ny - 1, cy - 1, -1))
    mask = jnp.where(outside, 0.0, mask)
    even = lane % 2 == 0
    both = jnp.concatenate([jnp.where(even, mask, 0.0), jnp.where(even, 0.0, mask)], axis=0)
    mv_ref[...] = t_dot(both.astype(BF16), pick)

    node = lax.broadcasted_iota(jnp.int32, (S, 2 * tile), 0)
    order = [c for i in range(cy // 2) for c in (i, i + cy // 2)]
    total = jnp.zeros((S, chan), F32)
    for low in range(0, rows, 8):
        group = range(low, min(low + 8, rows))
        hot, beads = [], []
        for r in group:
            pairs = paired(pv_ref[r])
            hot += [
                (jnp.broadcast_to(pairs[i : i + 1], node.shape) == node).astype(F32).astype(BF16) for i in range(cy // 2)
            ]
        for r in group:
            beads_in[r].wait()
        for r in group:
            beads += [fv_ref[r, tile * c : tile * (c + 1)] for c in order]
        total += dot(jnp.concatenate(hot, axis=1), jnp.concatenate(beads, axis=0))
        for r in group:
            for ref, low_side in ((inward_ref, my % 2), (outward_ref, 1 - my % 2)):
                column = pl.ds(pl.multiple_of((1 - low_side) * (span - tile), tile), tile)
                ref[tile * r : tile * (r + 1)] = fv_ref[r, column]
    pooled_ref[...] = (total * math.sqrt(S / (rows * span))).astype(BF16)


def pool(nx, ny, features, tile_mask, pool_map, w_query, w_key):
    cx, cy, tile, chan = features.shape
    span = cy * tile
    edge = pltpu.VMEM((cx * tile, chan), BF16)
    return pl.pallas_call(
        functools.partial(pool_kernel, tile, nx, ny),
        in_specs=[IN_HBM] * 5,
        out_specs=[IN_VMEM] * 7,
        out_shape=[
            pltpu.VMEM((cx, span, chan), BF16),
            pltpu.VMEM((cx, cy, tile), jnp.int32),
            pltpu.VMEM((cx * cy, 12 * tile), F32),
            pltpu.VMEM((chan, chan), BF16),
            pltpu.VMEM((S, chan), BF16),
            edge,
            edge,
        ],
        scratch_shapes=[
            pltpu.VMEM((9 * cx, cy), jnp.int32),
            pltpu.VMEM((chan, chan), BF16),
            pltpu.VMEM((chan, chan), BF16),
            pltpu.SemaphoreType.DMA((cx + 4,)),
        ],
        compiler_params=params(16),
        name="pool",
    )(
        in_hbm(features.reshape(cx, span, chan)),
        in_hbm(pool_map),
        in_hbm(jnp.transpose(tile_mask, (2, 0, 1)).reshape(9 * cx, cy)),
        in_hbm(w_query),
        in_hbm(w_key),
    )


def attend(tile, tasks, between=()):
    waiting = []

    def finish(task, weights):
        _, windows, _, store = task
        near = jnp.concatenate([window() for window in windows], axis=0)
        store(dot(jnp.concatenate(weights, axis=1), near).astype(BF16))

    for at, task in enumerate(tasks):
        if at in between:
            between[at]()
        query, windows, masks, _ = task
        weights = []
        for r, window in enumerate(windows):
            half = dot_t(query, window())
            lanes = slice(4 * tile * r, 4 * tile * (r + 1))
            mask = jnp.concatenate([jnp.broadcast_to(masks(h, lanes), (tile, 4 * tile)) for h in (0, 1)], axis=0)
            weights.append((half * jnp.tanh(half) + half).astype(BF16) * mask.astype(BF16))
        waiting.append((task, weights))
        if len(waiting) > DEPTH:
            finish(*waiting.pop(0))
    while waiting:
        finish(*waiting.pop(0))


def row_tasks(refs, row, first, last, window):
    fv, pv, mv, m, o = refs
    chan = fv.shape[2]
    cy, tile = pv.shape[1:]
    side = 2 * tile
    queries = dot(fv[row, side * first : side * last], m[...]).astype(BF16)
    tasks = []
    for j in range(first, last):

        def store(value, lo=side * j):
            o[row, lo : lo + side, :chan] = value

        tasks.append((
            queries[side * (j - first) : side * (j - first + 1)],
            [functools.partial(window, r, j) for r in (row - 1, row, row + 1)],
            lambda h, lanes, lo=row * cy + 2 * j: mv[lo + h : lo + h + 1, lanes],
            store,
        ))
    return tasks


def node_rows(refs, row):
    fv, pv, _, _, o = refs
    _, span, chan = fv.shape
    cy, tile = pv.shape[1:]
    pairs = paired(pv[row])
    node = lax.broadcasted_iota(jnp.int32, (chan, 2 * tile), 0)
    for i in range(cy // 2):
        turned = (jnp.broadcast_to(pairs[i : i + 1], node.shape) == node).astype(F32).T.astype(BF16)
        o[row, tile * i : tile * (i + 1), chan:] = turned[:tile]
        o[row, span // 2 + tile * i : span // 2 + tile * (i + 1), chan:] = turned[tile:]


def inner_tasks(refs, rows):
    fv, pv = refs[:2]
    cy, tile = pv.shape[1:]

    def window(r, j):
        return fv[r, tile * (2 * j - 1) : tile * (2 * j + 3)]

    tasks = []
    for row in rows:
        node_rows(refs, row)
        tasks += row_tasks(refs, row, 1, cy // 2 - 1, window)
    return tasks


def inner_kernel(rows, fv, pv, mv, m, *rest):
    attend(pv.shape[2], inner_tasks((fv, pv, mv, m, rest[-1]), rows))


def side_window(fv, tile, left, right):
    span = fv.shape[1]

    def window(r, j):
        if j == 0:
            return jnp.concatenate([left[tile * r : tile * (r + 1)], fv[r, : 3 * tile]], axis=0)
        if 2 * tile * (j + 1) == span:
            return jnp.concatenate([fv[r, span - 3 * tile :], right[tile * r : tile * (r + 1)]], axis=0)
        return fv[r, tile * (2 * j - 1) : tile * (2 * j + 3)]

    return window


def sides_kernel(rows, fv, pv, mv, m, out_in, left, right, *rest):
    cy, tile = pv.shape[1:]
    refs = (fv, pv, mv, m, rest[-1])
    window = side_window(fv, tile, left, right)
    tasks = inner_tasks(refs, rows)
    for row in range(1, fv.shape[0] - 1):
        for j in (0, cy // 2 - 1):
            tasks += row_tasks(refs, row, j, j + 1, window)
    attend(tile, tasks)


def ends_kernel(nx, ny, fv, pv, mv, m, out_in, left, right, paired_row, other_row, *rest):
    first, second, *weights, o, mix, above, below = rest
    cy, tile = pv.shape[1:]
    rows = fv.shape[0]
    refs = (fv, pv, mv, m, o)
    near = side_window(fv, tile, left, right)
    odd = lax.axis_index("gx") % 2 == 1

    @pl.when(odd)
    def _():
        above[...] = paired_row[...]
        below[...] = other_row[...]

    @pl.when(jnp.logical_not(odd))
    def _():
        above[...] = other_row[...]
        below[...] = paired_row[...]

    def window(r, j):
        if r in (-1, rows):
            return (above if r < 0 else below)[2 * tile * j : 2 * tile * (j + 2)]
        return near(r, j)

    between = coarse(nx, ny, (first, second), *weights, mix)
    tasks = []
    for row in (0, rows - 1):
        node_rows(refs, row)
        tasks += row_tasks(refs, row, 0, cy // 2, window)
    attend(tile, tasks, between)


def estimate(rows):
    return pl.CostEstimate(flops=int(rows * 400_000_000), bytes_accessed=1_000_000, transcendentals=0)


def piece(kernel, rows_done, name, base, out, near=(), ties=()):
    cx, span, chan = base[0].shape
    done = [] if out is None else [out]
    return pl.pallas_call(
        kernel,
        in_specs=[IN_VMEM] * (4 + len(done) + len(near)) + [pl.BlockSpec(memory_space=pl.ANY)] * len(ties),
        out_specs=IN_VMEM,
        out_shape=pltpu.VMEM((cx, span, 2 * chan), BF16),
        input_output_aliases={4: 0} if done else {},
        compiler_params=params(16),
        cost_estimate=estimate(rows_done),
        name=name,
    )(*base, *done, *near, *ties)


def coarse(nx, ny, blocks, readers_ref, wcq_ref, wck_ref, wcv_ref, wv_ref, mix):
    nodes = jnp.concatenate([ref[...] for ref in blocks], axis=0)
    count, chan = nodes.shape
    mx, my = lax.axis_index("gx"), lax.axis_index("gy")
    block = lax.broadcasted_iota(jnp.int32, (readers_ref.shape[0], count), 1) // S
    rest = block // nx
    turn = (rest % (ny // 2)) * 2 + rest // (ny // 2)
    domain = ((block % nx) ^ mx) * ny + (turn ^ my)
    lane = lax.broadcasted_iota(jnp.int32, readers_ref.shape, 1)
    mine = jnp.sum(jnp.where(lane == mx * ny + my, readers_ref[...], 0), axis=1, keepdims=True)
    live = jnp.sum(jnp.where(domain == mine, 1.0, 0.0), axis=0, keepdims=True)
    held = {}

    def project():
        held["query"] = dot(nodes[:S], wcq_ref[...]).astype(BF16)
        held["key"] = dot(nodes, wck_ref[...]).astype(BF16)
        held["value"] = dot(nodes, wcv_ref[...]).astype(BF16)

    def weigh():
        half = dot_t(held["query"], held["key"]) * (0.5 / math.sqrt(chan))
        weight = (half * jnp.tanh(half) + half).astype(BF16).astype(F32) * live
        held["weight"] = weight.astype(BF16)

    def gather():
        mix[:chan] = wv_ref[...]
        mix[chan : chan + S] = (dot(held["weight"], held["value"]) / math.sqrt(S)).astype(BF16)
        mix[chan + S :] = jnp.zeros((chan - S, chan), BF16)

    return {2: project, 6: weigh, 10: gather}


def ends(nx, ny, base, out, halos, blocks, readers, w_cquery, w_ckey, w_cvalue, w_value):
    chan = base[0].shape[2]
    operands = (*base, out, *halos, *blocks, readers.T, w_cquery, w_ckey, w_cvalue, w_value)
    return pl.pallas_call(
        functools.partial(ends_kernel, nx, ny),
        in_specs=[IN_VMEM] * len(operands),
        out_specs=[IN_VMEM] * 2,
        out_shape=[pltpu.VMEM(out.shape, BF16), pltpu.VMEM((2 * chan, chan), BF16)],
        scratch_shapes=[pltpu.VMEM(halos[-1].shape, BF16)] * 2,
        input_output_aliases={4: 0},
        compiler_params=params(16),
        cost_estimate=estimate(2),
        name="ends",
    )(*operands)


def final_kernel(o_ref, mix, out_ref, rows_out, sems):
    rows = rows_out.shape[0]

    def send(r):
        return pltpu.make_async_copy(rows_out.at[r], out_ref.at[r], sems.at[r])

    for r in range(rows):
        rows_out[r] = dot(o_ref[r], mix[...]).astype(BF16)
        send(r).start()
    for r in range(rows):
        send(r).wait()


def final(out, mix):
    cx, span, wide = out.shape
    chan = wide // 2
    return pl.pallas_call(
        final_kernel,
        in_specs=[IN_VMEM] * 2,
        out_specs=IN_HBM,
        out_shape=jax.ShapeDtypeStruct((cx, span, chan), BF16),
        scratch_shapes=[pltpu.VMEM((cx, span, chan), BF16), pltpu.SemaphoreType.DMA((cx,))],
        compiler_params=params(16),
        name="final",
    )(out, mix)


def swap(array, axis, bits):
    return lax.ppermute(array, axis, [(i, i ^ bits) for i in range(lax.axis_size(axis))])


def join_kernel(count, *refs):
    parts, out = refs[:count], refs[-1]
    at = 0
    for part in parts:
        out[at : at + part.shape[0]] = part[...]
        at += part.shape[0]


def join(parts, ties):
    rows = sum(part.shape[0] for part in parts)
    return pl.pallas_call(
        functools.partial(join_kernel, len(parts)),
        in_specs=[IN_VMEM] * len(parts) + [pl.BlockSpec(memory_space=pl.ANY)] * len(ties),
        out_specs=IN_VMEM,
        out_shape=pltpu.VMEM((rows, parts[0].shape[1]), BF16),
        compiler_params=params(4),
        name="join",
    )(*parts, *ties)


def edge_rows_kernel(tile, fv_ref, paired_ref, other_ref, *rest):
    left_ref, right_ref, inward_ref, outward_ref = rest[-4:]
    rows, span, _ = fv_ref.shape

    @pl.when(lax.axis_index("gy") % 2 == 1)
    def _():
        left_ref[...] = paired_ref[...]
        right_ref[...] = other_ref[...]

    @pl.when(lax.axis_index("gy") % 2 == 0)
    def _():
        left_ref[...] = other_ref[...]
        right_ref[...] = paired_ref[...]

    odd = lax.axis_index("gx") % 2
    for ref, low in ((inward_ref, odd), (outward_ref, 1 - odd)):
        r = (1 - low) * (rows - 1)
        corner = pl.ds(pl.multiple_of(tile * r, tile), tile)
        ref[:tile] = left_ref[corner]
        ref[tile : tile + span] = fv_ref[r]
        ref[tile + span :] = right_ref[corner]


def edge_rows(tile, fv, paired_column, other_column, ties):
    rows, span, chan = fv.shape
    column = pltpu.VMEM((rows * tile, chan), BF16)
    edge = pltpu.VMEM((span + 2 * tile, chan), BF16)
    return pl.pallas_call(
        functools.partial(edge_rows_kernel, tile),
        in_specs=[IN_VMEM] * 3 + [pl.BlockSpec(memory_space=pl.ANY)] * len(ties),
        out_specs=[IN_VMEM] * 4,
        out_shape=[column, column, edge, edge],
        compiler_params=params(4),
        name="edge_rows",
    )(fv, paired_column, other_column, *ties)


def swap_across(array, axis, nx, ny):
    moves = []
    for x in range(nx):
        for y in range(ny):
            if axis == "gx":
                near = x + 1 if x % 2 else x - 1
                there = near * ny + y if 0 <= near < nx else x * ny + (y ^ 1)
            else:
                near = y + 1 if y % 2 else y - 1
                there = x * ny + near if 0 <= near < ny else (x ^ 1) * ny + y
            moves.append((x * ny + y, there))
    return lax.ppermute(array, ("gx", "gy"), moves)


def per_device(features, tile_mask, pool_map, readers, w_query, w_key, w_value, w_cquery, w_ckey, w_cvalue):
    cx, cy, tile, chan = features.shape
    nx, ny = lax.axis_size("gx"), lax.axis_size("gy")
    *base, pooled, inward, outward = pool(nx, ny, features, tile_mask, pool_map, w_query, w_key)
    fv = base[0]
    cuts = [1] + [1 + (cx - 2) * part // 14 for part in CUTS] + [cx - 1]
    rows = [range(lo, hi) for lo, hi in zip(cuts, cuts[1:])]
    steps = [("gx", 1 << b) for b in range(nx.bit_length() - 1)]
    steps += [("gy", 1 << b) for b in range(1, ny.bit_length() - 1)] + [("gy", 1)]
    paired_column = swap(inward, "gy", 1)
    other_column = swap_across(outward, "gy", nx, ny)
    out, first, ties = None, pooled, (pooled,)
    for step, (axis, bit) in enumerate(steps):
        second = swap(first, axis, bit)
        if step == 2:
            left, right, inward, outward = edge_rows(tile, fv, paired_column, other_column, (out, first))
            paired_row = swap(inward, "gx", 1)
            other_row = swap_across(outward, "gx", nx, ny)
            ties += (inward,)
        if step == len(steps) - 1:
            break
        if step < len(rows) - 1:
            kernel = functools.partial(inner_kernel, rows[step])
            out = piece(kernel, len(rows[step]), f"inner_{step}", base, out, (), ties)
        first = join((first, second), (out,))
        ties = (first,)
    out = piece(functools.partial(sides_kernel, rows[-1]), len(rows[-1]) + 3.5, "sides", base, out, (left, right), ties)
    halos = (left, right, paired_row, other_row)
    out, mix = ends(nx, ny, base, out, halos, (first, second), readers, w_cquery, w_ckey, w_cvalue, w_value)
    update = final(out, mix)
    return update.reshape(features.shape)


def solution(mesh):
    in_specs = (P("gx", "gy", None, None), P("gx", "gy", None), P("gx", "gy", None)) + (P(),) * 7
    return jax.shard_map(
        per_device, mesh=mesh, in_specs=in_specs, out_specs=P("gx", "gy", None, None), check_vma=False
    )
```
